32 devices in a mesh: dp: 2 (over y), row: 4 (over x, core), col: 4 (over z).
Axes of the slice: x: 2, y: 2, z: 4, core: 2. Of those that a mesh axis runs over, the one named last changes fastest.
Arguments:
- block_input: bfloat16 [2, 4096, 1088], P('dp', 'col', 'row'), may hold values from -6 to 6
- cotangent: bfloat16 [2, 4096, 1088], P('dp', 'col', 'row'), may hold values from -6 to 6
- prefix_len: int32 [2], P('dp'), may hold values from 409 to 2048
- first_gain: float32 [1088], P('row'), may hold values from 0.5 to 1.5
- first_shift: float32 [1088], P('row'), may hold values from -1 to 1
- qkv_weight: bfloat16 [1088, 3264], P('row', 'col'), may hold values from -0.1875 to 0.1875
- qkv_bias: bfloat16 [3264], P('col'), may hold values from -1.5 to 1.5
- out_weight: bfloat16 [1088, 1088], P('col', 'row'), may hold values from -6 to 6
- out_bias: float32 [1088], P('row'), may hold values from -1.5 to 1.5
- second_gain: float32 [1088], P('row'), may hold values from 0.5 to 1.5
- second_shift: float32 [1088], P('row'), may hold values from -1 to 1
- up_weight: bfloat16 [1088, 4352], P('row', 'col'), may hold values from -0.1875 to 0.1875
- up_bias: bfloat16 [4352], P('col'), may hold values from -1.5 to 1.5
- down_weight: bfloat16 [4352, 1088], P('col', 'row'), may hold values from -0.09375 to 0.09375
- down_bias: float32 [1088], P('row'), may hold values from -1.5 to 1.5
Outputs:
- block_output: bfloat16 [2, 4096, 1088], P('dp', 'col', 'row')
- input_grad: float32 [2, 4096, 1088], P('dp', 'col', 'row')
- first_gain_grad: float32 [1088], P('row')
- first_shift_grad: float32 [1088], P('row')
- qkv_weight_grad: float32 [1088, 3264], P('row', 'col')
- qkv_bias_grad: float32 [3264], P('col')
- out_weight_grad: float32 [1088, 1088], P('col', 'row')
- out_bias_grad: float32 [1088], P('row')
- second_gain_grad: float32 [1088], P('row')
- second_shift_grad: float32 [1088], P('row')
- up_weight_grad: float32 [1088, 4352], P('row', 'col')
- up_bias_grad: float32 [4352], P('col')
- down_weight_grad: float32 [4352, 1088], P('col', 'row')
- down_bias_grad: float32 [1088], P('row')
The draws below stay inside these ranges and needn't reach their ends.
All inputs are finite; a program needn't handle non-finite values.
Results may differ from the reference program's by a relative error of at most 0.029.
Values may be sent and summed in bfloat16 or wider, within the bound.
No kernel may reach another device: no remote copies, remote signals or barrier semaphores. Data moves between devices by JAX's collectives and lax.ppermute only.
A program may use at most 192 MiB of HBM per device.

```python
import jax
import jax.numpy as jnp
from jax import lax

HEADS = 17
HDIM = 64
D = 1088
FF = 4352
LEN = 4096
SEQS = 2


def level_of(own_key, dims, shards, low, high):
    gain, own = 1.0, jax.random.fold_in(own_key, 6)
    for position, shards_of in shards:
        steps = jnp.exp(jax.random.uniform(jax.random.fold_in(own, position), (shards_of,), jnp.float32, low / len(shards), high / len(shards)))
        gain = gain * jnp.repeat(steps, dims[position] // shards_of).reshape([-1 if axis == position else 1 for axis in range(len(dims))])
    return gain


def noise(rng, dims, deviation, bound, shards=(), kind=jnp.bfloat16):
    drawn = jax.random.normal(rng, dims, jnp.float32) * deviation
    if len(shards) > 0:
        drawn = level_of(rng, dims, shards, -0.22, 0.18) * drawn
    return jnp.clip(drawn, min=-bound, max=bound).astype(kind)


def setup_inputs(seed: int = 0) -> dict:
    keys = jax.random.split(jax.random.key(seed), 16)
    block_input = noise(keys[0], (SEQS, LEN, D), 1.0, 6.0, ((0, 2), (1, 4), (2, 4)))
    cotangent = noise(keys[1], (SEQS, LEN, D), 1.0, 6.0, ((0, 2), (1, 4), (2, 4)))
    prefix_len = jax.random.randint(keys[2], (SEQS,), LEN // 10, LEN // 2 + 1).astype(jnp.int32)
    first_gain = jnp.clip(1.0 + 0.1 * jax.random.normal(keys[3], (D,), jnp.float32), 0.5, 1.5)
    first_shift = noise(keys[4], (D,), 0.2, 1.0, ((0, 4),), jnp.float32)
    qkv_weight = noise(keys[5], (D, 3 * D), D ** -0.5, 0.1875, ((0, 4), (1, 4)))
    qkv_bias = noise(keys[6], (3 * D,), 0.3, 1.5, ((0, 4),))
    out_weight = noise(keys[7], (D, D), (max(1, D * 4 // LEN)) ** -0.5, 6.0, ((0, 4), (1, 4)))
    out_bias = noise(keys[8], (D,), 0.3, 1.5, ((0, 4),), jnp.float32)
    second_gain = jnp.clip(1.0 + 0.1 * jax.random.normal(keys[9], (D,), jnp.float32), 0.5, 1.5)
    second_shift = noise(keys[10], (D,), 0.2, 1.0, ((0, 4),), jnp.float32)
    up_weight = noise(keys[11], (D, FF), D ** -0.5, 0.1875, ((0, 4), (1, 4)))
    up_bias = noise(keys[12], (FF,), 0.3, 1.5, ((0, 4),))
    down_weight = noise(keys[13], (FF, D), FF ** -0.5, 0.09375, ((0, 4), (1, 4)))
    down_bias = noise(keys[14], (D,), 0.3, 1.5, ((0, 4),), jnp.float32)
    return dict(block_input=block_input, cotangent=cotangent, prefix_len=prefix_len, first_gain=first_gain, first_shift=first_shift, qkv_weight=qkv_weight, qkv_bias=qkv_bias, out_weight=out_weight, out_bias=out_bias, second_gain=second_gain, second_shift=second_shift, up_weight=up_weight, up_bias=up_bias, down_weight=down_weight, down_bias=down_bias)


@jax.custom_vjp
def low(v):
    return lax.optimization_barrier(v.astype(jnp.bfloat16)).astype(jnp.float32)

@jax.custom_vjp
def low_back(v):
    return v

def low_keep(v):
    return (low(v), None)

def low_pass(kept, grad):
    return (grad,)

def back_keep(v):
    return (v, None)

def back_low(kept, grad):
    return (low(grad),)
low.defvjp(low_keep, low_pass)
low_back.defvjp(back_keep, back_low)

def matmul(left, right):
    return jnp.dot(left, right, precision=lax.Precision.HIGHEST)

def layer_norm(values, norm_gain, norm_shift):
    row_mean = lax.optimization_barrier(jnp.mean(values, -1, keepdims=True))
    variance = lax.optimization_barrier(jnp.mean(values * values, -1, keepdims=True)) - row_mean * row_mean
    return (values - row_mean) * lax.rsqrt(variance + 1e-05) * norm_gain + norm_shift

def block_attend(query_block, first_row, key_rows, value_rows, prefix_end):
    scores = jnp.einsum('qhd,khd->hqk', query_block, key_rows, precision=lax.Precision.HIGHEST) * HDIM ** (-0.5)
    scores = low_back(scores)
    query_pos = first_row + jnp.arange(query_block.shape[0], dtype=jnp.int32)
    key_pos = jnp.arange(key_rows.shape[0], dtype=jnp.int32)
    allowed = (key_pos[None, :] < prefix_end) | (key_pos[None, :] <= query_pos[:, None])
    scores = jnp.where(allowed[None], scores, -1e+30)
    weights_low = low(jax.nn.softmax(scores, axis=-1))
    return jnp.einsum('hqk,khd->qhd', weights_low, value_rows, precision=lax.Precision.HIGHEST)

def sequence_attend(packed):
    query_rows, key_rows, value_rows, prefix_end = packed
    block_len = min(512, LEN)
    blocks = query_rows.reshape(LEN // block_len, block_len, HEADS, HDIM)
    starts = jnp.arange(LEN // block_len, dtype=jnp.int32) * block_len

    def per_block(block_pair):
        return block_attend(block_pair[0], block_pair[1], key_rows, value_rows, prefix_end)
    attended = lax.map(jax.checkpoint(per_block), (blocks, starts))
    return attended.reshape(LEN, HEADS * HDIM)

def forward(block_input, first_gain, first_shift, qkv_weight, qkv_bias, out_weight, out_bias, second_gain, second_shift, up_weight, up_bias, down_weight, down_bias, prefix_len):
    normed = low(layer_norm(block_input, first_gain, first_shift))
    mixed_qkv = low(low_back(matmul(normed, qkv_weight) + qkv_bias))
    split_qkv = mixed_qkv.reshape(block_input.shape[0], LEN, 3, HEADS, HDIM)
    attended = lax.map(sequence_attend, (split_qkv[:, :, 0], split_qkv[:, :, 1], split_qkv[:, :, 2], prefix_len))
    attended = low(low_back(attended))
    residual = block_input + low_back(matmul(attended, out_weight) + out_bias)
    normed_two = low(layer_norm(residual, second_gain, second_shift))
    hidden = low_back(matmul(normed_two, up_weight) + up_bias)
    active = low(jax.nn.gelu(hidden, approximate=False))
    return residual + low_back(matmul(active, down_weight) + down_bias)

def reference(block_input, cotangent, prefix_len, first_gain, first_shift, qkv_weight, qkv_bias, out_weight, out_bias, second_gain, second_shift, up_weight, up_bias, down_weight, down_bias):
    floats = [block_input, first_gain, first_shift, qkv_weight, qkv_bias, out_weight, out_bias, second_gain, second_shift, up_weight, up_bias, down_weight, down_bias]
    floats = [member.astype(jnp.float32) for member in floats]

    def run_block(*params):
        return forward(*params, prefix_len)
    result, pull_back = jax.vjp(run_block, *floats)
    gradients = pull_back(cotangent.astype(jnp.float32))
    return (result.astype(jnp.bfloat16), gradients[0], gradients[1], gradients[2], gradients[3], gradients[4], gradients[5], gradients[6], gradients[7], gradients[8], gradients[9], gradients[10], gradients[11], gradients[12])
```

```python
from functools import partial

import jax
import jax.numpy as jnp
import numpy as np
from jax import lax
from jax.experimental import pallas as pl
from jax.experimental.pallas import tpu as pltpu
from jax.sharding import PartitionSpec as P

HEADS = 17
HDIM = 64
D = 1088


def positions(first_row, piece_len, tok_b, tok_a, col_total):
    flat_rows = first_row + jnp.arange(piece_len, dtype=jnp.int32)
    shard_no = flat_rows // tok_b
    return shard_no % col_total * tok_a + shard_no // col_total * tok_b + flat_rows % tok_b


def over_blocks(folded, pieces, step_fn):
    piece_len = pieces[0].shape[0]
    block_len = 512

    def one_block(block_no, running):
        offset = block_no * block_len
        sliced = tuple(
            (lax.dynamic_slice_in_dim(member, offset, block_len, 0) for member in pieces)
        )
        return step_fn(running, sliced, offset)

    return lax.fori_loop(0, piece_len // block_len, one_block, folded)


def head_scores(left, right, scale_factor):
    return (
        jnp.einsum("qhd,khd->hqk", left, right, preferred_element_type=jnp.float32) * scale_factor
    )


def normalize(values, norm_gain, norm_shift):
    width_all = values.shape[1] * lax.axis_size("row")
    row_sums = lax.psum((jnp.sum(values, 1), jnp.sum(values * values, 1)), "row")
    row_mean = row_sums[0] / width_all
    variance = row_sums[1] / width_all - row_mean * row_mean
    inv_std = lax.rsqrt(variance + 1e-05)
    centred = (values - row_mean[:, None]) * inv_std[:, None]
    return (centred * norm_gain + norm_shift, centred, inv_std)


def norm_back(d_normed, centred, inv_std, norm_gain):
    width_all = d_normed.shape[1] * lax.axis_size("row")
    scaled = d_normed * norm_gain
    row_sums = lax.psum((jnp.sum(scaled, 1), jnp.sum(scaled * centred, 1)), "row")
    d_values = inv_std[:, None] * (
        scaled - row_sums[0][:, None] / width_all - centred * row_sums[1][:, None] / width_all
    )
    return (d_values, jnp.sum(d_normed * centred, 0), jnp.sum(d_normed, 0))


def row_partials(term_fn, tok_b):
    return lax.psum_scatter(
        term_fn(jnp.int32(0), tok_b * lax.axis_size("row")).astype(jnp.bfloat16),
        "row",
        scatter_dimension=0,
        tiled=True,
    ).astype(jnp.float32)


def rows_gather(values):
    return lax.all_gather(values, "row", axis=0, tiled=True)


def row_product(normed_low, weight, tok_b):

    def term_fn(first_row, row_count):
        return jnp.dot(normed_low, weight, preferred_element_type=jnp.float32)

    return row_partials(term_fn, tok_b)


def back_product(grad_low, weight, tok_b):

    def term_fn(first_row, row_count):
        return lax.dot_general(
            grad_low, weight, (((1,), (1,)), ((), ())), preferred_element_type=jnp.float32
        )

    return row_partials(term_fn, tok_b)


def fold_back(grad_rows, normed_low, weight_full):
    piece = lax.all_gather(grad_rows, "row", axis=0, tiled=True)
    contrib = lax.dot_general(
        piece, weight_full, (((1,), (1,)), ((), ())), preferred_element_type=jnp.float32
    )
    d_weight = lax.dot_general(
        normed_low, piece, (((0,), (0,)), ((), ())), preferred_element_type=jnp.float32
    )
    return (contrib, d_weight, jnp.sum(piece.astype(jnp.float32), 0))


def scatter_columns(gradients):
    return (
        lax.psum_scatter(
            gradients[0].astype(jnp.bfloat16), "col", scatter_dimension=1, tiled=True
        ).astype(jnp.float32),
        lax.psum_scatter(
            gradients[1].astype(jnp.bfloat16), "col", scatter_dimension=0, tiled=True
        ).astype(jnp.float32),
        lax.psum_scatter(
            gradients[2].astype(jnp.bfloat16), "col", scatter_dimension=0, tiled=True
        ).astype(jnp.float32),
        lax.psum_scatter(
            gradients[3].astype(jnp.bfloat16), "col", scatter_dimension=1, tiled=True
        ).astype(jnp.float32),
        lax.psum_scatter(
            gradients[4].astype(jnp.bfloat16), "col", scatter_dimension=0, tiled=True
        ).astype(jnp.float32),
        lax.psum_scatter(
            gradients[5].astype(jnp.bfloat16), "col", scatter_dimension=0, tiled=True
        ).astype(jnp.float32),
    )


def sum_over_data(gradients):
    return (
        lax.psum(gradients[0].astype(jnp.bfloat16), "dp").astype(jnp.float32),
        lax.psum(gradients[1].astype(jnp.bfloat16), "dp").astype(jnp.float32),
        lax.psum(gradients[2].astype(jnp.bfloat16), "dp").astype(jnp.float32),
        lax.psum(gradients[3].astype(jnp.bfloat16), "dp").astype(jnp.float32),
        lax.psum(gradients[4].astype(jnp.bfloat16), "dp").astype(jnp.float32),
        lax.psum(gradients[5].astype(jnp.bfloat16), "dp").astype(jnp.float32),
    )


def shards(
    block_input,
    cotangent,
    prefix_len,
    first_gain,
    first_shift,
    qkv_weight,
    qkv_bias,
    out_weight,
    out_bias,
    second_gain,
    second_shift,
    up_weight,
    up_bias,
    down_weight,
    down_bias,
):
    row_total = lax.axis_size("row")
    col_total = lax.axis_size("col")
    tok_a = block_input.shape[1]
    tok_b = tok_a // row_total
    scale_factor = HDIM ** (-0.5)
    gathered = (
        lax.all_gather(qkv_weight, "col", axis=1, tiled=True),
        lax.all_gather(qkv_bias, "col", axis=0, tiled=True),
        lax.all_gather(out_weight, "col", axis=0, tiled=True),
        lax.all_gather(up_weight, "col", axis=1, tiled=True),
        lax.all_gather(up_bias, "col", axis=0, tiled=True),
        lax.all_gather(down_weight, "col", axis=0, tiled=True),
    )
    qkv_full, qkv_bias_full, out_full, up_full, up_bias_full, down_full = gathered
    residual = block_input[0].astype(jnp.float32)
    prefix_end = prefix_len[0]
    own_pos = (
        lax.axis_index("col") * tok_a
        + lax.axis_index("row") * tok_b
        + jnp.arange(tok_b, dtype=jnp.int32)
    )

    def visible(key_pos, query_pos):
        return (key_pos[None, :] < prefix_end) | (key_pos[None, :] <= query_pos[:, None])

    def piece_pos(first_row, piece_len):
        return positions(first_row, piece_len, tok_b, tok_a, col_total)

    normed_one, centred_one, inv_one = normalize(residual, first_gain, first_shift)
    normed_one_low = normed_one.astype(jnp.bfloat16)
    mixed_qkv = (
        row_product(normed_one_low, qkv_full, tok_b) + qkv_bias_full.astype(jnp.float32)
    ).astype(jnp.bfloat16)
    query_rows = mixed_qkv[:, :D]
    key_rows = mixed_qkv[:, D : 2 * D]
    value_rows = mixed_qkv[:, 2 * D :]
    own_query = query_rows.reshape(tok_b, HEADS, HDIM)
    own_key = key_rows.reshape(tok_b, HEADS, HDIM)
    own_value = value_rows.reshape(tok_b, HEADS, HDIM)

    def max_step(running, sliced, first_row):
        key_block = sliced[0]
        allowed = visible(piece_pos(first_row, key_block.shape[0]), own_pos)
        scores = jnp.where(
            allowed[None],
            head_scores(own_query, key_block.reshape(-1, HEADS, HDIM), scale_factor),
            -1e30,
        )
        new_max = jnp.maximum(running[0], jnp.max(scores, 2))
        new_total = running[1] * jnp.exp(running[0] - new_max) + jnp.sum(
            jnp.where(allowed[None], jnp.exp(scores - new_max[:, :, None]), 0.0), 2
        )
        return (new_max, new_total)

    start_max = (
        jnp.full((HEADS, tok_b), -1e30, jnp.float32),
        jnp.zeros((HEADS, tok_b), jnp.float32),
    )
    run_max, run_total = over_blocks(
        start_max, (lax.all_gather(key_rows, ("row", "col"), axis=0, tiled=True),), max_step
    )
    log_total = run_max + jnp.log(run_total)

    def value_step(running, sliced, first_row):
        key_block, value_block = sliced
        allowed = visible(piece_pos(first_row, key_block.shape[0]), own_pos)
        scores = head_scores(own_query, key_block.reshape(-1, HEADS, HDIM), scale_factor)
        attn_probs = jnp.where(allowed[None], jnp.exp(scores - log_total[:, :, None]), 0.0).astype(
            jnp.bfloat16
        )
        return running + jnp.einsum(
            "hqk,khd->qhd",
            attn_probs,
            value_block.reshape(-1, HEADS, HDIM),
            preferred_element_type=jnp.float32,
        )

    attn_acc = over_blocks(
        jnp.zeros((tok_b, HEADS, HDIM), jnp.float32),
        (
            lax.all_gather(key_rows, ("row", "col"), axis=0, tiled=True),
            lax.all_gather(value_rows, ("row", "col"), axis=0, tiled=True),
        ),
        value_step,
    )
    attn_float = attn_acc.reshape(tok_b, D)
    attn_all = rows_gather(attn_float.astype(jnp.bfloat16))
    residual_two = (
        residual + jnp.dot(attn_all, out_full, preferred_element_type=jnp.float32) + out_bias
    )
    normed_two, centred_two, inv_two = normalize(residual_two, second_gain, second_shift)
    normed_two_low = normed_two.astype(jnp.bfloat16)
    hidden = row_product(normed_two_low, up_full, tok_b) + up_bias_full.astype(jnp.float32)
    active_all = rows_gather(jax.nn.gelu(hidden, approximate=False).astype(jnp.bfloat16))
    block_output = (
        residual_two
        + jnp.dot(active_all, down_full, preferred_element_type=jnp.float32)
        + down_bias
    ).astype(jnp.bfloat16)
    cot_low = cotangent[0]
    cot_float = cot_low.astype(jnp.float32)
    down_grad = lax.dot_general(
        active_all, cot_low, (((0,), (0,)), ((), ())), preferred_element_type=jnp.float32
    )
    down_bias_grad = jnp.sum(cot_float, 0)
    d_active = back_product(cot_low, down_full, tok_b)
    gelu_back = jax.vjp(partial(jax.nn.gelu, approximate=False), hidden)[1]
    d_hidden_low = gelu_back(d_active)[0].astype(jnp.bfloat16)
    d_norm_two, up_grad, up_bias_grad = fold_back(d_hidden_low, normed_two_low, up_full)
    d_part_two, second_gain_grad, second_shift_grad = norm_back(
        d_norm_two, centred_two, inv_two, second_gain
    )
    d_residual = cot_float + d_part_two
    branch_low = d_residual.astype(jnp.bfloat16)
    out_grad = lax.dot_general(
        attn_all, branch_low, (((0,), (0,)), ((), ())), preferred_element_type=jnp.float32
    )
    out_bias_grad = jnp.sum(branch_low.astype(jnp.float32), 0)
    d_attn_low = back_product(branch_low, out_full, tok_b).astype(jnp.bfloat16)
    delta_rows = jnp.sum(
        (d_attn_low.astype(jnp.float32) * attn_float).reshape(tok_b, HEADS, HDIM), 2
    )
    lse_rows = log_total.T
    all_lse, all_delta = (
        lax.all_gather(lse_rows, ("row", "col"), axis=0, tiled=True),
        lax.all_gather(delta_rows, ("row", "col"), axis=0, tiled=True),
    )
    own_grad = d_attn_low.reshape(tok_b, HEADS, HDIM)

    def back_step(running, sliced, first_row):
        query_p, key_p, value_p, grad_p = sliced
        piece_len = query_p.shape[0]
        pos_piece = piece_pos(first_row, piece_len)
        lse_piece = lax.dynamic_slice_in_dim(all_lse, first_row, piece_len, 0)
        delta_piece = lax.dynamic_slice_in_dim(all_delta, first_row, piece_len, 0)
        query_p3 = query_p.reshape(piece_len, HEADS, HDIM)
        key_p3 = key_p.reshape(piece_len, HEADS, HDIM)
        value_p3 = value_p.reshape(piece_len, HEADS, HDIM)
        grad_p3 = grad_p.reshape(piece_len, HEADS, HDIM)
        allowed_own = visible(pos_piece, own_pos)
        allowed_far = visible(own_pos, pos_piece)
        scores = head_scores(own_query, key_p3, scale_factor)
        attn_probs = jnp.where(allowed_own[None], jnp.exp(scores - log_total[:, :, None]), 0.0)
        d_probs = jnp.einsum("qhd,khd->hqk", own_grad, value_p3, preferred_element_type=jnp.float32)
        d_scores = (attn_probs * (d_probs - delta_rows.T[:, :, None])).astype(jnp.bfloat16)
        new_query = (
            running[0]
            + jnp.einsum("hqk,khd->qhd", d_scores, key_p3, preferred_element_type=jnp.float32)
            * scale_factor
        )
        scores = head_scores(query_p3, own_key, scale_factor)
        attn_probs = jnp.where(allowed_far[None], jnp.exp(scores - lse_piece.T[:, :, None]), 0.0)
        d_value = running[2] + jnp.einsum(
            "hqk,qhd->khd",
            attn_probs.astype(jnp.bfloat16),
            grad_p3,
            preferred_element_type=jnp.float32,
        )
        d_probs = jnp.einsum("qhd,khd->hqk", grad_p3, own_value, preferred_element_type=jnp.float32)
        d_scores = (attn_probs * (d_probs - delta_piece.T[:, :, None])).astype(jnp.bfloat16)
        d_key = (
            running[1]
            + jnp.einsum("hqk,qhd->khd", d_scores, query_p3, preferred_element_type=jnp.float32)
            * scale_factor
        )
        return (new_query, d_key, d_value)

    zero_heads = jnp.zeros((tok_b, HEADS, HDIM), jnp.float32)
    d_query, d_key, d_value = over_blocks(
        (zero_heads, zero_heads, zero_heads),
        (
            lax.all_gather(query_rows, ("row", "col"), axis=0, tiled=True),
            lax.all_gather(key_rows, ("row", "col"), axis=0, tiled=True),
            lax.all_gather(value_rows, ("row", "col"), axis=0, tiled=True),
            lax.all_gather(d_attn_low, ("row", "col"), axis=0, tiled=True),
        ),
        back_step,
    )
    d_mixed_low = jnp.concatenate(
        [d_query.reshape(tok_b, D), d_key.reshape(tok_b, D), d_value.reshape(tok_b, D)], 1
    ).astype(jnp.bfloat16)
    d_norm_one, qkv_grad, qkv_bias_grad = fold_back(d_mixed_low, normed_one_low, qkv_full)
    d_part_one, first_gain_grad, first_shift_grad = norm_back(
        d_norm_one, centred_one, inv_one, first_gain
    )
    input_grad = d_residual + d_part_one
    col_ready = (qkv_grad, qkv_bias_grad, out_grad, up_grad, up_bias_grad, down_grad)
    reduced = scatter_columns(sum_over_data(col_ready))
    small = lax.psum(
        (
            first_gain_grad,
            first_shift_grad,
            out_bias_grad,
            second_gain_grad,
            second_shift_grad,
            down_bias_grad,
        ),
        ("dp", "col"),
    )
    return (
        block_output[None],
        input_grad[None],
        small[0],
        small[1],
        reduced[0],
        reduced[1],
        reduced[2],
        small[2],
        small[3],
        small[4],
        reduced[3],
        reduced[4],
        reduced[5],
        small[5],
    )


LOG2E = 1.4426950408889634
LN2 = 0.6931471805599453
PAD = 16
VMEM_LIMIT = 56 * 1024 * 1024


def swap(value, step):
    size = lax.axis_size("row")
    return lax.ppermute(value, "row", [(i, i ^ step) for i in range(size)])


def pick(stacked, index, axis=0):
    return lax.dynamic_index_in_dim(stacked, index, axis, keepdims=False)


def row_gather(own):
    far = swap(own, 2)
    return [own, swap(own, 1), far, swap(far, 1)]


def row_exchange(parts):
    return [parts[0], swap(parts[1], 1), swap(parts[2], 2), swap(parts[3], 3)]


def row_reduce(parts):
    low = [p.astype(jnp.bfloat16) for p in parts]
    beyond = swap(low[3], 1)
    near = swap(low[1], 1)
    pair = (parts[2].astype(jnp.float32) + beyond.astype(jnp.float32)).astype(jnp.bfloat16)
    far = swap(pair, 2)
    return parts[0].astype(jnp.float32) + near.astype(jnp.float32) + far.astype(jnp.float32)


def in_order(parts, me):
    stacked = jnp.stack(parts)
    return [pick(stacked, me ^ i) for i in range(len(parts))]


def layer_norm(values, gain, shift):
    mean = jnp.mean(values, 1, keepdims=True)
    variance = jnp.mean(values * values, 1, keepdims=True) - mean * mean
    inv_std = lax.rsqrt(variance + 1e-05)
    centred = (values - mean) * inv_std
    return (centred * gain + shift, centred, inv_std)


def layer_norm_back(d_normed, centred, inv_std, gain):
    scaled = d_normed * gain
    return inv_std * (
        scaled
        - jnp.mean(scaled, 1, keepdims=True)
        - centred * jnp.mean(scaled * centred, 1, keepdims=True)
    )


def load_pieces(info, pieces, slot, transposed, plain, tok_b, block):
    cols = pieces[0].shape[-1] // tok_b
    per_block = block // tok_b
    rows = len(pieces)
    for s, piece in enumerate(pieces):
        source = info[0] ^ s
        for c in range(cols):
            part = piece[slot, :, c * tok_b : (c + 1) * tok_b]
            number = (info[3] ^ c) * rows + source
            where = number // per_block
            offset = pl.multiple_of((number % per_block) * tok_b, tok_b)
            if transposed is not None:
                transposed[where, :, pl.ds(offset, tok_b)] = part
            if plain is not None:
                plain[where, pl.ds(offset, tok_b), :] = part.T


def allowed_mask(key_start, query_start, shape, prefix):
    key_pos = key_start + lax.broadcasted_iota(jnp.int32, shape, 0)
    query_pos = query_start + lax.broadcasted_iota(jnp.int32, shape, 1)
    return (key_pos < prefix) | (key_pos <= query_pos)


def forward_kernel(n_pieces, own_query, tok_b, block, info, *refs):
    prefix, first = info[1], info[2]
    pieces = refs[:n_pieces]
    refs = refs[n_pieces:]
    if own_query:
        query_ref, refs = refs[0], refs[1:]
        q_len = query_ref.shape[1]
        n_query = 1
    else:
        q_len = block
        n_query = n_pieces * pieces[0].shape[-1] // block
    out_ref, full_ref, lse_ref, q_t, k_n, v_t, acc = refs
    key_slot = 0 if own_query else 1
    if not own_query:
        load_pieces(info, pieces, 0, q_t, None, tok_b, block)
    load_pieces(info, pieces, key_slot, None, k_n, tok_b, block)
    load_pieces(info, pieces, key_slot + 1, v_t, None, tok_b, block)
    edge = prefix // block
    out_len = out_ref.shape[-1]

    def one_query(n, carry):
        start = first + n * q_len
        query = query_ref[...] if own_query else q_t[n]
        last = jnp.maximum(start // block, edge)
        acc[...] = jnp.zeros_like(acc)

        def step(kb, carry, masked):
            top, total = carry
            scores = jnp.dot(k_n[kb], query, preferred_element_type=jnp.float32)
            if masked:
                keep = allowed_mask(kb * block, start, scores.shape, prefix)
                scores = jnp.where(keep, scores, -1e30)
            new_top = jnp.maximum(top, jnp.max(scores, 0, keepdims=True))
            probs = jnp.exp2(scores - new_top)
            if masked:
                probs = jnp.where(keep, probs, 0.0)
            fade = jnp.exp2(top - new_top)
            total = total * fade + jnp.sum(probs, 0, keepdims=True)
            acc[...] = acc[...] * fade + jnp.dot(
                v_t[kb], probs.astype(jnp.bfloat16), preferred_element_type=jnp.float32
            )
            return (new_top, total)

        start_carry = (
            jnp.full((1, q_len), -1e30, jnp.float32),
            jnp.zeros((1, q_len), jnp.float32),
        )
        carry = lax.fori_loop(0, last, partial(step, masked=False), start_carry)
        top, total = step(last, carry, True)
        result = acc[...] / total
        for i in range(q_len // out_len):
            full_ref[n * (q_len // out_len) + i] = result[:, i * out_len : (i + 1) * out_len]
            out_ref[n * (q_len // out_len) + i] = result[
                :, i * out_len : (i + 1) * out_len
            ].astype(jnp.bfloat16)
        lse_ref[n] = top + jnp.log2(total)
        return 0

    lax.fori_loop(0, n_query, one_query, 0)


def attend(info, pieces, query, tok_b, block):
    total = len(pieces) * pieces[0].shape[-1]
    own = query is not None
    q_len = query.shape[1] if own else block
    n_query = 1 if own else total // block
    n_out = n_query * q_len // tok_b
    vmem = pl.BlockSpec(memory_space=pltpu.VMEM)
    return pl.pallas_call(
        partial(forward_kernel, len(pieces), own, tok_b, block),
        out_shape=(
            jax.ShapeDtypeStruct((n_out, HDIM, tok_b), jnp.bfloat16),
            jax.ShapeDtypeStruct((n_out, HDIM, tok_b), jnp.float32),
            jax.ShapeDtypeStruct((n_query, 1, q_len), jnp.float32),
        ),
        in_specs=[pl.BlockSpec(memory_space=pltpu.SMEM)] + [vmem] * (len(pieces) + own),
        out_specs=(vmem, vmem, vmem),
        scratch_shapes=[
            pltpu.VMEM((total // block, HDIM, block), jnp.bfloat16),
            pltpu.VMEM((total // block, block, HDIM), jnp.bfloat16),
            pltpu.VMEM((total // block, HDIM, block), jnp.bfloat16),
            pltpu.VMEM((HDIM, q_len), jnp.float32),
        ],
        compiler_params=pltpu.CompilerParams(vmem_limit_bytes=VMEM_LIMIT),
        cost_estimate=pl.CostEstimate(
            flops=n_query * q_len * total * HDIM * 8, bytes_accessed=4 << 20, transcendentals=0
        ),
    )(info, *pieces, *([query] if own else []))


def backward_kernel(n_pieces, own_query, tok_b, block, info, *refs):
    prefix, first = info[1], info[2]
    pieces = refs[:n_pieces]
    refs = refs[n_pieces:]
    if own_query:
        query_ref, refs = refs[0], refs[1:]
    full_ref, lse_ref, grad_ref = refs[:3]
    refs = refs[3:]
    total = n_pieces * pieces[0].shape[-1]
    q_len = lse_ref.shape[-1]
    n_query = lse_ref.shape[0]
    outs = refs[:n_pieces]
    refs = refs[n_pieces:]
    if own_query:
        dq_ref, refs = refs[0], refs[1:]
    q_t, q_n, k_t, k_n, v_n, g_t, g_n, delta, dq_t, dk, dv = refs
    key_slot = 0 if own_query else 1
    if own_query:
        q_t[0] = query_ref[...]
        q_n[0] = query_ref[...].T
    else:
        load_pieces(info, pieces, 0, q_t, q_n, tok_b, block)
    load_pieces(info, pieces, key_slot, k_t, k_n, tok_b, block)
    load_pieces(info, pieces, key_slot + 1, None, v_n, tok_b, block)
    per_query = q_len // tok_b
    for n in range(n_query):
        for i in range(per_query):
            number = n * per_query + i
            span = slice(i * tok_b, (i + 1) * tok_b)
            grad = grad_ref[number]
            g_t[n, :, span] = grad
            g_n[n, span, :] = grad.T
            delta[n, :, span] = jnp.sum(
                grad.astype(jnp.float32) * full_ref[number], 0, keepdims=True
            )
    dk[...] = jnp.zeros_like(dk)
    dv[...] = jnp.zeros_like(dv)
    dq_t[...] = jnp.zeros_like(dq_t)
    edge = prefix // block

    def one_query(n, carry):
        start = first + n * q_len
        last = jnp.maximum(start // block, edge)

        def step(kb, carry, masked):
            scores = jnp.dot(k_n[kb], q_t[n], preferred_element_type=jnp.float32)
            probs = jnp.exp2(scores - lse_ref[n])
            if masked:
                keep = allowed_mask(kb * block, start, scores.shape, prefix)
                probs = jnp.where(keep, probs, 0.0)
            d_probs = jnp.dot(v_n[kb], g_t[n], preferred_element_type=jnp.float32)
            d_scores = (probs * (d_probs - delta[n])).astype(jnp.bfloat16)
            dv[kb] += jnp.dot(
                probs.astype(jnp.bfloat16), g_n[n], preferred_element_type=jnp.float32
            )
            dk[kb] += jnp.dot(d_scores, q_n[n], preferred_element_type=jnp.float32)
            dq_t[n] += jnp.dot(k_t[kb], d_scores, preferred_element_type=jnp.float32)
            return carry

        lax.fori_loop(0, last, partial(step, masked=False), 0)
        step(last, 0, True)
        return 0

    lax.fori_loop(0, n_query, one_query, 0)
    rows = n_pieces
    per_block = block // tok_b
    for s, out in enumerate(outs):
        source = info[0] ^ s
        for c in range(total // rows // tok_b):
            number = (info[3] ^ c) * rows + source
            where = number // per_block
            offset = pl.multiple_of((number % per_block) * tok_b, tok_b)
            span = slice(c * tok_b, (c + 1) * tok_b)
            if not own_query:
                out[0, :, span] = (
                    dq_t[where, :, pl.ds(offset, tok_b)] * HDIM ** (-0.5)
                ).astype(jnp.bfloat16)
            out[key_slot, :, span] = (
                (dk[where, pl.ds(offset, tok_b), :] * LN2).astype(jnp.bfloat16).T
            )
            out[key_slot + 1, :, span] = (
                dv[where, pl.ds(offset, tok_b), :].astype(jnp.bfloat16).T
            )
    if own_query:
        dq_ref[...] = (dq_t[0] * HDIM ** (-0.5)).astype(jnp.bfloat16)


def attend_back(info, pieces, query, full, lse, grad, tok_b, block):
    total = len(pieces) * pieces[0].shape[-1]
    own = query is not None
    n_query, _, q_len = lse.shape
    vmem = pl.BlockSpec(memory_space=pltpu.VMEM)
    n_key = total // block
    out_shape = tuple(jax.ShapeDtypeStruct(p.shape, jnp.bfloat16) for p in pieces)
    if own:
        out_shape += (jax.ShapeDtypeStruct(query.shape, jnp.bfloat16),)
    return pl.pallas_call(
        partial(backward_kernel, len(pieces), own, tok_b, block),
        out_shape=out_shape,
        in_specs=[pl.BlockSpec(memory_space=pltpu.SMEM)] + [vmem] * (len(pieces) + own + 3),
        out_specs=(vmem,) * len(out_shape),
        scratch_shapes=[
            pltpu.VMEM((n_query, HDIM, q_len), jnp.bfloat16),
            pltpu.VMEM((n_query, q_len, HDIM), jnp.bfloat16),
            pltpu.VMEM((n_key, HDIM, block), jnp.bfloat16),
            pltpu.VMEM((n_key, block, HDIM), jnp.bfloat16),
            pltpu.VMEM((n_key, block, HDIM), jnp.bfloat16),
            pltpu.VMEM((n_query, HDIM, q_len), jnp.bfloat16),
            pltpu.VMEM((n_query, q_len, HDIM), jnp.bfloat16),
            pltpu.VMEM((n_query, 1, q_len), jnp.float32),
            pltpu.VMEM((n_query, HDIM, q_len), jnp.float32),
            pltpu.VMEM((n_key, block, HDIM), jnp.float32),
            pltpu.VMEM((n_key, block, HDIM), jnp.float32),
        ],
        compiler_params=pltpu.CompilerParams(vmem_limit_bytes=VMEM_LIMIT),
        cost_estimate=pl.CostEstimate(
            flops=n_query * q_len * total * HDIM * 20, bytes_accessed=4 << 20, transcendentals=0
        ),
    )(info, *pieces, *([query] if own else []), full, lse, grad)


def dot(left, right, left_dim, right_dim):
    return lax.dot_general(
        left,
        right,
        (((left_dim,), (right_dim,)), ((), ())),
        preferred_element_type=jnp.float32,
    )


def dp_swap(value):
    return lax.ppermute(value, "dp", [(0, 1), (1, 0)])


def col_send(value, pairs):
    return lax.ppermute(value, "col", pairs)


NEAR = [(0, 1), (1, 0), (2, 3), (3, 2)]
MIDDLE = [(1, 2), (2, 1)]


def line_gather(own, col):
    near = col_send(own, NEAR)
    mid = col_send(own, MIDDLE)
    first = col == 1
    left = col_send(jnp.where(first, mid, near), [(1, 0), (2, 1)])
    right = col_send(jnp.where(first, near, mid), [(1, 2), (2, 3)])
    two = jnp.where(col < 2, left, right)
    ends = col_send(two, [(1, 0), (2, 3)])
    three = jnp.where(first | (col == 2), mid, ends)
    return [own, near, two, three]


def add_low(left, right):
    return (left.astype(jnp.float32) + right.astype(jnp.float32)).astype(jnp.bfloat16)


def line_reduce(parts, col):
    first = col == 1
    ends = col_send(parts[3], [(0, 1), (3, 2)])
    second = add_low(parts[2], ends)
    right = col_send(second, [(0, 1), (1, 2)])
    left = col_send(second, [(3, 2), (2, 1)])
    near = col_send(add_low(parts[1], jnp.where(first, left, right)), NEAR)
    mid = col_send(add_low(parts[3], jnp.where(first, right, left)), MIDDLE)
    return parts[0].astype(jnp.float32) + near.astype(jnp.float32) + mid.astype(jnp.float32)


def col_exchange(parts):
    return [parts[0]] + [
        col_send(parts[s], [(i, i ^ s) for i in range(len(parts))]) for s in range(1, len(parts))
    ]


def sum_everywhere(values):
    for axis in ("row", "col"):
        for step in (1, 2):
            values = values + lax.ppermute(values, axis, [(i, i ^ step) for i in range(4)])
    return values + dp_swap(values)


def dp_scatter(values, dp, axis):
    half = values.shape[axis] // 2
    values = values.astype(jnp.bfloat16)
    own = lax.dynamic_slice_in_dim(values, dp * half, half, axis)
    other = lax.dynamic_slice_in_dim(values, (1 - dp) * half, half, axis)
    return add_low(own, dp_swap(other))


def dp_gather(half, dp, axis):
    other = dp_swap(half)
    return jnp.concatenate(
        [jnp.where(dp == 0, half, other), jnp.where(dp == 0, other, half)], axis
    )


def after(value, *earlier):
    return lax.optimization_barrier((value,) + earlier)[0]


def with_bias_rows(weight, bias):
    return jnp.concatenate(
        [weight, bias[None], jnp.zeros((PAD - 1, weight.shape[1]), weight.dtype)], 0
    )


def strip_tables(cols, wide):
    native = 3 * D // cols
    slots = wide + HDIM
    from_native = np.full((cols, cols, slots), -1, np.int32)
    to_strip = np.full((cols, cols, slots), -1, np.int32)
    for c in range(cols):
        for s in range(cols):
            for block, group, table in ((c, c ^ s, 0), (c ^ s, c, 1)):
                count = 0
                for i in range(3):
                    for place in range(wide + HDIM):
                        last = place >= wide
                        column = i * D + (D - HDIM + place - wide if last else group * wide + place)
                        if column // native != block:
                            continue
                        slot = wide + place - wide if last else count
                        count += not last
                        if table == 0:
                            from_native[c, s, slot] = column - block * native
                        else:
                            to_strip[c, s, slot] = (
                                3 * wide + i * HDIM + place - wide if last else i * wide + place
                            )
    return from_native.reshape(cols, -1), to_strip.reshape(cols, -1)


def one_hot(table, col, size):
    slots = pick(jnp.asarray(table), col)
    return (lax.broadcasted_iota(jnp.int32, (size, table.shape[1]), 0) == slots[None]).astype(
        jnp.bfloat16
    )


def head_shards(
    block_input,
    cotangent,
    prefix_len,
    first_gain,
    first_shift,
    qkv_weight,
    qkv_bias,
    out_weight,
    out_bias,
    second_gain,
    second_shift,
    up_weight,
    up_bias,
    down_weight,
    down_bias,
):
    rows = lax.axis_size("row")
    cols = lax.axis_size("col")
    row = lax.axis_index("row")
    col = lax.axis_index("col")
    dp = lax.axis_index("dp")
    tok_a = block_input.shape[1]
    tok_b = tok_a // rows
    feat = block_input.shape[2]
    block = 2 * tok_b
    wide = rows * HDIM
    slots = wide + HDIM
    hidden_len = up_weight.shape[1]
    from_native, to_strip = strip_tables(cols, wide)

    narrow = jnp.stack(
        [first_gain, first_shift, out_bias, second_gain, second_shift, down_bias]
        + [jnp.zeros_like(first_gain)] * 2
    )
    narrow_all = jnp.concatenate(in_order(row_gather(narrow), row), 1)

    def to_tokens(values):
        tiles = values.reshape(rows, tok_b, feat)
        got = row_exchange([pick(tiles, row ^ s) for s in range(rows)])
        return jnp.concatenate(in_order(got, row), 1)

    def to_features(values):
        tiles = [
            lax.dynamic_slice_in_dim(values, (row ^ s) * feat, feat, 1) for s in range(rows)
        ]
        return jnp.concatenate(in_order(row_exchange(tiles), row), 0)

    x_tok = to_tokens(block_input[0]).astype(jnp.float32)
    normed_one, centred_one, inv_one = layer_norm(x_tok, narrow_all[0], narrow_all[1])
    normed_one = normed_one.astype(jnp.bfloat16)
    normed_parts = line_gather(normed_one, col)

    spread = one_hot(from_native, col, qkv_weight.shape[1])
    sent = dot(with_bias_rows(qkv_weight, qkv_bias), spread, 1, 0).astype(jnp.bfloat16)
    got = col_exchange([sent[:, s * slots : (s + 1) * slots] for s in range(cols)])
    placed = one_hot(to_strip, col, 3 * slots)
    strip = sum(
        dot(g, placed[:, s * slots : (s + 1) * slots], 1, 1) for s, g in enumerate(got)
    ).astype(jnp.bfloat16)
    strip_rows = in_order(row_gather(strip), row)
    qkv_strip = jnp.concatenate([s[:feat] for s in strip_rows], 0)
    strip_bias = strip[feat].astype(jnp.float32)

    out_cols = lax.all_gather(out_weight.T, "col")
    out_rows = out_cols.transpose(1, 0, 2).reshape(feat, -1)
    out_full = jnp.concatenate(in_order(row_gather(out_rows), row), 0)

    query_scale = LOG2E * HDIM ** (-0.5)
    scale = jnp.concatenate(
        [
            jnp.full((wide,), query_scale, jnp.float32),
            jnp.ones((2 * wide,), jnp.float32),
            jnp.full((HDIM,), query_scale, jnp.float32),
            jnp.ones((2 * HDIM,), jnp.float32),
        ]
    )
    normed_set = jnp.concatenate(normed_parts, 0)
    mixed = (
        (dot(qkv_strip, normed_set, 0, 1) + strip_bias[:, None]) * scale[:, None]
    ).astype(jnp.bfloat16)
    by_head = mixed[: 3 * wide].reshape(3, rows, HDIM, tok_a)
    pieces = row_exchange([pick(by_head, row ^ s, 1) for s in range(rows)])
    last_query = mixed[3 * wide : 3 * wide + HDIM, :tok_b]
    last_pieces = row_gather(after(mixed[3 * wide + HDIM :], pieces[3]).reshape(2, HDIM, tok_a))

    def hidden_slice(native, earlier):
        half = native.shape[0] // 2
        mine = after(lax.dynamic_slice_in_dim(native, dp * half, half, 0), earlier)
        blocks = lax.all_gather(mine, "col")
        got = row_exchange([pick(blocks, row ^ s) for s in range(rows)])
        got = jnp.stack(in_order(got, row))
        return blocks, dp_gather(got, dp, 1)

    up_blocks, up_got = hidden_slice(with_bias_rows(up_weight, up_bias), normed_parts[3])
    up_slice = up_got[:, :feat].reshape(rows * feat, hidden_len)
    up_slice_bias = up_got[0, feat].astype(jnp.float32)
    _, down_got = hidden_slice(down_weight.T, up_blocks)
    down_slice = down_got.reshape(rows * feat, hidden_len)

    cot_tok = to_tokens(after(cotangent[0], x_tok))
    cot_all = jnp.concatenate(row_gather(cot_tok), 0)

    zero = jnp.int32(0)
    info = jnp.stack([row, prefix_len[0], zero, col])
    last_info = jnp.stack([row, prefix_len[0], col * tok_a + row * tok_b, col])
    heads_out, heads_full, heads_lse = attend(info, pieces, None, tok_b, block)
    last_out, last_full, last_lse = attend(last_info, last_pieces, last_query, tok_b, block)
    attended = jnp.concatenate(
        [
            lax.all_to_all(heads_out, ("col", "row"), 0, 0, tiled=True).reshape(-1, tok_b),
            last_out[0],
        ],
        0,
    )
    residual = x_tok + dot(attended, out_full, 0, 1) + narrow_all[2]
    normed_two, centred_two, inv_two = layer_norm(residual, narrow_all[3], narrow_all[4])
    normed_two = jnp.concatenate(row_gather(normed_two.astype(jnp.bfloat16)), 0)
    hidden = dot(normed_two, up_slice, 1, 0) + up_slice_bias
    active, gelu_back = jax.vjp(partial(jax.nn.gelu, approximate=False), hidden)
    active = active.astype(jnp.bfloat16)
    d_active = dot(cot_all, down_slice, 1, 0)
    d_hidden = gelu_back(d_active)[0].astype(jnp.bfloat16)

    def token_parts(values):
        return [values[s * tok_b : (s + 1) * tok_b] for s in range(rows)]

    d_norm_two = row_reduce(token_parts(dot(d_hidden, up_slice, 1, 1)))
    d_residual = cot_tok.astype(jnp.float32) + layer_norm_back(
        d_norm_two, centred_two, inv_two, narrow_all[3]
    )
    branch = d_residual.astype(jnp.bfloat16)
    d_attended = dot(out_full, branch, 0, 1).astype(jnp.bfloat16)
    d_heads = lax.all_to_all(
        d_attended[: D - HDIM].reshape(rows * cols, HDIM, tok_b), ("col", "row"), 0, 0, tiled=True
    )
    *last_grads, d_last_query = attend_back(
        last_info,
        last_pieces,
        last_query,
        last_full,
        last_lse,
        d_attended[D - HDIM :][None],
        tok_b,
        block,
    )
    head_grads = attend_back(info, pieces, None, heads_full, heads_lse, d_heads, tok_b, block)
    d_last_keys = row_reduce([after(g, d_heads) for g in last_grads]).astype(jnp.bfloat16)

    partial_out = dot(after(active, d_heads), down_slice, 1, 1)
    block_output = to_features(
        (row_reduce(token_parts(partial_out)) + residual + narrow_all[5]).astype(jnp.bfloat16)
    )

    def hidden_grad(left, right):
        whole = dot(left, right, 0, 0).reshape(rows, feat, hidden_len)
        half = dp_scatter(whole, dp, 1)
        return jnp.stack(
            in_order(row_exchange([pick(half, row ^ s) for s in range(rows)]), row)
        )

    up_half = lax.psum_scatter(
        hidden_grad(normed_two, d_hidden), "col", scatter_dimension=0
    )
    up_grad = dp_gather(up_half, dp, 0).astype(jnp.float32)
    out_part = dp_scatter(dot(branch, attended, 0, 1).reshape(rows, feat, -1), dp, 1)
    out_sum = row_reduce([pick(out_part, row ^ s) for s in range(rows)]).astype(jnp.bfloat16)
    out_got = out_sum.reshape(feat // 2, cols, -1).transpose(1, 0, 2)
    down_out_half = lax.psum_scatter(
        jnp.concatenate([hidden_grad(cot_all, active), out_got], 2), "col", scatter_dimension=0
    )
    down_out_grad = dp_gather(down_out_half, dp, 0).astype(jnp.float32)

    got = jnp.stack(in_order(row_exchange(list(head_grads)), row), 1)
    d_mixed = jnp.concatenate(
        [
            got.reshape(3 * wide, tok_a),
            jnp.concatenate(
                [d_last_query, jnp.zeros((HDIM, tok_a - tok_b), jnp.bfloat16)], 1
            ),
            d_last_keys.reshape(2 * HDIM, tok_a),
        ],
        0,
    )
    d_norm_one = line_reduce(
        [
            dot(d_mixed[:, s * tok_b : (s + 1) * tok_b], qkv_strip, 0, 1).astype(jnp.bfloat16)
            for s in range(cols)
        ],
        col,
    )
    qkv_part = dp_scatter(dot(normed_set, d_mixed, 0, 1).reshape(rows, feat, -1), dp, 1)
    qkv_sum = row_reduce([pick(qkv_part, row ^ s) for s in range(rows)]).astype(jnp.bfloat16)
    got = col_exchange(
        [
            dot(qkv_sum, placed[:, s * slots : (s + 1) * slots], 1, 0).astype(jnp.bfloat16)
            for s in range(cols)
        ]
    )
    qkv_half = sum(
        dot(g, spread[:, s * slots : (s + 1) * slots], 1, 1) for s, g in enumerate(got)
    ).astype(jnp.bfloat16)
    qkv_grad = dp_gather(qkv_half, dp, 0).astype(jnp.float32)
    input_grad = d_residual + layer_norm_back(d_norm_one, centred_one, inv_one, narrow_all[0])
    input_grad = to_features(input_grad.astype(jnp.bfloat16)).astype(jnp.float32)

    at_row = (jnp.arange(rows) == row)[:, None]

    def own_row(values):
        return jnp.where(at_row, values[None], 0.0).reshape(-1)

    bias_strip = jnp.sum(d_mixed.astype(jnp.float32), 1)
    at_col = (jnp.arange(cols) == col)[None, :, None]
    bias_heads = jnp.where(at_col, bias_strip[: 3 * wide].reshape(3, 1, wide), 0.0)
    bias_all = jnp.concatenate(
        [bias_heads.reshape(3, -1), bias_strip[3 * wide :].reshape(3, HDIM)], 1
    ).reshape(-1)
    early = [
        own_row(jnp.sum(cotangent[0].astype(jnp.float32), 0)),
        jnp.sum(branch.astype(jnp.float32), 0),
        jnp.sum(d_norm_two * centred_two, 0),
        jnp.sum(d_norm_two, 0),
        own_row(jnp.sum(d_hidden.astype(jnp.float32), 0)),
        bias_all,
        jnp.sum(d_norm_one * centred_one, 0),
        jnp.sum(d_norm_one, 0),
    ]
    total = sum_everywhere(jnp.concatenate(early).reshape(8, -1)).reshape(-1)

    def own_part(start, size, index):
        return lax.dynamic_slice_in_dim(total, start + index * size, size, 0)

    width = rows * feat
    up_at = 4 * width
    qkv_at = up_at + rows * hidden_len
    first_at = qkv_at + 3 * width
    return (
        block_output[None],
        input_grad[None],
        own_part(first_at, feat, row),
        own_part(first_at + width, feat, row),
        qkv_grad,
        own_part(qkv_at, 3 * width // cols, col),
        down_out_grad[:, hidden_len:].T,
        own_part(width, feat, row),
        own_part(2 * width, feat, row),
        own_part(3 * width, feat, row),
        up_grad,
        own_part(up_at, hidden_len, col),
        down_out_grad[:, :hidden_len].T,
        own_part(0, feat, row),
    )


def solution(mesh):
    in_specs = (
        P("dp", "col", "row"),
        P("dp", "col", "row"),
        P("dp"),
        P("row"),
        P("row"),
        P("row", "col"),
        P("col"),
        P("col", "row"),
        P("row"),
        P("row"),
        P("row"),
        P("row", "col"),
        P("col"),
        P("col", "row"),
        P("row"),
    )
    out_specs = (
        P("dp", "col", "row"),
        P("dp", "col", "row"),
        P("row"),
        P("row"),
        P("row", "col"),
        P("col"),
        P("col", "row"),
        P("row"),
        P("row"),
        P("row"),
        P("row", "col"),
        P("col"),
        P("col", "row"),
        P("row"),
    )
    one_head_each = mesh.shape["row"] == 4 and mesh.shape["col"] == 4 and mesh.shape["dp"] == 2
    body = head_shards if one_head_each else shards
    return jax.shard_map(body, mesh=mesh, in_specs=in_specs, out_specs=out_specs, check_vma=False)
```

```python
from functools import partial

import jax
import jax.numpy as jnp
import numpy as np
from jax import lax
from jax.experimental import pallas as pl
from jax.experimental.pallas import tpu as pltpu
from jax.sharding import PartitionSpec as P

HEADS = 17
HDIM = 64
D = 1088


def positions(first_row, piece_len, tok_b, tok_a, col_total):
    flat_rows = first_row + jnp.arange(piece_len, dtype=jnp.int32)
    shard_no = flat_rows // tok_b
    return shard_no % col_total * tok_a + shard_no // col_total * tok_b + flat_rows % tok_b


def over_blocks(folded, pieces, step_fn):
    piece_len = pieces[0].shape[0]
    block_len = 512

    def one_block(block_no, running):
        offset = block_no * block_len
        sliced = tuple(
            (lax.dynamic_slice_in_dim(member, offset, block_len, 0) for member in pieces)
        )
        return step_fn(running, sliced, offset)

    return lax.fori_loop(0, piece_len // block_len, one_block, folded)


def head_scores(left, right, scale_factor):
    return (
        jnp.einsum("qhd,khd->hqk", left, right, preferred_element_type=jnp.float32) * scale_factor
    )


def normalize(values, norm_gain, norm_shift):
    width_all = values.shape[1] * lax.axis_size("row")
    row_sums = lax.psum((jnp.sum(values, 1), jnp.sum(values * values, 1)), "row")
    row_mean = row_sums[0] / width_all
    variance = row_sums[1] / width_all - row_mean * row_mean
    inv_std = lax.rsqrt(variance + 1e-05)
    centred = (values - row_mean[:, None]) * inv_std[:, None]
    return (centred * norm_gain + norm_shift, centred, inv_std)


def norm_back(d_normed, centred, inv_std, norm_gain):
    width_all = d_normed.shape[1] * lax.axis_size("row")
    scaled = d_normed * norm_gain
    row_sums = lax.psum((jnp.sum(scaled, 1), jnp.sum(scaled * centred, 1)), "row")
    d_values = inv_std[:, None] * (
        scaled - row_sums[0][:, None] / width_all - centred * row_sums[1][:, None] / width_all
    )
    return (d_values, jnp.sum(d_normed * centred, 0), jnp.sum(d_normed, 0))


def row_partials(term_fn, tok_b):
    return lax.psum_scatter(
        term_fn(jnp.int32(0), tok_b * lax.axis_size("row")).astype(jnp.bfloat16),
        "row",
        scatter_dimension=0,
        tiled=True,
    ).astype(jnp.float32)


def rows_gather(values):
    return lax.all_gather(values, "row", axis=0, tiled=True)


def row_product(normed_low, weight, tok_b):

    def term_fn(first_row, row_count):
        return jnp.dot(normed_low, weight, preferred_element_type=jnp.float32)

    return row_partials(term_fn, tok_b)


def back_product(grad_low, weight, tok_b):

    def term_fn(first_row, row_count):
        return lax.dot_general(
            grad_low, weight, (((1,), (1,)), ((), ())), preferred_element_type=jnp.float32
        )

    return row_partials(term_fn, tok_b)


def fold_back(grad_rows, normed_low, weight_full):
    piece = lax.all_gather(grad_rows, "row", axis=0, tiled=True)
    contrib = lax.dot_general(
        piece, weight_full, (((1,), (1,)), ((), ())), preferred_element_type=jnp.float32
    )
    d_weight = lax.dot_general(
        normed_low, piece, (((0,), (0,)), ((), ())), preferred_element_type=jnp.float32
    )
    return (contrib, d_weight, jnp.sum(piece.astype(jnp.float32), 0))


def scatter_columns(gradients):
    return (
        lax.psum_scatter(
            gradients[0].astype(jnp.bfloat16), "col", scatter_dimension=1, tiled=True
        ).astype(jnp.float32),
        lax.psum_scatter(
            gradients[1].astype(jnp.bfloat16), "col", scatter_dimension=0, tiled=True
        ).astype(jnp.float32),
        lax.psum_scatter(
            gradients[2].astype(jnp.bfloat16), "col", scatter_dimension=0, tiled=True
        ).astype(jnp.float32),
        lax.psum_scatter(
            gradients[3].astype(jnp.bfloat16), "col", scatter_dimension=1, tiled=True
        ).astype(jnp.float32),
        lax.psum_scatter(
            gradients[4].astype(jnp.bfloat16), "col", scatter_dimension=0, tiled=True
        ).astype(jnp.float32),
        lax.psum_scatter(
            gradients[5].astype(jnp.bfloat16), "col", scatter_dimension=0, tiled=True
        ).astype(jnp.float32),
    )


def sum_over_data(gradients):
    return (
        lax.psum(gradients[0].astype(jnp.bfloat16), "dp").astype(jnp.float32),
        lax.psum(gradients[1].astype(jnp.bfloat16), "dp").astype(jnp.float32),
        lax.psum(gradients[2].astype(jnp.bfloat16), "dp").astype(jnp.float32),
        lax.psum(gradients[3].astype(jnp.bfloat16), "dp").astype(jnp.float32),
        lax.psum(gradients[4].astype(jnp.bfloat16), "dp").astype(jnp.float32),
        lax.psum(gradients[5].astype(jnp.bfloat16), "dp").astype(jnp.float32),
    )


def shards(
    block_input,
    cotangent,
    prefix_len,
    first_gain,
    first_shift,
    qkv_weight,
    qkv_bias,
    out_weight,
    out_bias,
    second_gain,
    second_shift,
    up_weight,
    up_bias,
    down_weight,
    down_bias,
):
    row_total = lax.axis_size("row")
    col_total = lax.axis_size("col")
    tok_a = block_input.shape[1]
    tok_b = tok_a // row_total
    scale_factor = HDIM ** (-0.5)
    gathered = (
        lax.all_gather(qkv_weight, "col", axis=1, tiled=True),
        lax.all_gather(qkv_bias, "col", axis=0, tiled=True),
        lax.all_gather(out_weight, "col", axis=0, tiled=True),
        lax.all_gather(up_weight, "col", axis=1, tiled=True),
        lax.all_gather(up_bias, "col", axis=0, tiled=True),
        lax.all_gather(down_weight, "col", axis=0, tiled=True),
    )
    qkv_full, qkv_bias_full, out_full, up_full, up_bias_full, down_full = gathered
    residual = block_input[0].astype(jnp.float32)
    prefix_end = prefix_len[0]
    own_pos = (
        lax.axis_index("col") * tok_a
        + lax.axis_index("row") * tok_b
        + jnp.arange(tok_b, dtype=jnp.int32)
    )

    def visible(key_pos, query_pos):
        return (key_pos[None, :] < prefix_end) | (key_pos[None, :] <= query_pos[:, None])

    def piece_pos(first_row, piece_len):
        return positions(first_row, piece_len, tok_b, tok_a, col_total)

    normed_one, centred_one, inv_one = normalize(residual, first_gain, first_shift)
    normed_one_low = normed_one.astype(jnp.bfloat16)
    mixed_qkv = (
        row_product(normed_one_low, qkv_full, tok_b) + qkv_bias_full.astype(jnp.float32)
    ).astype(jnp.bfloat16)
    query_rows = mixed_qkv[:, :D]
    key_rows = mixed_qkv[:, D : 2 * D]
    value_rows = mixed_qkv[:, 2 * D :]
    own_query = query_rows.reshape(tok_b, HEADS, HDIM)
    own_key = key_rows.reshape(tok_b, HEADS, HDIM)
    own_value = value_rows.reshape(tok_b, HEADS, HDIM)

    def max_step(running, sliced, first_row):
        key_block = sliced[0]
        allowed = visible(piece_pos(first_row, key_block.shape[0]), own_pos)
        scores = jnp.where(
            allowed[None],
            head_scores(own_query, key_block.reshape(-1, HEADS, HDIM), scale_factor),
            -1e30,
        )
        new_max = jnp.maximum(running[0], jnp.max(scores, 2))
        new_total = running[1] * jnp.exp(running[0] - new_max) + jnp.sum(
            jnp.where(allowed[None], jnp.exp(scores - new_max[:, :, None]), 0.0), 2
        )
        return (new_max, new_total)

    start_max = (
        jnp.full((HEADS, tok_b), -1e30, jnp.float32),
        jnp.zeros((HEADS, tok_b), jnp.float32),
    )
    run_max, run_total = over_blocks(
        start_max, (lax.all_gather(key_rows, ("row", "col"), axis=0, tiled=True),), max_step
    )
    log_total = run_max + jnp.log(run_total)

    def value_step(running, sliced, first_row):
        key_block, value_block = sliced
        allowed = visible(piece_pos(first_row, key_block.shape[0]), own_pos)
        scores = head_scores(own_query, key_block.reshape(-1, HEADS, HDIM), scale_factor)
        attn_probs = jnp.where(allowed[None], jnp.exp(scores - log_total[:, :, None]), 0.0).astype(
            jnp.bfloat16
        )
        return running + jnp.einsum(
            "hqk,khd->qhd",
            attn_probs,
            value_block.reshape(-1, HEADS, HDIM),
            preferred_element_type=jnp.float32,
        )

    attn_acc = over_blocks(
        jnp.zeros((tok_b, HEADS, HDIM), jnp.float32),
        (
            lax.all_gather(key_rows, ("row", "col"), axis=0, tiled=True),
            lax.all_gather(value_rows, ("row", "col"), axis=0, tiled=True),
        ),
        value_step,
    )
    attn_float = attn_acc.reshape(tok_b, D)
    attn_all = rows_gather(attn_float.astype(jnp.bfloat16))
    residual_two = (
        residual + jnp.dot(attn_all, out_full, preferred_element_type=jnp.float32) + out_bias
    )
    normed_two, centred_two, inv_two = normalize(residual_two, second_gain, second_shift)
    normed_two_low = normed_two.astype(jnp.bfloat16)
    hidden = row_product(normed_two_low, up_full, tok_b) + up_bias_full.astype(jnp.float32)
    active_all = rows_gather(jax.nn.gelu(hidden, approximate=False).astype(jnp.bfloat16))
    block_output = (
        residual_two
        + jnp.dot(active_all, down_full, preferred_element_type=jnp.float32)
        + down_bias
    ).astype(jnp.bfloat16)
    cot_low = cotangent[0]
    cot_float = cot_low.astype(jnp.float32)
    down_grad = lax.dot_general(
        active_all, cot_low, (((0,), (0,)), ((), ())), preferred_element_type=jnp.float32
    )
    down_bias_grad = jnp.sum(cot_float, 0)
    d_active = back_product(cot_low, down_full, tok_b)
    gelu_back = jax.vjp(partial(jax.nn.gelu, approximate=False), hidden)[1]
    d_hidden_low = gelu_back(d_active)[0].astype(jnp.bfloat16)
    d_norm_two, up_grad, up_bias_grad = fold_back(d_hidden_low, normed_two_low, up_full)
    d_part_two, second_gain_grad, second_shift_grad = norm_back(
        d_norm_two, centred_two, inv_two, second_gain
    )
    d_residual = cot_float + d_part_two
    branch_low = d_residual.astype(jnp.bfloat16)
    out_grad = lax.dot_general(
        attn_all, branch_low, (((0,), (0,)), ((), ())), preferred_element_type=jnp.float32
    )
    out_bias_grad = jnp.sum(branch_low.astype(jnp.float32), 0)
    d_attn_low = back_product(branch_low, out_full, tok_b).astype(jnp.bfloat16)
    delta_rows = jnp.sum(
        (d_attn_low.astype(jnp.float32) * attn_float).reshape(tok_b, HEADS, HDIM), 2
    )
    lse_rows = log_total.T
    all_lse, all_delta = (
        lax.all_gather(lse_rows, ("row", "col"), axis=0, tiled=True),
        lax.all_gather(delta_rows, ("row", "col"), axis=0, tiled=True),
    )
    own_grad = d_attn_low.reshape(tok_b, HEADS, HDIM)

    def back_step(running, sliced, first_row):
        query_p, key_p, value_p, grad_p = sliced
        piece_len = query_p.shape[0]
        pos_piece = piece_pos(first_row, piece_len)
        lse_piece = lax.dynamic_slice_in_dim(all_lse, first_row, piece_len, 0)
        delta_piece = lax.dynamic_slice_in_dim(all_delta, first_row, piece_len, 0)
        query_p3 = query_p.reshape(piece_len, HEADS, HDIM)
        key_p3 = key_p.reshape(piece_len, HEADS, HDIM)
        value_p3 = value_p.reshape(piece_len, HEADS, HDIM)
        grad_p3 = grad_p.reshape(piece_len, HEADS, HDIM)
        allowed_own = visible(pos_piece, own_pos)
        allowed_far = visible(own_pos, pos_piece)
        scores = head_scores(own_query, key_p3, scale_factor)
        attn_probs = jnp.where(allowed_own[None], jnp.exp(scores - log_total[:, :, None]), 0.0)
        d_probs = jnp.einsum("qhd,khd->hqk", own_grad, value_p3, preferred_element_type=jnp.float32)
        d_scores = (attn_probs * (d_probs - delta_rows.T[:, :, None])).astype(jnp.bfloat16)
        new_query = (
            running[0]
            + jnp.einsum("hqk,khd->qhd", d_scores, key_p3, preferred_element_type=jnp.float32)
            * scale_factor
        )
        scores = head_scores(query_p3, own_key, scale_factor)
        attn_probs = jnp.where(allowed_far[None], jnp.exp(scores - lse_piece.T[:, :, None]), 0.0)
        d_value = running[2] + jnp.einsum(
            "hqk,qhd->khd",
            attn_probs.astype(jnp.bfloat16),
            grad_p3,
            preferred_element_type=jnp.float32,
        )
        d_probs = jnp.einsum("qhd,khd->hqk", grad_p3, own_value, preferred_element_type=jnp.float32)
        d_scores = (attn_probs * (d_probs - delta_piece.T[:, :, None])).astype(jnp.bfloat16)
        d_key = (
            running[1]
            + jnp.einsum("hqk,qhd->khd", d_scores, query_p3, preferred_element_type=jnp.float32)
            * scale_factor
        )
        return (new_query, d_key, d_value)

    zero_heads = jnp.zeros((tok_b, HEADS, HDIM), jnp.float32)
    d_query, d_key, d_value = over_blocks(
        (zero_heads, zero_heads, zero_heads),
        (
            lax.all_gather(query_rows, ("row", "col"), axis=0, tiled=True),
            lax.all_gather(key_rows, ("row", "col"), axis=0, tiled=True),
            lax.all_gather(value_rows, ("row", "col"), axis=0, tiled=True),
            lax.all_gather(d_attn_low, ("row", "col"), axis=0, tiled=True),
        ),
        back_step,
    )
    d_mixed_low = jnp.concatenate(
        [d_query.reshape(tok_b, D), d_key.reshape(tok_b, D), d_value.reshape(tok_b, D)], 1
    ).astype(jnp.bfloat16)
    d_norm_one, qkv_grad, qkv_bias_grad = fold_back(d_mixed_low, normed_one_low, qkv_full)
    d_part_one, first_gain_grad, first_shift_grad = norm_back(
        d_norm_one, centred_one, inv_one, first_gain
    )
    input_grad = d_residual + d_part_one
    col_ready = (qkv_grad, qkv_bias_grad, out_grad, up_grad, up_bias_grad, down_grad)
    reduced = scatter_columns(sum_over_data(col_ready))
    small = lax.psum(
        (
            first_gain_grad,
            first_shift_grad,
            out_bias_grad,
            second_gain_grad,
            second_shift_grad,
            down_bias_grad,
        ),
        ("dp", "col"),
    )
    return (
        block_output[None],
        input_grad[None],
        small[0],
        small[1],
        reduced[0],
        reduced[1],
        reduced[2],
        small[2],
        small[3],
        small[4],
        reduced[3],
        reduced[4],
        reduced[5],
        small[5],
    )


LOG2E = 1.4426950408889634
LN2 = 0.6931471805599453
PAD = 16
MEBI = 1024 * 1024
VMEM_LIMIT = 56 * MEBI


def swap(value, step):
    size = lax.axis_size("row")
    return lax.ppermute(value, "row", [(i, i ^ step) for i in range(size)])


def pick(stacked, index, axis=0):
    return lax.dynamic_index_in_dim(stacked, index, axis, keepdims=False)


def row_gather(own):
    far = swap(own, 2)
    return [own, swap(own, 1), far, swap(far, 1)]


def row_exchange(parts):
    return [parts[0], swap(parts[1], 1), swap(parts[2], 2), swap(parts[3], 3)]


def row_reduce_parts(parts):
    low = [p.astype(jnp.bfloat16) for p in parts]
    beyond = swap(low[3], 1)
    near = swap(low[1], 1)
    far = swap(add_low(parts[2], beyond), 2)
    return [parts[0], near, far]


def row_reduce(parts):
    return sum(p.astype(jnp.float32) for p in row_reduce_parts(parts))


def in_order(parts, me):
    stacked = jnp.stack(parts)
    return [pick(stacked, me ^ i) for i in range(len(parts))]


def layer_norm(values, gain, shift):
    mean = jnp.mean(values, 1, keepdims=True)
    variance = jnp.mean(values * values, 1, keepdims=True) - mean * mean
    inv_std = lax.rsqrt(variance + 1e-05)
    centred = (values - mean) * inv_std
    return (centred * gain + shift, centred, inv_std)


def layer_norm_back(d_normed, centred, inv_std, gain):
    scaled = d_normed * gain
    return inv_std * (
        scaled
        - jnp.mean(scaled, 1, keepdims=True)
        - centred * jnp.mean(scaled * centred, 1, keepdims=True)
    )


def load_pieces(info, pieces, slot, transposed, plain, tok_b, block):
    rows = 4
    groups = len(pieces) // rows
    cols = pieces[0].shape[-1] // tok_b
    per_block = block // tok_b
    for p, piece in enumerate(pieces):
        source = info[0] ^ (p // groups)
        for c in range(cols):
            part = piece[slot, :, c * tok_b : (c + 1) * tok_b]
            number = (info[3] ^ (p % groups * cols + c)) * rows + source
            where = number // per_block
            offset = pl.multiple_of((number % per_block) * tok_b, tok_b)
            if transposed is not None:
                transposed[where, :, pl.ds(offset, tok_b)] = part
            if plain is not None:
                plain[where, pl.ds(offset, tok_b), :] = part.T


def allowed_mask(key_start, query_start, shape, prefix):
    key_pos = key_start + lax.broadcasted_iota(jnp.int32, shape, 0)
    query_pos = query_start + lax.broadcasted_iota(jnp.int32, shape, 1)
    return (key_pos < prefix) | (key_pos <= query_pos)


def forward_kernel(n_pieces, own_query, n_earlier, tok_b, block, info, *refs):
    prefix, first = info[1], info[2]
    pieces = refs[:n_pieces]
    refs = refs[n_pieces:]
    if own_query:
        query_ref, refs = refs[0], refs[1:]
        q_len = query_ref.shape[1]
        n_query = 1
    else:
        q_len = block
        n_query = n_pieces * pieces[0].shape[-1] // block
    out_ref, full_ref, lse_ref, q_t, k_n, v_t, acc = refs[n_earlier:]
    key_slot = 0 if own_query else 1
    if not own_query:
        load_pieces(info, pieces, 0, q_t, None, tok_b, block)
    load_pieces(info, pieces, key_slot, None, k_n, tok_b, block)
    load_pieces(info, pieces, key_slot + 1, v_t, None, tok_b, block)
    edge = prefix // block
    out_len = out_ref.shape[-1]

    def one_query(n, carry):
        start = first + n * q_len
        query = query_ref[...] if own_query else q_t[n]
        last = jnp.maximum(start // block, edge)
        acc[...] = jnp.zeros_like(acc)

        def step(kb, carry, masked):
            top, total = carry
            scores = jnp.dot(k_n[kb], query, preferred_element_type=jnp.float32)
            if masked:
                keep = allowed_mask(kb * block, start, scores.shape, prefix)
                scores = jnp.where(keep, scores, -1e30)
            new_top = jnp.maximum(top, jnp.max(scores, 0, keepdims=True))
            probs = jnp.exp2(scores - new_top)
            if masked:
                probs = jnp.where(keep, probs, 0.0)
            fade = jnp.exp2(top - new_top)
            total = total * fade + jnp.sum(probs, 0, keepdims=True)
            acc[...] = acc[...] * fade + jnp.dot(
                v_t[kb], probs.astype(jnp.bfloat16), preferred_element_type=jnp.float32
            )
            return (new_top, total)

        start_carry = (
            jnp.full((1, q_len), -1e30, jnp.float32),
            jnp.zeros((1, q_len), jnp.float32),
        )
        carry = lax.fori_loop(0, last, partial(step, masked=False), start_carry)
        top, total = step(last, carry, True)
        result = acc[...] / total
        for i in range(q_len // out_len):
            full_ref[n * (q_len // out_len) + i] = result[:, i * out_len : (i + 1) * out_len]
            out_ref[n * (q_len // out_len) + i] = result[
                :, i * out_len : (i + 1) * out_len
            ].astype(jnp.bfloat16)
        lse_ref[n] = top + jnp.log2(total)
        return 0

    lax.fori_loop(0, n_query, one_query, 0)


def attend(info, pieces, query, tok_b, block, earlier=()):
    total = len(pieces) * pieces[0].shape[-1]
    own = query is not None
    q_len = query.shape[1] if own else block
    n_query = 1 if own else total // block
    n_out = n_query * q_len // tok_b
    vmem = pl.BlockSpec(memory_space=pltpu.VMEM)
    return pl.pallas_call(
        partial(forward_kernel, len(pieces), own, len(earlier), tok_b, block),
        out_shape=(
            jax.ShapeDtypeStruct((n_out, HDIM, tok_b), jnp.bfloat16),
            jax.ShapeDtypeStruct((n_out, HDIM, tok_b), jnp.float32),
            jax.ShapeDtypeStruct((n_query, 1, q_len), jnp.float32),
        ),
        in_specs=[IN_SMEM] + [vmem] * (len(pieces) + own) + [ANY] * len(earlier),
        out_specs=(vmem, vmem, vmem),
        scratch_shapes=[
            pltpu.VMEM((total // block, HDIM, block), jnp.bfloat16),
            pltpu.VMEM((total // block, block, HDIM), jnp.bfloat16),
            pltpu.VMEM((total // block, HDIM, block), jnp.bfloat16),
            pltpu.VMEM((HDIM, q_len), jnp.float32),
        ],
        compiler_params=pltpu.CompilerParams(vmem_limit_bytes=VMEM_LIMIT),
        cost_estimate=pl.CostEstimate(
            flops=n_query * q_len * total * 1700, bytes_accessed=4 << 20, transcendentals=0
        ),
    )(info, *pieces, *([query] if own else []), *earlier)


def backward_kernel(n_pieces, own_query, tok_b, block, info, *refs):
    prefix, first = info[1], info[2]
    pieces = refs[:n_pieces]
    refs = refs[n_pieces:]
    if own_query:
        query_ref, refs = refs[0], refs[1:]
    full_ref, lse_ref, grad_ref = refs[:3]
    refs = refs[3:]
    total = n_pieces * pieces[0].shape[-1]
    rows = 4
    q_len = lse_ref.shape[-1]
    n_query = lse_ref.shape[0]
    outs = refs[:rows]
    refs = refs[rows:]
    if own_query:
        dq_ref, refs = refs[0], refs[1:]
    q_t, q_n, k_t, k_n, v_n, g_t, g_n, delta, dq_t, dk, dv = refs
    key_slot = 0 if own_query else 1
    if own_query:
        q_t[0] = query_ref[...]
        q_n[0] = query_ref[...].T
    else:
        load_pieces(info, pieces, 0, q_t, q_n, tok_b, block)
    load_pieces(info, pieces, key_slot, k_t, k_n, tok_b, block)
    load_pieces(info, pieces, key_slot + 1, None, v_n, tok_b, block)
    per_query = q_len // tok_b
    for n in range(n_query):
        for i in range(per_query):
            number = n * per_query + i
            span = slice(i * tok_b, (i + 1) * tok_b)
            grad = grad_ref[number]
            g_t[n, :, span] = grad
            g_n[n, span, :] = grad.T
            delta[n, :, span] = jnp.sum(
                grad.astype(jnp.float32) * full_ref[number], 0, keepdims=True
            )
    dk[...] = jnp.zeros_like(dk)
    dv[...] = jnp.zeros_like(dv)
    dq_t[...] = jnp.zeros_like(dq_t)
    edge = prefix // block

    def one_query(n, carry):
        start = first + n * q_len
        last = jnp.maximum(start // block, edge)

        def step(kb, carry, masked):
            scores = jnp.dot(k_n[kb], q_t[n], preferred_element_type=jnp.float32)
            probs = jnp.exp2(scores - lse_ref[n])
            if masked:
                keep = allowed_mask(kb * block, start, scores.shape, prefix)
                probs = jnp.where(keep, probs, 0.0)
            d_probs = jnp.dot(v_n[kb], g_t[n], preferred_element_type=jnp.float32)
            d_scores = (probs * (d_probs - delta[n])).astype(jnp.bfloat16)
            dv[kb] += jnp.dot(
                probs.astype(jnp.bfloat16), g_n[n], preferred_element_type=jnp.float32
            )
            dk[kb] += jnp.dot(d_scores, q_n[n], preferred_element_type=jnp.float32)
            dq_t[n] += jnp.dot(k_t[kb], d_scores, preferred_element_type=jnp.float32)
            return carry

        lax.fori_loop(0, last, partial(step, masked=False), 0)
        step(last, 0, True)
        return 0

    lax.fori_loop(0, n_query, one_query, 0)
    per_block = block // tok_b
    for s, out in enumerate(outs):
        source = info[0] ^ s
        for c in range(total // rows // tok_b):
            number = (info[3] ^ c) * rows + source
            where = number // per_block
            offset = pl.multiple_of((number % per_block) * tok_b, tok_b)
            span = slice(c * tok_b, (c + 1) * tok_b)
            if not own_query:
                out[0, :, span] = (
                    dq_t[where, :, pl.ds(offset, tok_b)] * HDIM ** (-0.5)
                ).astype(jnp.bfloat16)
            out[key_slot, :, span] = (
                (dk[where, pl.ds(offset, tok_b), :] * LN2).astype(jnp.bfloat16).T
            )
            out[key_slot + 1, :, span] = (
                dv[where, pl.ds(offset, tok_b), :].astype(jnp.bfloat16).T
            )
    if own_query:
        dq_ref[...] = (dq_t[0] * HDIM ** (-0.5)).astype(jnp.bfloat16)


def attend_back(info, pieces, query, full, lse, grad, tok_b, block):
    total = len(pieces) * pieces[0].shape[-1]
    own = query is not None
    n_query, _, q_len = lse.shape
    vmem = pl.BlockSpec(memory_space=pltpu.VMEM)
    n_key = total // block
    out_shape = tuple(
        jax.ShapeDtypeStruct(pieces[0].shape[:2] + (total // 4,), jnp.bfloat16) for _ in range(4)
    )
    if own:
        out_shape += (jax.ShapeDtypeStruct(query.shape, jnp.bfloat16),)
    return pl.pallas_call(
        partial(backward_kernel, len(pieces), own, tok_b, block),
        out_shape=out_shape,
        in_specs=[pl.BlockSpec(memory_space=pltpu.SMEM)] + [vmem] * (len(pieces) + own + 3),
        out_specs=(vmem,) * len(out_shape),
        scratch_shapes=[
            pltpu.VMEM((n_query, HDIM, q_len), jnp.bfloat16),
            pltpu.VMEM((n_query, q_len, HDIM), jnp.bfloat16),
            pltpu.VMEM((n_key, HDIM, block), jnp.bfloat16),
            pltpu.VMEM((n_key, block, HDIM), jnp.bfloat16),
            pltpu.VMEM((n_key, block, HDIM), jnp.bfloat16),
            pltpu.VMEM((n_query, HDIM, q_len), jnp.bfloat16),
            pltpu.VMEM((n_query, q_len, HDIM), jnp.bfloat16),
            pltpu.VMEM((n_query, 1, q_len), jnp.float32),
            pltpu.VMEM((n_query, HDIM, q_len), jnp.float32),
            pltpu.VMEM((n_key, block, HDIM), jnp.float32),
            pltpu.VMEM((n_key, block, HDIM), jnp.float32),
        ],
        compiler_params=pltpu.CompilerParams(vmem_limit_bytes=VMEM_LIMIT),
        cost_estimate=pl.CostEstimate(
            flops=n_query * q_len * total * 2200, bytes_accessed=4 << 20, transcendentals=0
        ),
    )(info, *pieces, *([query] if own else []), full, lse, grad)


def dot(left, right, left_dim, right_dim):
    return lax.dot_general(
        left,
        right,
        (((left_dim,), (right_dim,)), ((), ())),
        preferred_element_type=jnp.float32,
    )


def dp_swap(value):
    return lax.ppermute(value, "dp", [(0, 1), (1, 0)])


def col_send(value, pairs):
    return lax.ppermute(value, "col", pairs)


NEAR = [(0, 1), (1, 0), (2, 3), (3, 2)]
MIDDLE = [(1, 2), (2, 1)]


OUTWARD = [(1, 0), (2, 3)]
INWARD = [(0, 1), (3, 2)]


def pair_sum(value):
    return value.astype(jnp.float32) + dp_swap(value).astype(jnp.float32)


def add_low(left, right):
    return (left.astype(jnp.float32) + right.astype(jnp.float32)).astype(jnp.bfloat16)


def line_reduce(parts, beside=lambda stage, arrived: ()):
    ends = col_send(parts[3], INWARD)
    ends = after(ends, *parts[:3], *beside(0, None))
    outer = col_send(after(parts[2], ends), INWARD)
    inner = col_send(add_low(parts[2], ends), MIDDLE)
    inner, outer = after([inner, outer], *beside(1, ends))
    mid = col_send(add_low(parts[3], outer), MIDDLE)
    near = col_send(add_low(parts[1], inner), NEAR)
    near, mid = after([near, mid], *beside(2, inner))
    return [parts[0], near, mid]


def col_exchange(parts):
    return [parts[0]] + [
        col_send(parts[s], [(i, i ^ s) for i in range(len(parts))]) for s in range(1, len(parts))
    ]


def sum_everywhere(values):
    for axis in ("row", "col"):
        for step in (1, 2):
            values = values + lax.ppermute(values, axis, [(i, i ^ step) for i in range(4)])
    return values + dp_swap(values)


def dp_scatter(values, dp, axis):
    half = values.shape[axis] // 2
    values = values.astype(jnp.bfloat16)
    own = lax.dynamic_slice_in_dim(values, dp * half, half, axis)
    other = lax.dynamic_slice_in_dim(values, (1 - dp) * half, half, axis)
    return add_low(own, dp_swap(other))


def dp_gather(half, dp, axis):
    other = dp_swap(half)
    return jnp.concatenate(
        [jnp.where(dp == 0, half, other), jnp.where(dp == 0, other, half)], axis
    )


ANY = pl.BlockSpec(memory_space=pl.ANY)
IN_VMEM = pl.BlockSpec(memory_space=pltpu.VMEM)
IN_SMEM = pl.BlockSpec(memory_space=pltpu.SMEM)


def after(values, *earlier):
    single = not isinstance(values, (list, tuple))
    arrays = [values] if single else list(values)

    def nothing(*refs):
        pass

    got = pl.pallas_call(
        nothing,
        out_shape=[jax.ShapeDtypeStruct(a.shape, a.dtype) for a in arrays],
        in_specs=[ANY] * (len(arrays) + len(earlier)),
        out_specs=[ANY] * len(arrays),
        input_output_aliases={i: i for i in range(len(arrays))},
        cost_estimate=pl.CostEstimate(flops=0, bytes_accessed=0, transcendentals=0),
    )(*arrays, *earlier)
    return got[0] if single else list(got)


def cost(flops, *arrays):
    moved = sum(a.size * a.dtype.itemsize for a in arrays)
    return pl.CostEstimate(flops=flops, bytes_accessed=moved, transcendentals=0)


def small_kernel(body, out_shape, *operands, scalars=1, flops=0):
    return pl.pallas_call(
        body,
        out_shape=out_shape,
        in_specs=[IN_SMEM] * scalars + [IN_VMEM] * (len(operands) - scalars),
        out_specs=jax.tree.map(lambda _: IN_VMEM, out_shape),
        compiler_params=pltpu.CompilerParams(vmem_limit_bytes=VMEM_LIMIT),
        cost_estimate=cost(flops, *operands[scalars:], *jax.tree.leaves(out_shape)),
    )(*operands)


def shape_of(shape, dtype):
    return jax.ShapeDtypeStruct(shape, dtype)


def assemble(me, pieces, keep):
    def body(info, *refs):
        out = refs[-1]
        for s in range(len(pieces)):
            at = pl.multiple_of((info[0] ^ s) * keep, 16)
            out[pl.ds(at, keep), :] = refs[s][0:keep, :]

    piece = pieces[0]
    return small_kernel(
        body, shape_of((len(pieces) * keep, piece.shape[1]), piece.dtype), me, *pieces
    )


def feature_sums(values):
    return jnp.sum(values, 0, keepdims=True)


def normalised(total, squares, width):
    mean = total / width
    return mean, lax.rsqrt(squares / width - mean * mean + 1e-05)


def token_tiles(me, values, narrow, count):
    feat, tokens = values.shape
    tok = tokens // count
    extra = 0 if narrow is None else 128

    def body(info, *refs):
        outs = refs[-count:]
        if narrow is not None:
            rest = refs[1][...].T[:feat, :]
            cuts = []
            for _ in range(3):
                cuts.append(rest.astype(jnp.bfloat16))
                rest = rest - cuts[-1].astype(jnp.float32)
        for s in range(count):
            at = pl.multiple_of((info[0] ^ s) * tok, tok)
            outs[s][:, 0:tok] = refs[0][:, pl.ds(at, tok)]
            if narrow is not None:
                for n, cut in enumerate(cuts):
                    outs[s][:, tok + n * cut.shape[1] : tok + (n + 1) * cut.shape[1]] = cut
                outs[s][:, tok + 3 * cuts[0].shape[1] :] = jnp.zeros(
                    (feat, extra - 3 * cuts[0].shape[1]), jnp.bfloat16
                )

    return small_kernel(
        body,
        (shape_of((feat, tok + extra), jnp.bfloat16),) * count,
        me,
        values,
        *(() if narrow is None else (narrow,)),
    )


def first_norm(me, pieces, tok, kinds):
    count = len(pieces)
    feat = pieces[0].shape[0]

    def body(info, *refs):
        x_refs = refs[:count]
        x_out, n_out, cols_out = refs[count:]
        total = sum(feature_sums(x[:, 0:tok].astype(jnp.float32)) for x in x_refs)
        squares = sum(feature_sums(jnp.square(x[:, 0:tok].astype(jnp.float32))) for x in x_refs)
        mean, inv_std = normalised(total, squares, count * feat)
        for s in range(count):
            at = pl.multiple_of((info[0] ^ s) * feat, 16)
            extra = x_refs[s][:, tok:].astype(jnp.float32)
            cols = (
                extra[:, 0:kinds]
                + extra[:, kinds : 2 * kinds]
                + extra[:, 2 * kinds : 3 * kinds]
            )
            cols_out[pl.ds(at, feat), :] = cols
            value = x_refs[s][:, 0:tok]
            x_out[pl.ds(at, feat), :] = value
            n_out[pl.ds(at, feat), :] = (
                (value.astype(jnp.float32) - mean) * inv_std * cols[:, 0:1] + cols[:, 1:2]
            ).astype(jnp.bfloat16)

    return small_kernel(
        body,
        (
            shape_of((count * feat, tok), jnp.bfloat16),
            shape_of((count * feat, tok), jnp.bfloat16),
            shape_of((count * feat, kinds), jnp.float32),
        ),
        me,
        *pieces,
    )


def project_out(info, heads, last, out_full, x_tok, cols):
    width, tok = x_tok.shape

    def body(info, heads_ref, last_ref, out_ref, x_ref, cols_ref, att_ref, res_ref, n_ref):
        inner = heads_ref.shape[0] * heads_ref.shape[1]
        att_ref[0:inner, :] = heads_ref[...].reshape(inner, tok)
        att_ref[inner:width, :] = last_ref[0]
        blocks, feat, hd = out_ref.shape
        per_row = width // hd
        for r in range(blocks // per_row):
            span = slice(r * feat, (r + 1) * feat)
            res_ref[span, :] = (
                sum(
                    jnp.dot(
                        out_ref[r * per_row + (c ^ info[3])],
                        att_ref[c * hd : (c + 1) * hd, :],
                        preferred_element_type=jnp.float32,
                    )
                    for c in range(per_row)
                )
                + x_ref[span, :].astype(jnp.float32)
                + cols_ref[span, 2:3]
            )
        value = res_ref[...]
        mean, inv_std = normalised(feature_sums(value), feature_sums(value * value), width)
        n_ref[...] = ((value - mean) * inv_std * cols_ref[:, 3:4] + cols_ref[:, 4:5]).astype(
            jnp.bfloat16
        )

    return small_kernel(
        body,
        (
            shape_of((width, tok), jnp.bfloat16),
            shape_of((width, tok), jnp.float32),
            shape_of((width, tok), jnp.bfloat16),
        ),
        info,
        heads,
        last,
        out_full,
        x_tok,
        cols,
    )


def norm_gradient(parts, values_ref, gain):
    d_normed = sum(p[...].astype(jnp.float32) for p in parts)
    values = values_ref[...].astype(jnp.float32)
    width = values.shape[0]
    mean, inv_std = normalised(feature_sums(values), feature_sums(values * values), width)
    centred = (values - mean) * inv_std
    scaled = d_normed * gain
    d_values = inv_std * (
        scaled - feature_sums(scaled) / width - centred * (feature_sums(scaled * centred) / width)
    )
    return (
        d_values,
        jnp.sum(d_normed * centred, 1, keepdims=True),
        jnp.sum(d_normed, 1, keepdims=True),
    )


def second_norm_back(info, parts, residual, cot, cols, out_full):
    width, tok = residual.shape

    def body(info, *refs):
        parts_refs = refs[:3]
        res_ref, cot_ref, cols_ref, out_ref, d_ref, low_ref, sums_ref, att_ref = refs[3:]
        d_values, gain_sum, shift_sum = norm_gradient(parts_refs, res_ref, cols_ref[:, 3:4])
        d_res = cot_ref[...].astype(jnp.float32) + d_values
        low = d_res.astype(jnp.bfloat16)
        d_ref[...] = d_res
        low_ref[...] = low
        sums_ref[:, 0:1] = gain_sum
        sums_ref[:, 1:2] = shift_sum
        sums_ref[:, 2:3] = jnp.sum(low.astype(jnp.float32), 1, keepdims=True)
        blocks, feat, hd = out_ref.shape
        per_row = width // hd
        for c in range(per_row):
            att_ref[c * hd : (c + 1) * hd, :] = sum(
                lax.dot_general(
                    out_ref[r * per_row + (c ^ info[3])],
                    low_ref[r * feat : (r + 1) * feat, :],
                    (((0,), (0,)), ((), ())),
                    preferred_element_type=jnp.float32,
                )
                for r in range(blocks // per_row)
            ).astype(jnp.bfloat16)

    return small_kernel(
        body,
        (
            shape_of((width, tok), jnp.float32),
            shape_of((width, tok), jnp.bfloat16),
            shape_of((width, 3), jnp.float32),
            shape_of((width, tok), jnp.bfloat16),
        ),
        info,
        *parts,
        residual,
        cot,
        cols,
        out_full,
    )


def first_norm_back(me, parts, x_tok, d_residual, cols, count):
    width, tok = x_tok.shape
    feat = width // count

    def body(info, *refs):
        parts_refs = refs[:3]
        x_ref, d_ref, cols_ref = refs[3:6]
        outs = refs[6 : 6 + count]
        sums_ref, whole = refs[6 + count :]
        d_values, gain_sum, shift_sum = norm_gradient(parts_refs, x_ref, cols_ref[:, 0:1])
        whole[...] = d_ref[...] + d_values
        for s in range(count):
            at = pl.multiple_of((info[0] ^ s) * feat, 16)
            outs[s][...] = whole[pl.ds(at, feat), :].astype(jnp.bfloat16)
        sums_ref[:, 0:1] = gain_sum
        sums_ref[:, 1:2] = shift_sum

    vmem_count = 6
    return pl.pallas_call(
        body,
        out_shape=tuple(shape_of((feat, tok), jnp.bfloat16) for _ in range(count))
        + (shape_of((width, 2), jnp.float32),),
        in_specs=[IN_SMEM] + [IN_VMEM] * vmem_count,
        out_specs=(IN_VMEM,) * (count + 1),
        scratch_shapes=[pltpu.VMEM((width, tok), jnp.float32)],
        compiler_params=pltpu.CompilerParams(vmem_limit_bytes=VMEM_LIMIT),
        cost_estimate=cost(0, *parts, x_tok, d_residual, d_residual),
    )(me, *parts, x_tok, d_residual, cols)


def side_by_side(me, pieces, dtype):
    feat, tok = pieces[0].shape

    def body(info, *refs):
        for s in range(len(pieces)):
            at = pl.multiple_of((info[0] ^ s) * tok, tok)
            refs[-1][:, pl.ds(at, tok)] = refs[s][...].astype(dtype)

    return small_kernel(body, shape_of((feat, len(pieces) * tok), dtype), me, *pieces)


def normal_tail(value):
    z = value * 0.7071067811865476
    t = 1.0 / (1.0 + 0.5 * z)
    poly = jnp.full_like(t, 0.17087277)
    for factor in (
        -0.82215223,
        1.48851587,
        -1.13520398,
        0.27886807,
        -0.18628806,
        0.09678418,
        0.37409196,
        1.00002368,
        -1.26551223,
    ):
        poly = poly * t + factor
    return t * jnp.exp(poly - z * z)


def feed_forward(normed, cot, up, down, bias):
    width, tok = normed.shape
    hidden_len = up.shape[1]

    def body(n_ref, cot_ref, up_ref, down_ref, bias_ref, active_ref, d_ref, sent_ref):
        hidden = (
            jnp.dot(n_ref[...].T, up_ref[...], preferred_element_type=jnp.float32) + bias_ref[...]
        )
        d_active = jnp.dot(cot_ref[...].T, down_ref[...], preferred_element_type=jnp.float32)
        tail = 0.5 * normal_tail(jnp.abs(hidden))
        below = jnp.where(hidden < 0, tail, 1.0 - tail)
        density = 0.3989422804014327 * jnp.exp(-0.5 * hidden * hidden)
        active_ref[...] = (hidden * below).astype(jnp.bfloat16)
        d_hidden = (d_active * (below + hidden * density)).astype(jnp.bfloat16)
        d_ref[...] = d_hidden
        sent_ref[...] = lax.dot_general(
            up_ref[...],
            d_hidden,
            (((1,), (1,)), ((), ())),
            preferred_element_type=jnp.float32,
        ).astype(jnp.bfloat16)

    return small_kernel(
        body,
        (
            shape_of((tok, hidden_len), jnp.bfloat16),
            shape_of((tok, hidden_len), jnp.bfloat16),
            shape_of((width, tok), jnp.bfloat16),
        ),
        normed,
        cot,
        up,
        down,
        bias,
        scalars=0,
        flops=10 * tok * width * hidden_len,
    )


def block_products(left, right, feat, hd):
    rows, cols = left.shape[0] // feat, right.shape[0] // hd

    def body(left_ref, right_ref, out_ref):
        for r in range(rows):
            whole = lax.dot_general(
                left_ref[r * feat : (r + 1) * feat, :],
                right_ref[...],
                (((1,), (1,)), ((), ())),
                preferred_element_type=jnp.float32,
            ).astype(jnp.bfloat16)
            for c in range(cols):
                out_ref[r * cols + c] = whole[:, c * hd : (c + 1) * hd]

    return small_kernel(
        body, shape_of((rows * cols, feat, hd), jnp.bfloat16), left, right, scalars=0
    )


def row_products(me, left, right, count):
    feat = left.shape[0] // count

    def body(info, left_ref, right_ref, *outs):
        for s in range(count):
            at = pl.multiple_of((info[0] ^ s) * feat, 16)
            outs[s][...] = lax.dot_general(
                left_ref[pl.ds(at, feat), :],
                right_ref[...],
                (((1,), (1,)), ((), ())),
                preferred_element_type=jnp.float32,
            ).astype(jnp.bfloat16)

    shape = shape_of((feat, right.shape[0]), jnp.bfloat16)
    return small_kernel(body, (shape,) * count, me, left, right)


def mixed_gradient(me, heads, d_query, last_parts):
    count = len(heads)
    kinds, hdim, tokens = heads[0].shape
    rows = kinds * count * hdim + kinds * hdim

    def body(info, *refs):
        query_ref = refs[count]
        last_refs = refs[count + 1 : count + 4]
        out = refs[count + 4]
        for s in range(count):
            for k in range(kinds):
                at = pl.multiple_of((k * count + (info[0] ^ s)) * hdim, hdim)
                out[pl.ds(at, hdim), :] = refs[s][k]
        base = kinds * count * hdim
        out[base : base + hdim, :] = jnp.zeros((hdim, tokens), jnp.bfloat16)
        out[base : base + hdim, 0 : query_ref.shape[1]] = query_ref[...]
        for k in range(2):
            out[base + (k + 1) * hdim : base + (k + 2) * hdim, :] = sum(
                ref[k].astype(jnp.float32) for ref in last_refs
            ).astype(jnp.bfloat16)

    return small_kernel(
        body, shape_of((rows, tokens), jnp.bfloat16), me, *heads, d_query, *last_parts
    )


def with_bias_rows(weight, bias):
    return jnp.concatenate(
        [weight, bias[None], jnp.zeros((PAD - 1, weight.shape[1]), weight.dtype)], 0
    )


def strip_tables(cols, wide):
    native = 3 * D // cols
    slots = wide + HDIM
    from_native = np.full((cols, cols, slots), -1, np.int32)
    to_strip = np.full((cols, cols, slots), -1, np.int32)
    for c in range(cols):
        for s in range(cols):
            for block, group, table in ((c, c ^ s, 0), (c ^ s, c, 1)):
                count = 0
                for i in range(3):
                    for place in range(wide + HDIM):
                        last = place >= wide
                        column = i * D + (D - HDIM + place - wide if last else group * wide + place)
                        if column // native != block:
                            continue
                        slot = wide + place - wide if last else count
                        count += not last
                        if table == 0:
                            from_native[c, s, slot] = column - block * native
                        else:
                            to_strip[c, s, slot] = (
                                3 * wide + i * HDIM + place - wide if last else i * wide + place
                            )
    return from_native.reshape(cols, -1), to_strip.reshape(cols, -1)


def one_hot(table, col, size):
    slots = pick(jnp.asarray(table), col)
    return (lax.broadcasted_iota(jnp.int32, (size, table.shape[1]), 0) == slots[None]).astype(
        jnp.bfloat16
    )


def head_shards(
    block_input,
    cotangent,
    prefix_len,
    first_gain,
    first_shift,
    qkv_weight,
    qkv_bias,
    out_weight,
    out_bias,
    second_gain,
    second_shift,
    up_weight,
    up_bias,
    down_weight,
    down_bias,
):
    rows = lax.axis_size("row")
    cols = lax.axis_size("col")
    row = lax.axis_index("row")
    col = lax.axis_index("col")
    dp = lax.axis_index("dp")
    tok_a = block_input.shape[1]
    tok_b = tok_a // rows
    feat = block_input.shape[2]
    block = 2 * tok_b
    wide = rows * HDIM
    slots = wide + HDIM
    hidden_len = up_weight.shape[1]
    from_native, to_strip = strip_tables(cols, wide)

    me = row[None]
    narrow = jnp.concatenate(
        [
            jnp.stack(
                [first_gain, first_shift, out_bias, second_gain, second_shift, down_bias]
                + [jnp.zeros_like(first_gain)] * 2
            ),
            jnp.zeros((8, 384 - feat), jnp.float32),
        ],
        1,
    )

    x_got = row_exchange(list(token_tiles(me, block_input[0].T, narrow, rows)))
    spread = one_hot(from_native, col, qkv_weight.shape[1])
    sent = dot(with_bias_rows(qkv_weight, qkv_bias), spread, 1, 0).astype(jnp.bfloat16)
    out_rows = jnp.concatenate([out_weight.T, jnp.zeros((PAD, out_weight.shape[0]), jnp.bfloat16)])
    got = col_exchange(
        [
            jnp.concatenate([sent[:, s * slots : (s + 1) * slots], out_rows], 1)
            for s in range(cols)
        ]
    )
    x_got[1], *got[1:] = after([x_got[1], *got[1:]])
    out_got = [g[:feat, slots:] for g in got]
    got = [g[:, :slots] for g in got]
    x_tok, normed_one, cols_all = first_norm(me, x_got, tok_b, narrow.shape[0])

    near = col_send(normed_one, NEAR)
    mid = col_send(normed_one, MIDDLE)
    cot_got = row_exchange(
        list(token_tiles(me, after(cotangent[0].T, normed_one), None, rows))
    )
    near, mid, *cot_got[1:] = after([near, mid, *cot_got[1:]])
    inner = col_send(near, MIDDLE)
    outer = col_send(mid, OUTWARD)
    placed = one_hot(to_strip, col, 3 * slots)
    strip = dot(jnp.concatenate(got, 1), placed, 1, 1).astype(jnp.bfloat16)
    strip_bias = strip[feat].astype(jnp.float32)
    strip_near = swap(strip, 1)
    strip_far = swap(strip, 2)
    cot_tok = assemble(me, cot_got, feat)
    inner, outer, strip_near, strip_far = after([inner, outer, strip_near, strip_far], cot_tok)
    ends = col_send(inner, OUTWARD)
    qkv_strip = assemble(me, [strip, strip_near, strip_far, swap(strip_far, 1)], feat)

    up_down = lax.all_gather(jnp.stack([up_weight, down_weight.T]), "row")
    up_slice = up_down[:, 0].reshape(rows * feat, hidden_len)
    down_slice = up_down[:, 1].reshape(rows * feat, hidden_len)

    out_full = lax.all_gather(jnp.stack(out_got), "row").reshape((-1,) + out_weight.shape)

    query_scale = LOG2E * HDIM ** (-0.5)
    scale = jnp.concatenate(
        [
            jnp.full((wide,), query_scale, jnp.float32),
            jnp.ones((2 * wide,), jnp.float32),
            jnp.full((HDIM,), query_scale, jnp.float32),
            jnp.ones((2 * HDIM,), jnp.float32),
        ]
    )
    def project(normed):
        mixed = (
            (dot(qkv_strip, normed, 0, 0) + strip_bias[:, None]) * scale[:, None]
        ).astype(jnp.bfloat16)
        by_head = mixed[: 3 * wide].reshape(3, rows, HDIM, -1)
        return mixed, [pick(by_head, row ^ s, 1) for s in range(rows)]

    first_set = jnp.concatenate([normed_one, near], 1)
    mixed_first, tiles_first = project(first_set)
    got_first = row_exchange(tiles_first)
    ends = after(ends, *tiles_first)
    middle = (col == 1) | (col == 2)
    second_set = jnp.concatenate(
        [jnp.where(middle, inner, outer), jnp.where(middle, mid, ends)], 1
    )
    mixed_second, tiles_second = project(second_set)
    got_second = row_exchange(tiles_second)
    pieces = [p for pair in zip(got_first, got_second) for p in pair]
    last_query = mixed_first[3 * wide : 3 * wide + HDIM, :tok_b]
    last_pieces = row_gather(
        jnp.concatenate(
            [m[3 * wide + HDIM :].reshape(2, HDIM, -1) for m in (mixed_first, mixed_second)], 2
        )
    )
    normed_set = jnp.concatenate([first_set, second_set], 1)
    cot_tok = after(cot_tok, second_set)
    cot_cols = lax.all_gather(cot_tok, "col")
    cot_parts = [cot_tok] + [pick(cot_cols, col ^ s) for s in range(1, cols)]

    zero = jnp.int32(0)
    info = jnp.stack([row, prefix_len[0], zero, col])
    last_info = jnp.stack([row, prefix_len[0], col * tok_a + row * tok_b, col])
    heads_out, heads_full, heads_lse = attend(
        info, pieces, None, tok_b, block, (up_slice, down_slice, last_pieces[1])
    )
    last_out, last_full, last_lse = attend(last_info, last_pieces, last_query, tok_b, block)
    heads_got = lax.all_to_all(heads_out, ("col", "row"), 0, 0, tiled=True)
    attended, residual, normed_two = project_out(
        info, heads_got, last_out, out_full, x_tok, cols_all
    )
    hidden_bias = up_bias.astype(jnp.float32)[None]

    def through_hidden(normed, s):
        return feed_forward(normed, cot_parts[s], up_slice, down_slice, hidden_bias)

    near = col_send(normed_two, NEAR)
    mid = col_send(normed_two, MIDDLE)
    through = [through_hidden(normed_two, 0)]
    near, mid = after([near, mid], through[0][2])
    inner = col_send(near, MIDDLE)
    outer = col_send(mid, OUTWARD)
    through.append(through_hidden(near, 1))
    inner, outer = after([inner, outer], through[1][2])
    ends = col_send(inner, OUTWARD)
    second = jnp.where(middle, inner, outer)
    through.append(through_hidden(second, 2))
    ends = after(ends, through[2][2])
    third = jnp.where(middle, mid, ends)
    through.append(through_hidden(third, 3))
    d_norm_sent = [t[2] for t in through]
    normed_two = jnp.concatenate([normed_two, near, second, third], 1)
    cot_all = jnp.concatenate(cot_parts, 1)
    work = {}

    def weight_products(stage, arrived):
        if stage == 0:
            return ()
        source, left = ((1, normed_two), (0, cot_all))[stage - 1]
        right = jnp.concatenate(after([t[source] for t in through], arrived), 0)
        work[stage] = right, dot(left, right, 1, 0).astype(jnp.bfloat16)
        return (work[stage][1],)

    d_norm_two = line_reduce(d_norm_sent, weight_products)
    (low_hidden, up_part), (low_active, down_part) = work[1], work[2]
    d_residual, branch, second_sums, d_attended = second_norm_back(
        info, d_norm_two, residual, cot_tok, cols_all, out_full
    )
    d_heads = lax.all_to_all(
        d_attended[: D - HDIM].reshape(rows * cols, HDIM, tok_b), ("col", "row"), 0, 0, tiled=True
    )
    *last_grads, d_last_query = attend_back(
        last_info,
        last_pieces,
        last_query,
        last_full,
        last_lse,
        d_attended[D - HDIM :][None],
        tok_b,
        block,
    )
    head_grads = attend_back(info, pieces, None, heads_full, heads_lse, d_heads, tok_b, block)
    d_last_parts = row_reduce_parts(last_grads)

    up_down_part = jnp.stack(
        [p.reshape(rows, feat, hidden_len) for p in (up_part, down_part)], 1
    )
    up_down_half = lax.psum_scatter(up_down_part, "row", scatter_dimension=0)
    active_parts = after(low_active, d_attended).reshape(cols, tok_b, hidden_len)
    partial_out = jnp.stack(
        [
            dot(down_slice, pick(active_parts, col ^ i), 1, 1).astype(jnp.bfloat16)
            for i in range(cols)
        ]
    )
    sent_out = lax.psum_scatter(partial_out, "col", scatter_dimension=0)
    out_half = lax.psum_scatter(
        block_products(branch, attended, feat, D).reshape(rows, feat, D),
        "row",
        scatter_dimension=0,
    )

    up_down_grad = pair_sum(up_down_half)
    head_got = row_exchange(list(head_grads))
    head_got[1] = after(head_got[1], up_down_grad)
    d_mixed = mixed_gradient(me, head_got, d_last_query, d_last_parts)
    d_normed_sent = [
        dot(qkv_strip, d_mixed[:, s * tok_b : (s + 1) * tok_b], 1, 0).astype(jnp.bfloat16)
        for s in range(cols)
    ]
    kept = {}

    def beside(stage, arrived):
        if stage == 0:
            parts = row_products(me, normed_set, after(d_mixed, *d_normed_sent), rows)
            beyond, kept["near"] = swap(parts[3], 1), swap(parts[1], 1)
            pair = add_low(parts[2], beyond)
            kept["own"], kept["far"] = parts[0], swap(pair, 2)
            return (pair,)
        kept[stage] = arrived
        return ()

    d_norm_one = line_reduce(d_normed_sent, beside)
    arrived = [kept[1], kept[2], d_norm_one[1]]
    near, far = after([kept["near"], kept["far"]], arrived[1])
    total = sum(p.astype(jnp.float32) for p in (kept["own"], near, far)).astype(jnp.bfloat16)
    both = jnp.concatenate([total, out_half], 1)
    half = feat // 2
    other = dp_swap(lax.dynamic_slice_in_dim(both, (1 - dp) * half, half, 0))
    total = add_low(lax.dynamic_slice_in_dim(both, dp * half, half, 0), other)
    sent = dot(total[:, : 3 * slots], placed, 1, 0).astype(jnp.bfloat16)
    hd = D // cols
    got = col_exchange(
        [
            jnp.concatenate(
                [
                    sent[:, s * slots : (s + 1) * slots],
                    lax.dynamic_slice_in_dim(total, 3 * slots + (col ^ s) * hd, hd, 1),
                ],
                1,
            )
            for s in range(cols)
        ]
    )
    qkv = dot(jnp.concatenate([g[:, :slots] for g in got], 1), spread, 1, 1)
    out = sum(g[:, slots:].astype(jnp.float32) for g in got)
    last_grad = dp_gather(jnp.concatenate([qkv, out], 1).astype(jnp.bfloat16), dp, 0)
    qkv_grad, out_grad = jnp.split(last_grad.astype(jnp.float32), [qkv_weight.shape[1]], 1)

    out_value = (
        after(sent_out, arrived[0]).astype(jnp.float32) + residual + cols_all[:, 5:6]
    ).astype(jnp.bfloat16)
    block_got = row_exchange(
        [lax.dynamic_slice_in_dim(out_value, (row ^ s) * feat, feat, 0) for s in range(rows)]
    )
    block_output = side_by_side(me, after(block_got, arrived[1]), jnp.bfloat16)
    *input_parts, first_sums = first_norm_back(
        me, d_norm_one, x_tok, d_residual, cols_all, rows
    )
    input_grad = side_by_side(me, row_exchange(input_parts), jnp.float32)

    at_row = (jnp.arange(rows) == row)[:, None]

    def own_row(values):
        return jnp.where(at_row, values[None], 0.0).reshape(-1)

    def own_col(values):
        return jnp.where((jnp.arange(cols) == col)[:, None], values[None], 0.0).reshape(-1)

    bias_strip = jnp.sum(d_mixed.astype(jnp.float32), 1)
    at_col = (jnp.arange(cols) == col)[None, :, None]
    bias_heads = jnp.where(at_col, bias_strip[: 3 * wide].reshape(3, 1, wide), 0.0)
    bias_all = jnp.concatenate(
        [bias_heads.reshape(3, -1), bias_strip[3 * wide :].reshape(3, HDIM)], 1
    ).reshape(-1)
    early = [
        own_row(jnp.sum(cotangent[0].astype(jnp.float32), 0)),
        second_sums[:, 2],
        second_sums[:, 0],
        second_sums[:, 1],
        own_col(jnp.sum(low_hidden.astype(jnp.float32), 0)),
        bias_all,
        first_sums[:, 0],
        first_sums[:, 1],
    ]
    total = sum_everywhere(jnp.concatenate(early).reshape(8, -1)).reshape(-1)

    def own_part(start, size, index):
        return lax.dynamic_slice_in_dim(total, start + index * size, size, 0)

    width = rows * feat
    up_at = 4 * width
    qkv_at = up_at + cols * hidden_len
    first_at = qkv_at + 3 * width
    return (
        block_output.T[None],
        input_grad.T[None],
        own_part(first_at, feat, row),
        own_part(first_at + width, feat, row),
        qkv_grad,
        own_part(qkv_at, 3 * width // cols, col),
        out_grad.T,
        own_part(width, feat, row),
        own_part(2 * width, feat, row),
        own_part(3 * width, feat, row),
        up_down_grad[0],
        own_part(up_at, hidden_len, col),
        up_down_grad[1].T,
        own_part(0, feat, row),
    )


def solution(mesh):
    in_specs = (
        P("dp", "col", "row"),
        P("dp", "col", "row"),
        P("dp"),
        P("row"),
        P("row"),
        P("row", "col"),
        P("col"),
        P("col", "row"),
        P("row"),
        P("row"),
        P("row"),
        P("row", "col"),
        P("col"),
        P("col", "row"),
        P("row"),
    )
    out_specs = (
        P("dp", "col", "row"),
        P("dp", "col", "row"),
        P("row"),
        P("row"),
        P("row", "col"),
        P("col"),
        P("col", "row"),
        P("row"),
        P("row"),
        P("row"),
        P("row", "col"),
        P("col"),
        P("col", "row"),
        P("row"),
    )
    one_head_each = mesh.shape["row"] == 4 and mesh.shape["col"] == 4 and mesh.shape["dp"] == 2
    body = head_shards if one_head_each else shards
    return jax.shard_map(body, mesh=mesh, in_specs=in_specs, out_specs=out_specs, check_vma=False)
```

```python
from functools import partial

import jax
import jax.numpy as jnp
import numpy as np
from jax import lax
from jax.experimental import pallas as pl
from jax.experimental.pallas import tpu as pltpu
from jax.sharding import PartitionSpec as P

HEADS = 17
HDIM = 64
D = 1088


def positions(first_row, piece_len, tok_b, tok_a, col_total):
    flat_rows = first_row + jnp.arange(piece_len, dtype=jnp.int32)
    shard_no = flat_rows // tok_b
    return shard_no % col_total * tok_a + shard_no // col_total * tok_b + flat_rows % tok_b


def over_blocks(folded, pieces, step_fn):
    piece_len = pieces[0].shape[0]
    block_len = 512

    def one_block(block_no, running):
        offset = block_no * block_len
        sliced = tuple(
            (lax.dynamic_slice_in_dim(member, offset, block_len, 0) for member in pieces)
        )
        return step_fn(running, sliced, offset)

    return lax.fori_loop(0, piece_len // block_len, one_block, folded)


def head_scores(left, right, scale_factor):
    return (
        jnp.einsum("qhd,khd->hqk", left, right, preferred_element_type=jnp.float32) * scale_factor
    )


def normalize(values, norm_gain, norm_shift):
    width_all = values.shape[1] * lax.axis_size("row")
    row_sums = lax.psum((jnp.sum(values, 1), jnp.sum(values * values, 1)), "row")
    row_mean = row_sums[0] / width_all
    variance = row_sums[1] / width_all - row_mean * row_mean
    inv_std = lax.rsqrt(variance + 1e-05)
    centred = (values - row_mean[:, None]) * inv_std[:, None]
    return (centred * norm_gain + norm_shift, centred, inv_std)


def norm_back(d_normed, centred, inv_std, norm_gain):
    width_all = d_normed.shape[1] * lax.axis_size("row")
    scaled = d_normed * norm_gain
    row_sums = lax.psum((jnp.sum(scaled, 1), jnp.sum(scaled * centred, 1)), "row")
    d_values = inv_std[:, None] * (
        scaled - row_sums[0][:, None] / width_all - centred * row_sums[1][:, None] / width_all
    )
    return (d_values, jnp.sum(d_normed * centred, 0), jnp.sum(d_normed, 0))


def row_partials(term_fn, tok_b):
    return lax.psum_scatter(
        term_fn(jnp.int32(0), tok_b * lax.axis_size("row")).astype(jnp.bfloat16),
        "row",
        scatter_dimension=0,
        tiled=True,
    ).astype(jnp.float32)


def rows_gather(values):
    return lax.all_gather(values, "row", axis=0, tiled=True)


def row_product(normed_low, weight, tok_b):

    def term_fn(first_row, row_count):
        return jnp.dot(normed_low, weight, preferred_element_type=jnp.float32)

    return row_partials(term_fn, tok_b)


def back_product(grad_low, weight, tok_b):

    def term_fn(first_row, row_count):
        return lax.dot_general(
            grad_low, weight, (((1,), (1,)), ((), ())), preferred_element_type=jnp.float32
        )

    return row_partials(term_fn, tok_b)


def fold_back(grad_rows, normed_low, weight_full):
    piece = lax.all_gather(grad_rows, "row", axis=0, tiled=True)
    contrib = lax.dot_general(
        piece, weight_full, (((1,), (1,)), ((), ())), preferred_element_type=jnp.float32
    )
    d_weight = lax.dot_general(
        normed_low, piece, (((0,), (0,)), ((), ())), preferred_element_type=jnp.float32
    )
    return (contrib, d_weight, jnp.sum(piece.astype(jnp.float32), 0))


def scatter_columns(gradients):
    return (
        lax.psum_scatter(
            gradients[0].astype(jnp.bfloat16), "col", scatter_dimension=1, tiled=True
        ).astype(jnp.float32),
        lax.psum_scatter(
            gradients[1].astype(jnp.bfloat16), "col", scatter_dimension=0, tiled=True
        ).astype(jnp.float32),
        lax.psum_scatter(
            gradients[2].astype(jnp.bfloat16), "col", scatter_dimension=0, tiled=True
        ).astype(jnp.float32),
        lax.psum_scatter(
            gradients[3].astype(jnp.bfloat16), "col", scatter_dimension=1, tiled=True
        ).astype(jnp.float32),
        lax.psum_scatter(
            gradients[4].astype(jnp.bfloat16), "col", scatter_dimension=0, tiled=True
        ).astype(jnp.float32),
        lax.psum_scatter(
            gradients[5].astype(jnp.bfloat16), "col", scatter_dimension=0, tiled=True
        ).astype(jnp.float32),
    )


def sum_over_data(gradients):
    return (
        lax.psum(gradients[0].astype(jnp.bfloat16), "dp").astype(jnp.float32),
        lax.psum(gradients[1].astype(jnp.bfloat16), "dp").astype(jnp.float32),
        lax.psum(gradients[2].astype(jnp.bfloat16), "dp").astype(jnp.float32),
        lax.psum(gradients[3].astype(jnp.bfloat16), "dp").astype(jnp.float32),
        lax.psum(gradients[4].astype(jnp.bfloat16), "dp").astype(jnp.float32),
        lax.psum(gradients[5].astype(jnp.bfloat16), "dp").astype(jnp.float32),
    )


def shards(
    block_input,
    cotangent,
    prefix_len,
    first_gain,
    first_shift,
    qkv_weight,
    qkv_bias,
    out_weight,
    out_bias,
    second_gain,
    second_shift,
    up_weight,
    up_bias,
    down_weight,
    down_bias,
):
    row_total = lax.axis_size("row")
    col_total = lax.axis_size("col")
    tok_a = block_input.shape[1]
    tok_b = tok_a // row_total
    scale_factor = HDIM ** (-0.5)
    gathered = (
        lax.all_gather(qkv_weight, "col", axis=1, tiled=True),
        lax.all_gather(qkv_bias, "col", axis=0, tiled=True),
        lax.all_gather(out_weight, "col", axis=0, tiled=True),
        lax.all_gather(up_weight, "col", axis=1, tiled=True),
        lax.all_gather(up_bias, "col", axis=0, tiled=True),
        lax.all_gather(down_weight, "col", axis=0, tiled=True),
    )
    qkv_full, qkv_bias_full, out_full, up_full, up_bias_full, down_full = gathered
    residual = block_input[0].astype(jnp.float32)
    prefix_end = prefix_len[0]
    own_pos = (
        lax.axis_index("col") * tok_a
        + lax.axis_index("row") * tok_b
        + jnp.arange(tok_b, dtype=jnp.int32)
    )

    def visible(key_pos, query_pos):
        return (key_pos[None, :] < prefix_end) | (key_pos[None, :] <= query_pos[:, None])

    def piece_pos(first_row, piece_len):
        return positions(first_row, piece_len, tok_b, tok_a, col_total)

    normed_one, centred_one, inv_one = normalize(residual, first_gain, first_shift)
    normed_one_low = normed_one.astype(jnp.bfloat16)
    mixed_qkv = (
        row_product(normed_one_low, qkv_full, tok_b) + qkv_bias_full.astype(jnp.float32)
    ).astype(jnp.bfloat16)
    query_rows = mixed_qkv[:, :D]
    key_rows = mixed_qkv[:, D : 2 * D]
    value_rows = mixed_qkv[:, 2 * D :]
    own_query = query_rows.reshape(tok_b, HEADS, HDIM)
    own_key = key_rows.reshape(tok_b, HEADS, HDIM)
    own_value = value_rows.reshape(tok_b, HEADS, HDIM)

    def max_step(running, sliced, first_row):
        key_block = sliced[0]
        allowed = visible(piece_pos(first_row, key_block.shape[0]), own_pos)
        scores = jnp.where(
            allowed[None],
            head_scores(own_query, key_block.reshape(-1, HEADS, HDIM), scale_factor),
            -1e30,
        )
        new_max = jnp.maximum(running[0], jnp.max(scores, 2))
        new_total = running[1] * jnp.exp(running[0] - new_max) + jnp.sum(
            jnp.where(allowed[None], jnp.exp(scores - new_max[:, :, None]), 0.0), 2
        )
        return (new_max, new_total)

    start_max = (
        jnp.full((HEADS, tok_b), -1e30, jnp.float32),
        jnp.zeros((HEADS, tok_b), jnp.float32),
    )
    run_max, run_total = over_blocks(
        start_max, (lax.all_gather(key_rows, ("row", "col"), axis=0, tiled=True),), max_step
    )
    log_total = run_max + jnp.log(run_total)

    def value_step(running, sliced, first_row):
        key_block, value_block = sliced
        allowed = visible(piece_pos(first_row, key_block.shape[0]), own_pos)
        scores = head_scores(own_query, key_block.reshape(-1, HEADS, HDIM), scale_factor)
        attn_probs = jnp.where(allowed[None], jnp.exp(scores - log_total[:, :, None]), 0.0).astype(
            jnp.bfloat16
        )
        return running + jnp.einsum(
            "hqk,khd->qhd",
            attn_probs,
            value_block.reshape(-1, HEADS, HDIM),
            preferred_element_type=jnp.float32,
        )

    attn_acc = over_blocks(
        jnp.zeros((tok_b, HEADS, HDIM), jnp.float32),
        (
            lax.all_gather(key_rows, ("row", "col"), axis=0, tiled=True),
            lax.all_gather(value_rows, ("row", "col"), axis=0, tiled=True),
        ),
        value_step,
    )
    attn_float = attn_acc.reshape(tok_b, D)
    attn_all = rows_gather(attn_float.astype(jnp.bfloat16))
    residual_two = (
        residual + jnp.dot(attn_all, out_full, preferred_element_type=jnp.float32) + out_bias
    )
    normed_two, centred_two, inv_two = normalize(residual_two, second_gain, second_shift)
    normed_two_low = normed_two.astype(jnp.bfloat16)
    hidden = row_product(normed_two_low, up_full, tok_b) + up_bias_full.astype(jnp.float32)
    active_all = rows_gather(jax.nn.gelu(hidden, approximate=False).astype(jnp.bfloat16))
    block_output = (
        residual_two
        + jnp.dot(active_all, down_full, preferred_element_type=jnp.float32)
        + down_bias
    ).astype(jnp.bfloat16)
    cot_low = cotangent[0]
    cot_float = cot_low.astype(jnp.float32)
    down_grad = lax.dot_general(
        active_all, cot_low, (((0,), (0,)), ((), ())), preferred_element_type=jnp.float32
    )
    down_bias_grad = jnp.sum(cot_float, 0)
    d_active = back_product(cot_low, down_full, tok_b)
    gelu_back = jax.vjp(partial(jax.nn.gelu, approximate=False), hidden)[1]
    d_hidden_low = gelu_back(d_active)[0].astype(jnp.bfloat16)
    d_norm_two, up_grad, up_bias_grad = fold_back(d_hidden_low, normed_two_low, up_full)
    d_part_two, second_gain_grad, second_shift_grad = norm_back(
        d_norm_two, centred_two, inv_two, second_gain
    )
    d_residual = cot_float + d_part_two
    branch_low = d_residual.astype(jnp.bfloat16)
    out_grad = lax.dot_general(
        attn_all, branch_low, (((0,), (0,)), ((), ())), preferred_element_type=jnp.float32
    )
    out_bias_grad = jnp.sum(branch_low.astype(jnp.float32), 0)
    d_attn_low = back_product(branch_low, out_full, tok_b).astype(jnp.bfloat16)
    delta_rows = jnp.sum(
        (d_attn_low.astype(jnp.float32) * attn_float).reshape(tok_b, HEADS, HDIM), 2
    )
    lse_rows = log_total.T
    all_lse, all_delta = (
        lax.all_gather(lse_rows, ("row", "col"), axis=0, tiled=True),
        lax.all_gather(delta_rows, ("row", "col"), axis=0, tiled=True),
    )
    own_grad = d_attn_low.reshape(tok_b, HEADS, HDIM)

    def back_step(running, sliced, first_row):
        query_p, key_p, value_p, grad_p = sliced
        piece_len = query_p.shape[0]
        pos_piece = piece_pos(first_row, piece_len)
        lse_piece = lax.dynamic_slice_in_dim(all_lse, first_row, piece_len, 0)
        delta_piece = lax.dynamic_slice_in_dim(all_delta, first_row, piece_len, 0)
        query_p3 = query_p.reshape(piece_len, HEADS, HDIM)
        key_p3 = key_p.reshape(piece_len, HEADS, HDIM)
        value_p3 = value_p.reshape(piece_len, HEADS, HDIM)
        grad_p3 = grad_p.reshape(piece_len, HEADS, HDIM)
        allowed_own = visible(pos_piece, own_pos)
        allowed_far = visible(own_pos, pos_piece)
        scores = head_scores(own_query, key_p3, scale_factor)
        attn_probs = jnp.where(allowed_own[None], jnp.exp(scores - log_total[:, :, None]), 0.0)
        d_probs = jnp.einsum("qhd,khd->hqk", own_grad, value_p3, preferred_element_type=jnp.float32)
        d_scores = (attn_probs * (d_probs - delta_rows.T[:, :, None])).astype(jnp.bfloat16)
        new_query = (
            running[0]
            + jnp.einsum("hqk,khd->qhd", d_scores, key_p3, preferred_element_type=jnp.float32)
            * scale_factor
        )
        scores = head_scores(query_p3, own_key, scale_factor)
        attn_probs = jnp.where(allowed_far[None], jnp.exp(scores - lse_piece.T[:, :, None]), 0.0)
        d_value = running[2] + jnp.einsum(
            "hqk,qhd->khd",
            attn_probs.astype(jnp.bfloat16),
            grad_p3,
            preferred_element_type=jnp.float32,
        )
        d_probs = jnp.einsum("qhd,khd->hqk", grad_p3, own_value, preferred_element_type=jnp.float32)
        d_scores = (attn_probs * (d_probs - delta_piece.T[:, :, None])).astype(jnp.bfloat16)
        d_key = (
            running[1]
            + jnp.einsum("hqk,qhd->khd", d_scores, query_p3, preferred_element_type=jnp.float32)
            * scale_factor
        )
        return (new_query, d_key, d_value)

    zero_heads = jnp.zeros((tok_b, HEADS, HDIM), jnp.float32)
    d_query, d_key, d_value = over_blocks(
        (zero_heads, zero_heads, zero_heads),
        (
            lax.all_gather(query_rows, ("row", "col"), axis=0, tiled=True),
            lax.all_gather(key_rows, ("row", "col"), axis=0, tiled=True),
            lax.all_gather(value_rows, ("row", "col"), axis=0, tiled=True),
            lax.all_gather(d_attn_low, ("row", "col"), axis=0, tiled=True),
        ),
        back_step,
    )
    d_mixed_low = jnp.concatenate(
        [d_query.reshape(tok_b, D), d_key.reshape(tok_b, D), d_value.reshape(tok_b, D)], 1
    ).astype(jnp.bfloat16)
    d_norm_one, qkv_grad, qkv_bias_grad = fold_back(d_mixed_low, normed_one_low, qkv_full)
    d_part_one, first_gain_grad, first_shift_grad = norm_back(
        d_norm_one, centred_one, inv_one, first_gain
    )
    input_grad = d_residual + d_part_one
    col_ready = (qkv_grad, qkv_bias_grad, out_grad, up_grad, up_bias_grad, down_grad)
    reduced = scatter_columns(sum_over_data(col_ready))
    small = lax.psum(
        (
            first_gain_grad,
            first_shift_grad,
            out_bias_grad,
            second_gain_grad,
            second_shift_grad,
            down_bias_grad,
        ),
        ("dp", "col"),
    )
    return (
        block_output[None],
        input_grad[None],
        small[0],
        small[1],
        reduced[0],
        reduced[1],
        reduced[2],
        small[2],
        small[3],
        small[4],
        reduced[3],
        reduced[4],
        reduced[5],
        small[5],
    )


LOG2E = 1.4426950408889634
LN2 = 0.6931471805599453
PAD = 16
MEBI = 1024 * 1024
VMEM_LIMIT = 56 * MEBI


def swap(value, step):
    size = lax.axis_size("row")
    return lax.ppermute(value, "row", [(i, i ^ step) for i in range(size)])


def pick(stacked, index, axis=0):
    return lax.dynamic_index_in_dim(stacked, index, axis, keepdims=False)


def row_gather(own):
    far = swap(own, 2)
    return [own, swap(own, 1), far, swap(far, 1)]


def row_exchange(parts):
    return [parts[0], swap(parts[1], 1), swap(parts[2], 2), swap(parts[3], 3)]


def row_reduce_parts(parts):
    low = [p.astype(jnp.bfloat16) for p in parts]
    beyond = swap(low[3], 1)
    near = swap(low[1], 1)
    far = swap(add_low(parts[2], beyond), 2)
    return [parts[0], near, far]


def row_reduce(parts):
    return sum(p.astype(jnp.float32) for p in row_reduce_parts(parts))


def in_order(parts, me):
    stacked = jnp.stack(parts)
    return [pick(stacked, me ^ i) for i in range(len(parts))]


def layer_norm(values, gain, shift):
    mean = jnp.mean(values, 1, keepdims=True)
    variance = jnp.mean(values * values, 1, keepdims=True) - mean * mean
    inv_std = lax.rsqrt(variance + 1e-05)
    centred = (values - mean) * inv_std
    return (centred * gain + shift, centred, inv_std)


def layer_norm_back(d_normed, centred, inv_std, gain):
    scaled = d_normed * gain
    return inv_std * (
        scaled
        - jnp.mean(scaled, 1, keepdims=True)
        - centred * jnp.mean(scaled * centred, 1, keepdims=True)
    )


def load_pieces(info, pieces, slot, transposed, plain, tok_b, block):
    rows = 4
    groups = len(pieces) // rows
    cols = pieces[0].shape[-1] // tok_b
    per_block = block // tok_b
    for p, piece in enumerate(pieces):
        source = info[0] ^ (p // groups)
        for c in range(cols):
            part = piece[slot, :, c * tok_b : (c + 1) * tok_b]
            number = (info[3] ^ (p % groups * cols + c)) * rows + source
            where = number // per_block
            offset = pl.multiple_of((number % per_block) * tok_b, tok_b)
            if transposed is not None:
                transposed[where, :, pl.ds(offset, tok_b)] = part
            if plain is not None:
                plain[where, pl.ds(offset, tok_b), :] = part.T


def allowed_mask(key_start, query_start, shape, prefix):
    key_pos = key_start + lax.broadcasted_iota(jnp.int32, shape, 0)
    query_pos = query_start + lax.broadcasted_iota(jnp.int32, shape, 1)
    return (key_pos < prefix) | (key_pos <= query_pos)


def forward_kernel(n_pieces, own_query, n_earlier, tok_b, block, info, *refs):
    prefix, first = info[1], info[2]
    pieces = refs[:n_pieces]
    refs = refs[n_pieces:]
    if own_query:
        query_ref, refs = refs[0], refs[1:]
        q_len = query_ref.shape[1]
        n_query = 1
    else:
        q_len = block
        n_query = n_pieces * pieces[0].shape[-1] // block
    out_ref, full_ref, lse_ref, q_t, k_n, v_t, acc = refs[n_earlier:]
    key_slot = 0 if own_query else 1
    if not own_query:
        load_pieces(info, pieces, 0, q_t, None, tok_b, block)
    load_pieces(info, pieces, key_slot, None, k_n, tok_b, block)
    load_pieces(info, pieces, key_slot + 1, v_t, None, tok_b, block)
    edge = prefix // block
    out_len = out_ref.shape[-1]

    def one_query(n, carry):
        start = first + n * q_len
        query = query_ref[...] if own_query else q_t[n]
        last = jnp.maximum(start // block, edge)
        acc[...] = jnp.zeros_like(acc)

        def step(kb, carry, masked):
            top, total = carry
            scores = jnp.dot(k_n[kb], query, preferred_element_type=jnp.float32)
            if masked:
                keep = allowed_mask(kb * block, start, scores.shape, prefix)
                scores = jnp.where(keep, scores, -1e30)
            new_top = jnp.maximum(top, jnp.max(scores, 0, keepdims=True))
            probs = jnp.exp2(scores - new_top)
            if masked:
                probs = jnp.where(keep, probs, 0.0)
            fade = jnp.exp2(top - new_top)
            total = total * fade + jnp.sum(probs, 0, keepdims=True)
            acc[...] = acc[...] * fade + jnp.dot(
                v_t[kb], probs.astype(jnp.bfloat16), preferred_element_type=jnp.float32
            )
            return (new_top, total)

        start_carry = (
            jnp.full((1, q_len), -1e30, jnp.float32),
            jnp.zeros((1, q_len), jnp.float32),
        )
        carry = lax.fori_loop(0, last, partial(step, masked=False), start_carry)
        top, total = step(last, carry, True)
        result = acc[...] / total
        for i in range(q_len // out_len):
            full_ref[n * (q_len // out_len) + i] = result[:, i * out_len : (i + 1) * out_len]
            out_ref[n * (q_len // out_len) + i] = result[
                :, i * out_len : (i + 1) * out_len
            ].astype(jnp.bfloat16)
        lse_ref[n] = top + jnp.log2(total)
        return 0

    lax.fori_loop(0, n_query, one_query, 0)


def attend(info, pieces, query, tok_b, block, earlier=()):
    total = len(pieces) * pieces[0].shape[-1]
    own = query is not None
    q_len = query.shape[1] if own else block
    n_query = 1 if own else total // block
    n_out = n_query * q_len // tok_b
    vmem = pl.BlockSpec(memory_space=pltpu.VMEM)
    return pl.pallas_call(
        partial(forward_kernel, len(pieces), own, len(earlier), tok_b, block),
        out_shape=(
            jax.ShapeDtypeStruct((n_out, HDIM, tok_b), jnp.bfloat16),
            jax.ShapeDtypeStruct((n_out, HDIM, tok_b), jnp.float32),
            jax.ShapeDtypeStruct((n_query, 1, q_len), jnp.float32),
        ),
        in_specs=[IN_SMEM] + [vmem] * (len(pieces) + own) + [ANY] * len(earlier),
        out_specs=(vmem, vmem, vmem),
        scratch_shapes=[
            pltpu.VMEM((total // block, HDIM, block), jnp.bfloat16),
            pltpu.VMEM((total // block, block, HDIM), jnp.bfloat16),
            pltpu.VMEM((total // block, HDIM, block), jnp.bfloat16),
            pltpu.VMEM((HDIM, q_len), jnp.float32),
        ],
        compiler_params=pltpu.CompilerParams(vmem_limit_bytes=VMEM_LIMIT),
        cost_estimate=pl.CostEstimate(
            flops=n_query * q_len * total * 1700, bytes_accessed=4 << 20, transcendentals=0
        ),
    )(info, *pieces, *([query] if own else []), *earlier)


def backward_kernel(n_pieces, own_query, tok_b, block, info, *refs):
    prefix, first = info[1], info[2]
    pieces = refs[:n_pieces]
    refs = refs[n_pieces:]
    if own_query:
        query_ref, refs = refs[0], refs[1:]
    full_ref, lse_ref, grad_ref = refs[:3]
    refs = refs[3:]
    total = n_pieces * pieces[0].shape[-1]
    rows = 4
    q_len = lse_ref.shape[-1]
    n_query = lse_ref.shape[0]
    outs = refs[:rows]
    refs = refs[rows:]
    if own_query:
        dq_ref, refs = refs[0], refs[1:]
    q_t, q_n, k_t, k_n, v_n, g_t, g_n, delta, dq_t, dk, dv = refs
    key_slot = 0 if own_query else 1
    if own_query:
        q_t[0] = query_ref[...]
        q_n[0] = query_ref[...].T
    else:
        load_pieces(info, pieces, 0, q_t, q_n, tok_b, block)
    load_pieces(info, pieces, key_slot, k_t, k_n, tok_b, block)
    load_pieces(info, pieces, key_slot + 1, None, v_n, tok_b, block)
    per_query = q_len // tok_b
    for n in range(n_query):
        for i in range(per_query):
            number = n * per_query + i
            span = slice(i * tok_b, (i + 1) * tok_b)
            grad = grad_ref[number]
            g_t[n, :, span] = grad
            g_n[n, span, :] = grad.T
            delta[n, :, span] = jnp.sum(
                grad.astype(jnp.float32) * full_ref[number], 0, keepdims=True
            )
    dk[...] = jnp.zeros_like(dk)
    dv[...] = jnp.zeros_like(dv)
    dq_t[...] = jnp.zeros_like(dq_t)
    edge = prefix // block

    def one_query(n, carry):
        start = first + n * q_len
        last = jnp.maximum(start // block, edge)

        def step(kb, carry, masked):
            scores = jnp.dot(k_n[kb], q_t[n], preferred_element_type=jnp.float32)
            probs = jnp.exp2(scores - lse_ref[n])
            if masked:
                keep = allowed_mask(kb * block, start, scores.shape, prefix)
                probs = jnp.where(keep, probs, 0.0)
            d_probs = jnp.dot(v_n[kb], g_t[n], preferred_element_type=jnp.float32)
            d_scores = (probs * (d_probs - delta[n])).astype(jnp.bfloat16)
            dv[kb] += jnp.dot(
                probs.astype(jnp.bfloat16), g_n[n], preferred_element_type=jnp.float32
            )
            dk[kb] += jnp.dot(d_scores, q_n[n], preferred_element_type=jnp.float32)
            dq_t[n] += jnp.dot(k_t[kb], d_scores, preferred_element_type=jnp.float32)
            return carry

        lax.fori_loop(0, last, partial(step, masked=False), 0)
        step(last, 0, True)
        return 0

    lax.fori_loop(0, n_query, one_query, 0)
    per_block = block // tok_b
    for s, out in enumerate(outs):
        source = info[0] ^ s
        for c in range(total // rows // tok_b):
            number = (info[3] ^ c) * rows + source
            where = number // per_block
            offset = pl.multiple_of((number % per_block) * tok_b, tok_b)
            span = slice(c * tok_b, (c + 1) * tok_b)
            if not own_query:
                out[0, :, span] = (
                    dq_t[where, :, pl.ds(offset, tok_b)] * HDIM ** (-0.5)
                ).astype(jnp.bfloat16)
            out[key_slot, :, span] = (
                (dk[where, pl.ds(offset, tok_b), :] * LN2).astype(jnp.bfloat16).T
            )
            out[key_slot + 1, :, span] = (
                dv[where, pl.ds(offset, tok_b), :].astype(jnp.bfloat16).T
            )
    if own_query:
        dq_ref[...] = (dq_t[0] * HDIM ** (-0.5)).astype(jnp.bfloat16)


def attend_back(info, pieces, query, full, lse, grad, tok_b, block):
    total = len(pieces) * pieces[0].shape[-1]
    own = query is not None
    n_query, _, q_len = lse.shape
    vmem = pl.BlockSpec(memory_space=pltpu.VMEM)
    n_key = total // block
    out_shape = tuple(
        jax.ShapeDtypeStruct(pieces[0].shape[:2] + (total // 4,), jnp.bfloat16) for _ in range(4)
    )
    if own:
        out_shape += (jax.ShapeDtypeStruct(query.shape, jnp.bfloat16),)
    return pl.pallas_call(
        partial(backward_kernel, len(pieces), own, tok_b, block),
        out_shape=out_shape,
        in_specs=[pl.BlockSpec(memory_space=pltpu.SMEM)] + [vmem] * (len(pieces) + own + 3),
        out_specs=(vmem,) * len(out_shape),
        scratch_shapes=[
            pltpu.VMEM((n_query, HDIM, q_len), jnp.bfloat16),
            pltpu.VMEM((n_query, q_len, HDIM), jnp.bfloat16),
            pltpu.VMEM((n_key, HDIM, block), jnp.bfloat16),
            pltpu.VMEM((n_key, block, HDIM), jnp.bfloat16),
            pltpu.VMEM((n_key, block, HDIM), jnp.bfloat16),
            pltpu.VMEM((n_query, HDIM, q_len), jnp.bfloat16),
            pltpu.VMEM((n_query, q_len, HDIM), jnp.bfloat16),
            pltpu.VMEM((n_query, 1, q_len), jnp.float32),
            pltpu.VMEM((n_query, HDIM, q_len), jnp.float32),
            pltpu.VMEM((n_key, block, HDIM), jnp.float32),
            pltpu.VMEM((n_key, block, HDIM), jnp.float32),
        ],
        compiler_params=pltpu.CompilerParams(vmem_limit_bytes=VMEM_LIMIT),
        cost_estimate=pl.CostEstimate(
            flops=n_query * q_len * total * 2200, bytes_accessed=4 << 20, transcendentals=0
        ),
    )(info, *pieces, *([query] if own else []), full, lse, grad)


def dot(left, right, left_dim, right_dim):
    return lax.dot_general(
        left,
        right,
        (((left_dim,), (right_dim,)), ((), ())),
        preferred_element_type=jnp.float32,
    )


def dp_swap(value):
    return lax.ppermute(value, "dp", [(0, 1), (1, 0)])


def col_send(value, pairs):
    return lax.ppermute(value, "col", pairs)


NEAR = [(0, 1), (1, 0), (2, 3), (3, 2)]
MIDDLE = [(1, 2), (2, 1)]


OUTWARD = [(1, 0), (2, 3)]
INWARD = [(0, 1), (3, 2)]


def pair_sum(value):
    return value.astype(jnp.float32) + dp_swap(value).astype(jnp.float32)


def add_low(left, right):
    return (left.astype(jnp.float32) + right.astype(jnp.float32)).astype(jnp.bfloat16)


def line_reduce(parts, beside=lambda stage, arrived: ()):
    ends = col_send(parts[3], INWARD)
    ends = after(ends, *parts[:3], *beside(0, None))
    outer = col_send(after(parts[2], ends), INWARD)
    inner = col_send(add_low(parts[2], ends), MIDDLE)
    inner, outer = after([inner, outer], *beside(1, ends))
    mid = col_send(add_low(parts[3], outer), MIDDLE)
    near = col_send(add_low(parts[1], inner), NEAR)
    near, mid = after([near, mid], *beside(2, inner))
    return [parts[0], near, mid]


def col_exchange(parts):
    return [parts[0]] + [
        col_send(parts[s], [(i, i ^ s) for i in range(len(parts))]) for s in range(1, len(parts))
    ]


def sum_everywhere(values):
    for axis in ("row", "col"):
        for step in (1, 2):
            values = values + lax.ppermute(values, axis, [(i, i ^ step) for i in range(4)])
    return values + dp_swap(values)


def dp_scatter(values, dp, axis):
    half = values.shape[axis] // 2
    values = values.astype(jnp.bfloat16)
    own = lax.dynamic_slice_in_dim(values, dp * half, half, axis)
    other = lax.dynamic_slice_in_dim(values, (1 - dp) * half, half, axis)
    return add_low(own, dp_swap(other))


def dp_gather(half, dp, axis):
    other = dp_swap(half)
    return jnp.concatenate(
        [jnp.where(dp == 0, half, other), jnp.where(dp == 0, other, half)], axis
    )


ANY = pl.BlockSpec(memory_space=pl.ANY)
IN_VMEM = pl.BlockSpec(memory_space=pltpu.VMEM)
IN_SMEM = pl.BlockSpec(memory_space=pltpu.SMEM)


def after(values, *earlier):
    single = not isinstance(values, (list, tuple))
    arrays = [values] if single else list(values)

    def nothing(*refs):
        pass

    got = pl.pallas_call(
        nothing,
        out_shape=[jax.ShapeDtypeStruct(a.shape, a.dtype) for a in arrays],
        in_specs=[ANY] * (len(arrays) + len(earlier)),
        out_specs=[ANY] * len(arrays),
        input_output_aliases={i: i for i in range(len(arrays))},
        cost_estimate=pl.CostEstimate(flops=0, bytes_accessed=0, transcendentals=0),
    )(*arrays, *earlier)
    return got[0] if single else list(got)


def cost(flops, *arrays):
    moved = sum(a.size * a.dtype.itemsize for a in arrays)
    return pl.CostEstimate(flops=flops, bytes_accessed=moved, transcendentals=0)


def small_kernel(body, out_shape, *operands, scalars=1, flops=0):
    return pl.pallas_call(
        body,
        out_shape=out_shape,
        in_specs=[IN_SMEM] * scalars + [IN_VMEM] * (len(operands) - scalars),
        out_specs=jax.tree.map(lambda _: IN_VMEM, out_shape),
        compiler_params=pltpu.CompilerParams(vmem_limit_bytes=VMEM_LIMIT),
        cost_estimate=cost(flops, *operands[scalars:], *jax.tree.leaves(out_shape)),
    )(*operands)


def shape_of(shape, dtype):
    return jax.ShapeDtypeStruct(shape, dtype)


def assemble(me, pieces, keep):
    def body(info, *refs):
        out = refs[-1]
        for s in range(len(pieces)):
            at = pl.multiple_of((info[0] ^ s) * keep, 16)
            out[pl.ds(at, keep), :] = refs[s][0:keep, :]

    piece = pieces[0]
    return small_kernel(
        body, shape_of((len(pieces) * keep, piece.shape[1]), piece.dtype), me, *pieces
    )


def feature_sums(values):
    return jnp.sum(values, 0, keepdims=True)


def normalised(total, squares, width):
    mean = total / width
    return mean, lax.rsqrt(squares / width - mean * mean + 1e-05)


def token_tiles(me, values, narrow, count):
    feat, tokens = values.shape
    tok = tokens // count
    extra = 0 if narrow is None else 128

    def body(info, *refs):
        outs = refs[-count:]
        if narrow is not None:
            rest = refs[1][...].T[:feat, :]
            cuts = []
            for _ in range(3):
                cuts.append(rest.astype(jnp.bfloat16))
                rest = rest - cuts[-1].astype(jnp.float32)
        for s in range(count):
            at = pl.multiple_of((info[0] ^ s) * tok, tok)
            outs[s][:, 0:tok] = refs[0][:, pl.ds(at, tok)]
            if narrow is not None:
                for n, cut in enumerate(cuts):
                    outs[s][:, tok + n * cut.shape[1] : tok + (n + 1) * cut.shape[1]] = cut
                outs[s][:, tok + 3 * cuts[0].shape[1] :] = jnp.zeros(
                    (feat, extra - 3 * cuts[0].shape[1]), jnp.bfloat16
                )

    return small_kernel(
        body,
        (shape_of((feat, tok + extra), jnp.bfloat16),) * count,
        me,
        values,
        *(() if narrow is None else (narrow,)),
    )


def first_norm(me, pieces, tok, kinds):
    count = len(pieces)
    feat = pieces[0].shape[0]

    def body(info, *refs):
        x_refs = refs[:count]
        x_out, n_out, cols_out = refs[count:]
        total = sum(feature_sums(x[:, 0:tok].astype(jnp.float32)) for x in x_refs)
        squares = sum(feature_sums(jnp.square(x[:, 0:tok].astype(jnp.float32))) for x in x_refs)
        mean, inv_std = normalised(total, squares, count * feat)
        for s in range(count):
            at = pl.multiple_of((info[0] ^ s) * feat, 16)
            extra = x_refs[s][:, tok:].astype(jnp.float32)
            cols = (
                extra[:, 0:kinds]
                + extra[:, kinds : 2 * kinds]
                + extra[:, 2 * kinds : 3 * kinds]
            )
            cols_out[pl.ds(at, feat), :] = cols
            value = x_refs[s][:, 0:tok]
            x_out[pl.ds(at, feat), :] = value
            n_out[pl.ds(at, feat), :] = (
                (value.astype(jnp.float32) - mean) * inv_std * cols[:, 0:1] + cols[:, 1:2]
            ).astype(jnp.bfloat16)

    return small_kernel(
        body,
        (
            shape_of((count * feat, tok), jnp.bfloat16),
            shape_of((count * feat, tok), jnp.bfloat16),
            shape_of((count * feat, kinds), jnp.float32),
        ),
        me,
        *pieces,
    )


def project_out(info, heads, last, out_full, x_tok, cols):
    width, tok = x_tok.shape

    def body(info, heads_ref, last_ref, out_ref, x_ref, cols_ref, att_ref, res_ref, n_ref):
        inner = heads_ref.shape[0] * heads_ref.shape[1]
        att_ref[0:inner, :] = heads_ref[...].reshape(inner, tok)
        att_ref[inner:width, :] = last_ref[0]
        blocks, feat, hd = out_ref.shape
        per_row = width // hd
        for r in range(blocks // per_row):
            span = slice(r * feat, (r + 1) * feat)
            res_ref[span, :] = (
                sum(
                    jnp.dot(
                        out_ref[r * per_row + (c ^ info[3])],
                        att_ref[c * hd : (c + 1) * hd, :],
                        preferred_element_type=jnp.float32,
                    )
                    for c in range(per_row)
                )
                + x_ref[span, :].astype(jnp.float32)
                + cols_ref[span, 2:3]
            )
        value = res_ref[...]
        mean, inv_std = normalised(feature_sums(value), feature_sums(value * value), width)
        n_ref[...] = ((value - mean) * inv_std * cols_ref[:, 3:4] + cols_ref[:, 4:5]).astype(
            jnp.bfloat16
        )

    return small_kernel(
        body,
        (
            shape_of((width, tok), jnp.bfloat16),
            shape_of((width, tok), jnp.float32),
            shape_of((width, tok), jnp.bfloat16),
        ),
        info,
        heads,
        last,
        out_full,
        x_tok,
        cols,
    )


def norm_gradient(parts, values_ref, gain):
    d_normed = sum(p[...].astype(jnp.float32) for p in parts)
    values = values_ref[...].astype(jnp.float32)
    width = values.shape[0]
    mean, inv_std = normalised(feature_sums(values), feature_sums(values * values), width)
    centred = (values - mean) * inv_std
    scaled = d_normed * gain
    d_values = inv_std * (
        scaled - feature_sums(scaled) / width - centred * (feature_sums(scaled * centred) / width)
    )
    return (
        d_values,
        jnp.sum(d_normed * centred, 1, keepdims=True),
        jnp.sum(d_normed, 1, keepdims=True),
    )


def second_norm_back(info, parts, residual, cot, cols, out_full):
    width, tok = residual.shape

    def body(info, *refs):
        parts_refs = refs[:3]
        res_ref, cot_ref, cols_ref, out_ref, d_ref, low_ref, sums_ref, att_ref = refs[3:]
        d_values, gain_sum, shift_sum = norm_gradient(parts_refs, res_ref, cols_ref[:, 3:4])
        d_res = cot_ref[...].astype(jnp.float32) + d_values
        low = d_res.astype(jnp.bfloat16)
        d_ref[...] = d_res
        low_ref[...] = low
        sums_ref[:, 0:1] = gain_sum
        sums_ref[:, 1:2] = shift_sum
        sums_ref[:, 2:3] = jnp.sum(low.astype(jnp.float32), 1, keepdims=True)
        blocks, feat, hd = out_ref.shape
        per_row = width // hd
        for c in range(per_row):
            att_ref[c * hd : (c + 1) * hd, :] = sum(
                lax.dot_general(
                    out_ref[r * per_row + (c ^ info[3])],
                    low_ref[r * feat : (r + 1) * feat, :],
                    (((0,), (0,)), ((), ())),
                    preferred_element_type=jnp.float32,
                )
                for r in range(blocks // per_row)
            ).astype(jnp.bfloat16)

    return small_kernel(
        body,
        (
            shape_of((width, tok), jnp.float32),
            shape_of((width, tok), jnp.bfloat16),
            shape_of((width, 3), jnp.float32),
            shape_of((width, tok), jnp.bfloat16),
        ),
        info,
        *parts,
        residual,
        cot,
        cols,
        out_full,
    )


def first_norm_back(me, parts, x_tok, d_residual, cols, count):
    width, tok = x_tok.shape
    feat = width // count

    def body(info, *refs):
        parts_refs = refs[:3]
        x_ref, d_ref, cols_ref = refs[3:6]
        outs = refs[6 : 6 + count]
        sums_ref, whole = refs[6 + count :]
        d_values, gain_sum, shift_sum = norm_gradient(parts_refs, x_ref, cols_ref[:, 0:1])
        whole[...] = d_ref[...] + d_values
        for s in range(count):
            at = pl.multiple_of((info[0] ^ s) * feat, 16)
            outs[s][...] = whole[pl.ds(at, feat), :].astype(jnp.bfloat16)
        sums_ref[:, 0:1] = gain_sum
        sums_ref[:, 1:2] = shift_sum

    vmem_count = 6
    return pl.pallas_call(
        body,
        out_shape=tuple(shape_of((feat, tok), jnp.bfloat16) for _ in range(count))
        + (shape_of((width, 2), jnp.float32),),
        in_specs=[IN_SMEM] + [IN_VMEM] * vmem_count,
        out_specs=(IN_VMEM,) * (count + 1),
        scratch_shapes=[pltpu.VMEM((width, tok), jnp.float32)],
        compiler_params=pltpu.CompilerParams(vmem_limit_bytes=VMEM_LIMIT),
        cost_estimate=cost(0, *parts, x_tok, d_residual, d_residual),
    )(me, *parts, x_tok, d_residual, cols)


def side_by_side(me, pieces, dtype):
    feat, tok = pieces[0].shape

    def body(info, *refs):
        for s in range(len(pieces)):
            at = pl.multiple_of((info[0] ^ s) * tok, tok)
            refs[-1][:, pl.ds(at, tok)] = refs[s][...].astype(dtype)

    return small_kernel(body, shape_of((feat, len(pieces) * tok), dtype), me, *pieces)


def normal_tail(value):
    z = value * 0.7071067811865476
    t = 1.0 / (1.0 + 0.5 * z)
    poly = jnp.full_like(t, 0.17087277)
    for factor in (
        -0.82215223,
        1.48851587,
        -1.13520398,
        0.27886807,
        -0.18628806,
        0.09678418,
        0.37409196,
        1.00002368,
        -1.26551223,
    ):
        poly = poly * t + factor
    return t * jnp.exp(poly - z * z)


def feed_forward(normed, cot, up, down, bias):
    width, tok = normed.shape
    hidden_len = up.shape[1]

    def body(n_ref, cot_ref, up_ref, down_ref, bias_ref, active_ref, d_ref, sent_ref):
        hidden = (
            jnp.dot(n_ref[...].T, up_ref[...], preferred_element_type=jnp.float32) + bias_ref[...]
        )
        d_active = jnp.dot(cot_ref[...].T, down_ref[...], preferred_element_type=jnp.float32)
        tail = 0.5 * normal_tail(jnp.abs(hidden))
        below = jnp.where(hidden < 0, tail, 1.0 - tail)
        density = 0.3989422804014327 * jnp.exp(-0.5 * hidden * hidden)
        active_ref[...] = (hidden * below).astype(jnp.bfloat16)
        d_hidden = (d_active * (below + hidden * density)).astype(jnp.bfloat16)
        d_ref[...] = d_hidden
        sent_ref[...] = lax.dot_general(
            up_ref[...],
            d_hidden,
            (((1,), (1,)), ((), ())),
            preferred_element_type=jnp.float32,
        ).astype(jnp.bfloat16)

    return small_kernel(
        body,
        (
            shape_of((tok, hidden_len), jnp.bfloat16),
            shape_of((tok, hidden_len), jnp.bfloat16),
            shape_of((width, tok), jnp.bfloat16),
        ),
        normed,
        cot,
        up,
        down,
        bias,
        scalars=0,
        flops=10 * tok * width * hidden_len,
    )


def block_products(left, right, feat, hd):
    rows, cols = left.shape[0] // feat, right.shape[0] // hd

    def body(left_ref, right_ref, out_ref):
        for r in range(rows):
            whole = lax.dot_general(
                left_ref[r * feat : (r + 1) * feat, :],
                right_ref[...],
                (((1,), (1,)), ((), ())),
                preferred_element_type=jnp.float32,
            ).astype(jnp.bfloat16)
            for c in range(cols):
                out_ref[r * cols + c] = whole[:, c * hd : (c + 1) * hd]

    return small_kernel(
        body, shape_of((rows * cols, feat, hd), jnp.bfloat16), left, right, scalars=0
    )


def row_products(me, left, right, count):
    feat = left.shape[0] // count

    def body(info, left_ref, right_ref, *outs):
        for s in range(count):
            at = pl.multiple_of((info[0] ^ s) * feat, 16)
            outs[s][...] = lax.dot_general(
                left_ref[pl.ds(at, feat), :],
                right_ref[...],
                (((1,), (1,)), ((), ())),
                preferred_element_type=jnp.float32,
            ).astype(jnp.bfloat16)

    shape = shape_of((feat, right.shape[0]), jnp.bfloat16)
    return small_kernel(body, (shape,) * count, me, left, right)


def mixed_gradient(me, heads, d_query, last_parts):
    count = len(heads)
    kinds, hdim, tokens = heads[0].shape
    rows = kinds * count * hdim + kinds * hdim

    def body(info, *refs):
        query_ref = refs[count]
        last_refs = refs[count + 1 : count + 4]
        out = refs[count + 4]
        for s in range(count):
            for k in range(kinds):
                at = pl.multiple_of((k * count + (info[0] ^ s)) * hdim, hdim)
                out[pl.ds(at, hdim), :] = refs[s][k]
        base = kinds * count * hdim
        out[base : base + hdim, :] = jnp.zeros((hdim, tokens), jnp.bfloat16)
        out[base : base + hdim, 0 : query_ref.shape[1]] = query_ref[...]
        for k in range(2):
            out[base + (k + 1) * hdim : base + (k + 2) * hdim, :] = sum(
                ref[k].astype(jnp.float32) for ref in last_refs
            ).astype(jnp.bfloat16)

    return small_kernel(
        body, shape_of((rows, tokens), jnp.bfloat16), me, *heads, d_query, *last_parts
    )


def with_bias_rows(weight, bias):
    return jnp.concatenate(
        [weight, bias[None], jnp.zeros((PAD - 1, weight.shape[1]), weight.dtype)], 0
    )


def strip_tables(cols, wide):
    native = 3 * D // cols
    slots = wide + HDIM
    from_native = np.full((cols, cols, slots), -1, np.int32)
    to_strip = np.full((cols, cols, slots), -1, np.int32)
    for c in range(cols):
        for s in range(cols):
            for block, group, table in ((c, c ^ s, 0), (c ^ s, c, 1)):
                count = 0
                for i in range(3):
                    for place in range(wide + HDIM):
                        last = place >= wide
                        column = i * D + (D - HDIM + place - wide if last else group * wide + place)
                        if column // native != block:
                            continue
                        slot = wide + place - wide if last else count
                        count += not last
                        if table == 0:
                            from_native[c, s, slot] = column - block * native
                        else:
                            to_strip[c, s, slot] = (
                                3 * wide + i * HDIM + place - wide if last else i * wide + place
                            )
    return from_native.reshape(cols, -1), to_strip.reshape(cols, -1)


def one_hot(table, col, size):
    slots = pick(jnp.asarray(table), col)
    return (lax.broadcasted_iota(jnp.int32, (size, table.shape[1]), 0) == slots[None]).astype(
        jnp.bfloat16
    )


def head_shards(
    block_input,
    cotangent,
    prefix_len,
    first_gain,
    first_shift,
    qkv_weight,
    qkv_bias,
    out_weight,
    out_bias,
    second_gain,
    second_shift,
    up_weight,
    up_bias,
    down_weight,
    down_bias,
):
    rows = lax.axis_size("row")
    cols = lax.axis_size("col")
    row = lax.axis_index("row")
    col = lax.axis_index("col")
    dp = lax.axis_index("dp")
    tok_a = block_input.shape[1]
    tok_b = tok_a // rows
    feat = block_input.shape[2]
    block = 4 * tok_b
    wide = rows * HDIM
    slots = wide + HDIM
    hidden_len = up_weight.shape[1]
    from_native, to_strip = strip_tables(cols, wide)

    me = row[None]
    narrow = jnp.concatenate(
        [
            jnp.stack(
                [first_gain, first_shift, out_bias, second_gain, second_shift, down_bias]
                + [jnp.zeros_like(first_gain)] * 2
            ),
            jnp.zeros((8, 384 - feat), jnp.float32),
        ],
        1,
    )

    x_got = row_exchange(list(token_tiles(me, block_input[0].T, narrow, rows)))
    spread = one_hot(from_native, col, qkv_weight.shape[1])
    sent = dot(with_bias_rows(qkv_weight, qkv_bias), spread, 1, 0).astype(jnp.bfloat16)
    out_rows = jnp.concatenate([out_weight.T, jnp.zeros((PAD, out_weight.shape[0]), jnp.bfloat16)])
    got = col_exchange(
        [
            jnp.concatenate([sent[:, s * slots : (s + 1) * slots], out_rows], 1)
            for s in range(cols)
        ]
    )
    x_got[1], *got[1:] = after([x_got[1], *got[1:]])
    out_got = [g[:feat, slots:] for g in got]
    got = [g[:, :slots] for g in got]
    x_tok, normed_one, cols_all = first_norm(me, x_got, tok_b, narrow.shape[0])

    near = col_send(normed_one, NEAR)
    mid = col_send(normed_one, MIDDLE)
    cot_got = row_exchange(
        list(token_tiles(me, after(cotangent[0].T, normed_one), None, rows))
    )
    near, mid, *cot_got[1:] = after([near, mid, *cot_got[1:]])
    inner = col_send(near, MIDDLE)
    outer = col_send(mid, OUTWARD)
    placed = one_hot(to_strip, col, 3 * slots)
    strip = dot(jnp.concatenate(got, 1), placed, 1, 1).astype(jnp.bfloat16)
    strip_bias = strip[feat].astype(jnp.float32)
    strip_near = swap(strip, 1)
    strip_far = swap(strip, 2)
    cot_tok = assemble(me, cot_got, feat)
    inner, outer, strip_near, strip_far = after([inner, outer, strip_near, strip_far], cot_tok)
    ends = col_send(inner, OUTWARD)
    qkv_strip = assemble(me, [strip, strip_near, strip_far, swap(strip_far, 1)], feat)

    up_down = lax.all_gather(jnp.stack([up_weight, down_weight.T]), "row")
    up_slice = up_down[:, 0].reshape(rows * feat, hidden_len)
    down_slice = up_down[:, 1].reshape(rows * feat, hidden_len)

    out_full = lax.all_gather(jnp.stack(out_got), "row").reshape((-1,) + out_weight.shape)

    query_scale = LOG2E * HDIM ** (-0.5)
    scale = jnp.concatenate(
        [
            jnp.full((wide,), query_scale, jnp.float32),
            jnp.ones((2 * wide,), jnp.float32),
            jnp.full((HDIM,), query_scale, jnp.float32),
            jnp.ones((2 * HDIM,), jnp.float32),
        ]
    )
    def project(normed):
        mixed = (
            (dot(qkv_strip, normed, 0, 0) + strip_bias[:, None]) * scale[:, None]
        ).astype(jnp.bfloat16)
        by_head = mixed[: 3 * wide].reshape(3, rows, HDIM, -1)
        return mixed, [pick(by_head, row ^ s, 1) for s in range(rows)]

    first_set = jnp.concatenate([normed_one, near], 1)
    mixed_first, tiles_first = project(first_set)
    got_first = row_exchange(tiles_first)
    ends = after(ends, *tiles_first)
    middle = (col == 1) | (col == 2)
    second_set = jnp.concatenate(
        [jnp.where(middle, inner, outer), jnp.where(middle, mid, ends)], 1
    )
    mixed_second, tiles_second = project(second_set)
    got_second = row_exchange(tiles_second)
    pieces = [p for pair in zip(got_first, got_second) for p in pair]
    last_query = mixed_first[3 * wide : 3 * wide + HDIM, :tok_b]
    last_pieces = row_gather(
        jnp.concatenate(
            [m[3 * wide + HDIM :].reshape(2, HDIM, -1) for m in (mixed_first, mixed_second)], 2
        )
    )
    normed_set = jnp.concatenate([first_set, second_set], 1)
    cot_tok = after(cot_tok, second_set)
    cot_cols = lax.all_gather(cot_tok, "col")
    cot_parts = [cot_tok] + [pick(cot_cols, col ^ s) for s in range(1, cols)]

    zero = jnp.int32(0)
    info = jnp.stack([row, prefix_len[0], zero, col])
    last_info = jnp.stack([row, prefix_len[0], col * tok_a + row * tok_b, col])
    heads_out, heads_full, heads_lse = attend(
        info, pieces, None, tok_b, block, (up_slice, down_slice, last_pieces[1])
    )
    last_out, last_full, last_lse = attend(last_info, last_pieces, last_query, tok_b, block)
    heads_got = lax.all_to_all(heads_out, ("col", "row"), 0, 0, tiled=True)
    attended, residual, normed_two = project_out(
        info, heads_got, last_out, out_full, x_tok, cols_all
    )
    hidden_bias = up_bias.astype(jnp.float32)[None]

    def through_hidden(normed, s):
        return feed_forward(normed, cot_parts[s], up_slice, down_slice, hidden_bias)

    near = col_send(normed_two, NEAR)
    mid = col_send(normed_two, MIDDLE)
    through = [through_hidden(normed_two, 0)]
    near, mid = after([near, mid], through[0][2])
    inner = col_send(near, MIDDLE)
    outer = col_send(mid, OUTWARD)
    through.append(through_hidden(near, 1))
    inner, outer = after([inner, outer], through[1][2])
    ends = col_send(inner, OUTWARD)
    second = jnp.where(middle, inner, outer)
    through.append(through_hidden(second, 2))
    ends = after(ends, through[2][2])
    third = jnp.where(middle, mid, ends)
    through.append(through_hidden(third, 3))
    d_norm_sent = [t[2] for t in through]
    normed_two = jnp.concatenate([normed_two, near, second, third], 1)
    cot_all = jnp.concatenate(cot_parts, 1)
    work = {}

    def weight_products(stage, arrived):
        if stage == 0:
            return ()
        source, left = ((1, normed_two), (0, cot_all))[stage - 1]
        right = jnp.concatenate(after([t[source] for t in through], arrived), 0)
        work[stage] = right, dot(left, right, 1, 0).astype(jnp.bfloat16)
        return (work[stage][1],)

    d_norm_two = line_reduce(d_norm_sent, weight_products)
    (low_hidden, up_part), (low_active, down_part) = work[1], work[2]
    d_residual, branch, second_sums, d_attended = second_norm_back(
        info, d_norm_two, residual, cot_tok, cols_all, out_full
    )
    d_heads = lax.all_to_all(
        d_attended[: D - HDIM].reshape(rows * cols, HDIM, tok_b), ("col", "row"), 0, 0, tiled=True
    )
    *last_grads, d_last_query = attend_back(
        last_info,
        last_pieces,
        last_query,
        last_full,
        last_lse,
        d_attended[D - HDIM :][None],
        tok_b,
        block,
    )
    head_grads = attend_back(info, pieces, None, heads_full, heads_lse, d_heads, tok_b, block)
    d_last_parts = row_reduce_parts(last_grads)

    up_down_part = jnp.stack(
        [p.reshape(rows, feat, hidden_len) for p in (up_part, down_part)], 1
    )
    up_down_half = lax.psum_scatter(up_down_part, "row", scatter_dimension=0)
    active_parts = after(low_active, d_attended).reshape(cols, tok_b, hidden_len)
    partial_out = jnp.stack(
        [
            dot(down_slice, pick(active_parts, col ^ i), 1, 1).astype(jnp.bfloat16)
            for i in range(cols)
        ]
    )
    sent_out = lax.psum_scatter(partial_out, "col", scatter_dimension=0)
    out_half = lax.psum_scatter(
        block_products(branch, attended, feat, D).reshape(rows, feat, D),
        "row",
        scatter_dimension=0,
    )

    up_down_grad = pair_sum(up_down_half)
    head_got = row_exchange(list(head_grads))
    head_got[1] = after(head_got[1], up_down_grad)
    d_mixed = mixed_gradient(me, head_got, d_last_query, d_last_parts)
    d_normed_sent = [
        dot(qkv_strip, d_mixed[:, s * tok_b : (s + 1) * tok_b], 1, 0).astype(jnp.bfloat16)
        for s in range(cols)
    ]
    kept = {}

    def beside(stage, arrived):
        if stage == 0:
            parts = row_products(me, normed_set, after(d_mixed, *d_normed_sent), rows)
            beyond, kept["near"] = swap(parts[3], 1), swap(parts[1], 1)
            pair = add_low(parts[2], beyond)
            kept["own"], kept["far"] = parts[0], swap(pair, 2)
            return (pair,)
        kept[stage] = arrived
        return ()

    d_norm_one = line_reduce(d_normed_sent, beside)
    arrived = [kept[1], kept[2], d_norm_one[1]]
    near, far = after([kept["near"], kept["far"]], arrived[1])
    total = sum(p.astype(jnp.float32) for p in (kept["own"], near, far)).astype(jnp.bfloat16)
    both = jnp.concatenate([total, out_half], 1)
    half = feat // 2
    other = dp_swap(lax.dynamic_slice_in_dim(both, (1 - dp) * half, half, 0))
    total = add_low(lax.dynamic_slice_in_dim(both, dp * half, half, 0), other)
    sent = dot(total[:, : 3 * slots], placed, 1, 0).astype(jnp.bfloat16)
    hd = D // cols
    got = col_exchange(
        [
            jnp.concatenate(
                [
                    sent[:, s * slots : (s + 1) * slots],
                    lax.dynamic_slice_in_dim(total, 3 * slots + (col ^ s) * hd, hd, 1),
                ],
                1,
            )
            for s in range(cols)
        ]
    )
    qkv = dot(jnp.concatenate([g[:, :slots] for g in got], 1), spread, 1, 1)
    out = sum(g[:, slots:].astype(jnp.float32) for g in got)
    last_grad = dp_gather(jnp.concatenate([qkv, out], 1).astype(jnp.bfloat16), dp, 0)
    qkv_grad, out_grad = jnp.split(last_grad.astype(jnp.float32), [qkv_weight.shape[1]], 1)

    out_value = (
        after(sent_out, arrived[0]).astype(jnp.float32) + residual + cols_all[:, 5:6]
    ).astype(jnp.bfloat16)
    block_got = row_exchange(
        [lax.dynamic_slice_in_dim(out_value, (row ^ s) * feat, feat, 0) for s in range(rows)]
    )
    block_output = side_by_side(me, after(block_got, arrived[1]), jnp.bfloat16)
    *input_parts, first_sums = first_norm_back(
        me, d_norm_one, x_tok, d_residual, cols_all, rows
    )
    input_grad = side_by_side(me, row_exchange(input_parts), jnp.float32)

    at_row = (jnp.arange(rows) == row)[:, None]

    def own_row(values):
        return jnp.where(at_row, values[None], 0.0).reshape(-1)

    def own_col(values):
        return jnp.where((jnp.arange(cols) == col)[:, None], values[None], 0.0).reshape(-1)

    bias_strip = jnp.sum(d_mixed.astype(jnp.float32), 1)
    at_col = (jnp.arange(cols) == col)[None, :, None]
    bias_heads = jnp.where(at_col, bias_strip[: 3 * wide].reshape(3, 1, wide), 0.0)
    bias_all = jnp.concatenate(
        [bias_heads.reshape(3, -1), bias_strip[3 * wide :].reshape(3, HDIM)], 1
    ).reshape(-1)
    early = [
        own_row(jnp.sum(cotangent[0].astype(jnp.float32), 0)),
        second_sums[:, 2],
        second_sums[:, 0],
        second_sums[:, 1],
        own_col(jnp.sum(low_hidden.astype(jnp.float32), 0)),
        bias_all,
        first_sums[:, 0],
        first_sums[:, 1],
    ]
    total = sum_everywhere(jnp.concatenate(early).reshape(8, -1)).reshape(-1)

    def own_part(start, size, index):
        return lax.dynamic_slice_in_dim(total, start + index * size, size, 0)

    width = rows * feat
    up_at = 4 * width
    qkv_at = up_at + cols * hidden_len
    first_at = qkv_at + 3 * width
    return (
        block_output.T[None],
        input_grad.T[None],
        own_part(first_at, feat, row),
        own_part(first_at + width, feat, row),
        qkv_grad,
        own_part(qkv_at, 3 * width // cols, col),
        out_grad.T,
        own_part(width, feat, row),
        own_part(2 * width, feat, row),
        own_part(3 * width, feat, row),
        up_down_grad[0],
        own_part(up_at, hidden_len, col),
        up_down_grad[1].T,
        own_part(0, feat, row),
    )


def solution(mesh):
    in_specs = (
        P("dp", "col", "row"),
        P("dp", "col", "row"),
        P("dp"),
        P("row"),
        P("row"),
        P("row", "col"),
        P("col"),
        P("col", "row"),
        P("row"),
        P("row"),
        P("row"),
        P("row", "col"),
        P("col"),
        P("col", "row"),
        P("row"),
    )
    out_specs = (
        P("dp", "col", "row"),
        P("dp", "col", "row"),
        P("row"),
        P("row"),
        P("row", "col"),
        P("col"),
        P("col", "row"),
        P("row"),
        P("row"),
        P("row"),
        P("row", "col"),
        P("col"),
        P("col", "row"),
        P("row"),
    )
    one_head_each = mesh.shape["row"] == 4 and mesh.shape["col"] == 4 and mesh.shape["dp"] == 2
    body = head_shards if one_head_each else shards
    return jax.shard_map(body, mesh=mesh, in_specs=in_specs, out_specs=out_specs, check_vma=False)
```

```python
from functools import partial

import jax
import jax.numpy as jnp
import numpy as np
from jax import lax
from jax.experimental import pallas as pl
from jax.experimental.pallas import tpu as pltpu
from jax.sharding import PartitionSpec as P

HEADS = 17
HDIM = 64
D = 1088


def positions(first_row, piece_len, tok_b, tok_a, col_total):
    flat_rows = first_row + jnp.arange(piece_len, dtype=jnp.int32)
    shard_no = flat_rows // tok_b
    return shard_no % col_total * tok_a + shard_no // col_total * tok_b + flat_rows % tok_b


def over_blocks(folded, pieces, step_fn):
    piece_len = pieces[0].shape[0]
    block_len = 512

    def one_block(block_no, running):
        offset = block_no * block_len
        sliced = tuple(
            (lax.dynamic_slice_in_dim(member, offset, block_len, 0) for member in pieces)
        )
        return step_fn(running, sliced, offset)

    return lax.fori_loop(0, piece_len // block_len, one_block, folded)


def head_scores(left, right, scale_factor):
    return (
        jnp.einsum("qhd,khd->hqk", left, right, preferred_element_type=jnp.float32) * scale_factor
    )


def normalize(values, norm_gain, norm_shift):
    width_all = values.shape[1] * lax.axis_size("row")
    row_sums = lax.psum((jnp.sum(values, 1), jnp.sum(values * values, 1)), "row")
    row_mean = row_sums[0] / width_all
    variance = row_sums[1] / width_all - row_mean * row_mean
    inv_std = lax.rsqrt(variance + 1e-05)
    centred = (values - row_mean[:, None]) * inv_std[:, None]
    return (centred * norm_gain + norm_shift, centred, inv_std)


def norm_back(d_normed, centred, inv_std, norm_gain):
    width_all = d_normed.shape[1] * lax.axis_size("row")
    scaled = d_normed * norm_gain
    row_sums = lax.psum((jnp.sum(scaled, 1), jnp.sum(scaled * centred, 1)), "row")
    d_values = inv_std[:, None] * (
        scaled - row_sums[0][:, None] / width_all - centred * row_sums[1][:, None] / width_all
    )
    return (d_values, jnp.sum(d_normed * centred, 0), jnp.sum(d_normed, 0))


def row_partials(term_fn, tok_b):
    return lax.psum_scatter(
        term_fn(jnp.int32(0), tok_b * lax.axis_size("row")).astype(jnp.bfloat16),
        "row",
        scatter_dimension=0,
        tiled=True,
    ).astype(jnp.float32)


def rows_gather(values):
    return lax.all_gather(values, "row", axis=0, tiled=True)


def row_product(normed_low, weight, tok_b):

    def term_fn(first_row, row_count):
        return jnp.dot(normed_low, weight, preferred_element_type=jnp.float32)

    return row_partials(term_fn, tok_b)


def back_product(grad_low, weight, tok_b):

    def term_fn(first_row, row_count):
        return lax.dot_general(
            grad_low, weight, (((1,), (1,)), ((), ())), preferred_element_type=jnp.float32
        )

    return row_partials(term_fn, tok_b)


def fold_back(grad_rows, normed_low, weight_full):
    piece = lax.all_gather(grad_rows, "row", axis=0, tiled=True)
    contrib = lax.dot_general(
        piece, weight_full, (((1,), (1,)), ((), ())), preferred_element_type=jnp.float32
    )
    d_weight = lax.dot_general(
        normed_low, piece, (((0,), (0,)), ((), ())), preferred_element_type=jnp.float32
    )
    return (contrib, d_weight, jnp.sum(piece.astype(jnp.float32), 0))


def scatter_columns(gradients):
    return (
        lax.psum_scatter(
            gradients[0].astype(jnp.bfloat16), "col", scatter_dimension=1, tiled=True
        ).astype(jnp.float32),
        lax.psum_scatter(
            gradients[1].astype(jnp.bfloat16), "col", scatter_dimension=0, tiled=True
        ).astype(jnp.float32),
        lax.psum_scatter(
            gradients[2].astype(jnp.bfloat16), "col", scatter_dimension=0, tiled=True
        ).astype(jnp.float32),
        lax.psum_scatter(
            gradients[3].astype(jnp.bfloat16), "col", scatter_dimension=1, tiled=True
        ).astype(jnp.float32),
        lax.psum_scatter(
            gradients[4].astype(jnp.bfloat16), "col", scatter_dimension=0, tiled=True
        ).astype(jnp.float32),
        lax.psum_scatter(
            gradients[5].astype(jnp.bfloat16), "col", scatter_dimension=0, tiled=True
        ).astype(jnp.float32),
    )


def sum_over_data(gradients):
    return (
        lax.psum(gradients[0].astype(jnp.bfloat16), "dp").astype(jnp.float32),
        lax.psum(gradients[1].astype(jnp.bfloat16), "dp").astype(jnp.float32),
        lax.psum(gradients[2].astype(jnp.bfloat16), "dp").astype(jnp.float32),
        lax.psum(gradients[3].astype(jnp.bfloat16), "dp").astype(jnp.float32),
        lax.psum(gradients[4].astype(jnp.bfloat16), "dp").astype(jnp.float32),
        lax.psum(gradients[5].astype(jnp.bfloat16), "dp").astype(jnp.float32),
    )


def shards(
    block_input,
    cotangent,
    prefix_len,
    first_gain,
    first_shift,
    qkv_weight,
    qkv_bias,
    out_weight,
    out_bias,
    second_gain,
    second_shift,
    up_weight,
    up_bias,
    down_weight,
    down_bias,
):
    row_total = lax.axis_size("row")
    col_total = lax.axis_size("col")
    tok_a = block_input.shape[1]
    tok_b = tok_a // row_total
    scale_factor = HDIM ** (-0.5)
    gathered = (
        lax.all_gather(qkv_weight, "col", axis=1, tiled=True),
        lax.all_gather(qkv_bias, "col", axis=0, tiled=True),
        lax.all_gather(out_weight, "col", axis=0, tiled=True),
        lax.all_gather(up_weight, "col", axis=1, tiled=True),
        lax.all_gather(up_bias, "col", axis=0, tiled=True),
        lax.all_gather(down_weight, "col", axis=0, tiled=True),
    )
    qkv_full, qkv_bias_full, out_full, up_full, up_bias_full, down_full = gathered
    residual = block_input[0].astype(jnp.float32)
    prefix_end = prefix_len[0]
    own_pos = (
        lax.axis_index("col") * tok_a
        + lax.axis_index("row") * tok_b
        + jnp.arange(tok_b, dtype=jnp.int32)
    )

    def visible(key_pos, query_pos):
        return (key_pos[None, :] < prefix_end) | (key_pos[None, :] <= query_pos[:, None])

    def piece_pos(first_row, piece_len):
        return positions(first_row, piece_len, tok_b, tok_a, col_total)

    normed_one, centred_one, inv_one = normalize(residual, first_gain, first_shift)
    normed_one_low = normed_one.astype(jnp.bfloat16)
    mixed_qkv = (
        row_product(normed_one_low, qkv_full, tok_b) + qkv_bias_full.astype(jnp.float32)
    ).astype(jnp.bfloat16)
    query_rows = mixed_qkv[:, :D]
    key_rows = mixed_qkv[:, D : 2 * D]
    value_rows = mixed_qkv[:, 2 * D :]
    own_query = query_rows.reshape(tok_b, HEADS, HDIM)
    own_key = key_rows.reshape(tok_b, HEADS, HDIM)
    own_value = value_rows.reshape(tok_b, HEADS, HDIM)

    def max_step(running, sliced, first_row):
        key_block = sliced[0]
        allowed = visible(piece_pos(first_row, key_block.shape[0]), own_pos)
        scores = jnp.where(
            allowed[None],
            head_scores(own_query, key_block.reshape(-1, HEADS, HDIM), scale_factor),
            -1e30,
        )
        new_max = jnp.maximum(running[0], jnp.max(scores, 2))
        new_total = running[1] * jnp.exp(running[0] - new_max) + jnp.sum(
            jnp.where(allowed[None], jnp.exp(scores - new_max[:, :, None]), 0.0), 2
        )
        return (new_max, new_total)

    start_max = (
        jnp.full((HEADS, tok_b), -1e30, jnp.float32),
        jnp.zeros((HEADS, tok_b), jnp.float32),
    )
    run_max, run_total = over_blocks(
        start_max, (lax.all_gather(key_rows, ("row", "col"), axis=0, tiled=True),), max_step
    )
    log_total = run_max + jnp.log(run_total)

    def value_step(running, sliced, first_row):
        key_block, value_block = sliced
        allowed = visible(piece_pos(first_row, key_block.shape[0]), own_pos)
        scores = head_scores(own_query, key_block.reshape(-1, HEADS, HDIM), scale_factor)
        attn_probs = jnp.where(allowed[None], jnp.exp(scores - log_total[:, :, None]), 0.0).astype(
            jnp.bfloat16
        )
        return running + jnp.einsum(
            "hqk,khd->qhd",
            attn_probs,
            value_block.reshape(-1, HEADS, HDIM),
            preferred_element_type=jnp.float32,
        )

    attn_acc = over_blocks(
        jnp.zeros((tok_b, HEADS, HDIM), jnp.float32),
        (
            lax.all_gather(key_rows, ("row", "col"), axis=0, tiled=True),
            lax.all_gather(value_rows, ("row", "col"), axis=0, tiled=True),
        ),
        value_step,
    )
    attn_float = attn_acc.reshape(tok_b, D)
    attn_all = rows_gather(attn_float.astype(jnp.bfloat16))
    residual_two = (
        residual + jnp.dot(attn_all, out_full, preferred_element_type=jnp.float32) + out_bias
    )
    normed_two, centred_two, inv_two = normalize(residual_two, second_gain, second_shift)
    normed_two_low = normed_two.astype(jnp.bfloat16)
    hidden = row_product(normed_two_low, up_full, tok_b) + up_bias_full.astype(jnp.float32)
    active_all = rows_gather(jax.nn.gelu(hidden, approximate=False).astype(jnp.bfloat16))
    block_output = (
        residual_two
        + jnp.dot(active_all, down_full, preferred_element_type=jnp.float32)
        + down_bias
    ).astype(jnp.bfloat16)
    cot_low = cotangent[0]
    cot_float = cot_low.astype(jnp.float32)
    down_grad = lax.dot_general(
        active_all, cot_low, (((0,), (0,)), ((), ())), preferred_element_type=jnp.float32
    )
    down_bias_grad = jnp.sum(cot_float, 0)
    d_active = back_product(cot_low, down_full, tok_b)
    gelu_back = jax.vjp(partial(jax.nn.gelu, approximate=False), hidden)[1]
    d_hidden_low = gelu_back(d_active)[0].astype(jnp.bfloat16)
    d_norm_two, up_grad, up_bias_grad = fold_back(d_hidden_low, normed_two_low, up_full)
    d_part_two, second_gain_grad, second_shift_grad = norm_back(
        d_norm_two, centred_two, inv_two, second_gain
    )
    d_residual = cot_float + d_part_two
    branch_low = d_residual.astype(jnp.bfloat16)
    out_grad = lax.dot_general(
        attn_all, branch_low, (((0,), (0,)), ((), ())), preferred_element_type=jnp.float32
    )
    out_bias_grad = jnp.sum(branch_low.astype(jnp.float32), 0)
    d_attn_low = back_product(branch_low, out_full, tok_b).astype(jnp.bfloat16)
    delta_rows = jnp.sum(
        (d_attn_low.astype(jnp.float32) * attn_float).reshape(tok_b, HEADS, HDIM), 2
    )
    lse_rows = log_total.T
    all_lse, all_delta = (
        lax.all_gather(lse_rows, ("row", "col"), axis=0, tiled=True),
        lax.all_gather(delta_rows, ("row", "col"), axis=0, tiled=True),
    )
    own_grad = d_attn_low.reshape(tok_b, HEADS, HDIM)

    def back_step(running, sliced, first_row):
        query_p, key_p, value_p, grad_p = sliced
        piece_len = query_p.shape[0]
        pos_piece = piece_pos(first_row, piece_len)
        lse_piece = lax.dynamic_slice_in_dim(all_lse, first_row, piece_len, 0)
        delta_piece = lax.dynamic_slice_in_dim(all_delta, first_row, piece_len, 0)
        query_p3 = query_p.reshape(piece_len, HEADS, HDIM)
        key_p3 = key_p.reshape(piece_len, HEADS, HDIM)
        value_p3 = value_p.reshape(piece_len, HEADS, HDIM)
        grad_p3 = grad_p.reshape(piece_len, HEADS, HDIM)
        allowed_own = visible(pos_piece, own_pos)
        allowed_far = visible(own_pos, pos_piece)
        scores = head_scores(own_query, key_p3, scale_factor)
        attn_probs = jnp.where(allowed_own[None], jnp.exp(scores - log_total[:, :, None]), 0.0)
        d_probs = jnp.einsum("qhd,khd->hqk", own_grad, value_p3, preferred_element_type=jnp.float32)
        d_scores = (attn_probs * (d_probs - delta_rows.T[:, :, None])).astype(jnp.bfloat16)
        new_query = (
            running[0]
            + jnp.einsum("hqk,khd->qhd", d_scores, key_p3, preferred_element_type=jnp.float32)
            * scale_factor
        )
        scores = head_scores(query_p3, own_key, scale_factor)
        attn_probs = jnp.where(allowed_far[None], jnp.exp(scores - lse_piece.T[:, :, None]), 0.0)
        d_value = running[2] + jnp.einsum(
            "hqk,qhd->khd",
            attn_probs.astype(jnp.bfloat16),
            grad_p3,
            preferred_element_type=jnp.float32,
        )
        d_probs = jnp.einsum("qhd,khd->hqk", grad_p3, own_value, preferred_element_type=jnp.float32)
        d_scores = (attn_probs * (d_probs - delta_piece.T[:, :, None])).astype(jnp.bfloat16)
        d_key = (
            running[1]
            + jnp.einsum("hqk,qhd->khd", d_scores, query_p3, preferred_element_type=jnp.float32)
            * scale_factor
        )
        return (new_query, d_key, d_value)

    zero_heads = jnp.zeros((tok_b, HEADS, HDIM), jnp.float32)
    d_query, d_key, d_value = over_blocks(
        (zero_heads, zero_heads, zero_heads),
        (
            lax.all_gather(query_rows, ("row", "col"), axis=0, tiled=True),
            lax.all_gather(key_rows, ("row", "col"), axis=0, tiled=True),
            lax.all_gather(value_rows, ("row", "col"), axis=0, tiled=True),
            lax.all_gather(d_attn_low, ("row", "col"), axis=0, tiled=True),
        ),
        back_step,
    )
    d_mixed_low = jnp.concatenate(
        [d_query.reshape(tok_b, D), d_key.reshape(tok_b, D), d_value.reshape(tok_b, D)], 1
    ).astype(jnp.bfloat16)
    d_norm_one, qkv_grad, qkv_bias_grad = fold_back(d_mixed_low, normed_one_low, qkv_full)
    d_part_one, first_gain_grad, first_shift_grad = norm_back(
        d_norm_one, centred_one, inv_one, first_gain
    )
    input_grad = d_residual + d_part_one
    col_ready = (qkv_grad, qkv_bias_grad, out_grad, up_grad, up_bias_grad, down_grad)
    reduced = scatter_columns(sum_over_data(col_ready))
    small = lax.psum(
        (
            first_gain_grad,
            first_shift_grad,
            out_bias_grad,
            second_gain_grad,
            second_shift_grad,
            down_bias_grad,
        ),
        ("dp", "col"),
    )
    return (
        block_output[None],
        input_grad[None],
        small[0],
        small[1],
        reduced[0],
        reduced[1],
        reduced[2],
        small[2],
        small[3],
        small[4],
        reduced[3],
        reduced[4],
        reduced[5],
        small[5],
    )


LOG2E = 1.4426950408889634
LN2 = 0.6931471805599453
PAD = 16
MEBI = 1024 * 1024
VMEM_LIMIT = 56 * MEBI


def swap(value, step):
    size = lax.axis_size("row")
    return lax.ppermute(value, "row", [(i, i ^ step) for i in range(size)])


def pick(stacked, index, axis=0):
    return lax.dynamic_index_in_dim(stacked, index, axis, keepdims=False)


def row_gather(own):
    far = swap(own, 2)
    return [own, swap(own, 1), far, swap(far, 1)]


def row_exchange(parts):
    return [parts[0], swap(parts[1], 1), swap(parts[2], 2), swap(parts[3], 3)]


def row_reduce_parts(parts):
    low = [p.astype(jnp.bfloat16) for p in parts]
    beyond = swap(low[3], 1)
    near = swap(low[1], 1)
    far = swap(add_low(parts[2], beyond), 2)
    return [parts[0], near, far]


def row_reduce(parts):
    return sum(p.astype(jnp.float32) for p in row_reduce_parts(parts))


def in_order(parts, me):
    stacked = jnp.stack(parts)
    return [pick(stacked, me ^ i) for i in range(len(parts))]


def layer_norm(values, gain, shift):
    mean = jnp.mean(values, 1, keepdims=True)
    variance = jnp.mean(values * values, 1, keepdims=True) - mean * mean
    inv_std = lax.rsqrt(variance + 1e-05)
    centred = (values - mean) * inv_std
    return (centred * gain + shift, centred, inv_std)


def layer_norm_back(d_normed, centred, inv_std, gain):
    scaled = d_normed * gain
    return inv_std * (
        scaled
        - jnp.mean(scaled, 1, keepdims=True)
        - centred * jnp.mean(scaled * centred, 1, keepdims=True)
    )


def load_pieces(info, pieces, slot, transposed, plain, tok_b, block):
    rows = 4
    groups = len(pieces) // rows
    cols = pieces[0].shape[-1] // tok_b
    per_block = block // tok_b
    for p, piece in enumerate(pieces):
        source = info[0] ^ (p // groups)
        for c in range(cols):
            part = piece[slot, :, c * tok_b : (c + 1) * tok_b]
            number = (info[3] ^ (p % groups * cols + c)) * rows + source
            where = number // per_block
            offset = pl.multiple_of((number % per_block) * tok_b, tok_b)
            if transposed is not None:
                transposed[where, :, pl.ds(offset, tok_b)] = part
            if plain is not None:
                plain[where, pl.ds(offset, tok_b), :] = part.T


def allowed_mask(key_start, query_start, shape, prefix):
    key_pos = key_start + lax.broadcasted_iota(jnp.int32, shape, 0)
    query_pos = query_start + lax.broadcasted_iota(jnp.int32, shape, 1)
    return (key_pos < prefix) | (key_pos <= query_pos)


def forward_kernel(n_pieces, own_query, n_earlier, tok_b, block, info, *refs):
    prefix, first = info[1], info[2]
    pieces = refs[:n_pieces]
    refs = refs[n_pieces:]
    if own_query:
        query_ref, refs = refs[0], refs[1:]
        q_len = query_ref.shape[1]
        n_query = 1
    else:
        q_len = block
        n_query = n_pieces * pieces[0].shape[-1] // block
    out_ref, full_ref, lse_ref, q_t, k_n, v_t, acc = refs[n_earlier:]
    key_slot = 0 if own_query else 1
    if not own_query:
        load_pieces(info, pieces, 0, q_t, None, tok_b, block)
    load_pieces(info, pieces, key_slot, None, k_n, tok_b, block)
    load_pieces(info, pieces, key_slot + 1, v_t, None, tok_b, block)
    edge = prefix // block
    out_len = out_ref.shape[-1]

    def one_query(n, carry):
        start = first + n * q_len
        query = query_ref[...] if own_query else q_t[n]
        last = jnp.maximum(start // block, edge)
        acc[...] = jnp.zeros_like(acc)

        def step(kb, carry, masked):
            top, total = carry
            scores = jnp.dot(k_n[kb], query, preferred_element_type=jnp.float32)
            if masked:
                keep = allowed_mask(kb * block, start, scores.shape, prefix)
                scores = jnp.where(keep, scores, -1e30)
            new_top = jnp.maximum(top, jnp.max(scores, 0, keepdims=True))
            probs = jnp.exp2(scores - new_top)
            if masked:
                probs = jnp.where(keep, probs, 0.0)
            fade = jnp.exp2(top - new_top)
            total = total * fade + jnp.sum(probs, 0, keepdims=True)
            acc[...] = acc[...] * fade + jnp.dot(
                v_t[kb], probs.astype(jnp.bfloat16), preferred_element_type=jnp.float32
            )
            return (new_top, total)

        start_carry = (
            jnp.full((1, q_len), -1e30, jnp.float32),
            jnp.zeros((1, q_len), jnp.float32),
        )
        carry = lax.fori_loop(0, last, partial(step, masked=False), start_carry)
        top, total = step(last, carry, True)
        result = acc[...] / total
        for i in range(q_len // out_len):
            full_ref[n * (q_len // out_len) + i] = result[:, i * out_len : (i + 1) * out_len]
            out_ref[n * (q_len // out_len) + i] = result[
                :, i * out_len : (i + 1) * out_len
            ].astype(jnp.bfloat16)
        lse_ref[n] = top + jnp.log2(total)
        return 0

    lax.fori_loop(0, n_query, one_query, 0)


def attend(info, pieces, query, tok_b, block, earlier=()):
    total = len(pieces) * pieces[0].shape[-1]
    own = query is not None
    q_len = query.shape[1] if own else block
    n_query = 1 if own else total // block
    n_out = n_query * q_len // tok_b
    vmem = pl.BlockSpec(memory_space=pltpu.VMEM)
    return pl.pallas_call(
        partial(forward_kernel, len(pieces), own, len(earlier), tok_b, block),
        out_shape=(
            jax.ShapeDtypeStruct((n_out, HDIM, tok_b), jnp.bfloat16),
            jax.ShapeDtypeStruct((n_out, HDIM, tok_b), jnp.float32),
            jax.ShapeDtypeStruct((n_query, 1, q_len), jnp.float32),
        ),
        in_specs=[IN_SMEM] + [vmem] * (len(pieces) + own) + [ANY] * len(earlier),
        out_specs=(vmem, vmem, vmem),
        scratch_shapes=[
            pltpu.VMEM((total // block, HDIM, block), jnp.bfloat16),
            pltpu.VMEM((total // block, block, HDIM), jnp.bfloat16),
            pltpu.VMEM((total // block, HDIM, block), jnp.bfloat16),
            pltpu.VMEM((HDIM, q_len), jnp.float32),
        ],
        compiler_params=pltpu.CompilerParams(vmem_limit_bytes=VMEM_LIMIT),
        cost_estimate=pl.CostEstimate(
            flops=n_query * q_len * total * 1700, bytes_accessed=4 << 20, transcendentals=0
        ),
    )(info, *pieces, *([query] if own else []), *earlier)


def backward_kernel(n_pieces, own_query, tok_b, block, info, *refs):
    prefix, first = info[1], info[2]
    pieces = refs[:n_pieces]
    refs = refs[n_pieces:]
    if own_query:
        query_ref, refs = refs[0], refs[1:]
    full_ref, lse_ref, grad_ref = refs[:3]
    refs = refs[3:]
    total = n_pieces * pieces[0].shape[-1]
    rows = 4
    q_len = lse_ref.shape[-1]
    n_query = lse_ref.shape[0]
    outs = refs[:rows]
    refs = refs[rows:]
    if own_query:
        dq_ref, refs = refs[0], refs[1:]
    q_t, q_n, k_t, k_n, v_n, g_t, g_n, delta, dq_t, dk, dv = refs
    key_slot = 0 if own_query else 1
    if own_query:
        q_t[0] = query_ref[...]
        q_n[0] = query_ref[...].T
    else:
        load_pieces(info, pieces, 0, q_t, q_n, tok_b, block)
    load_pieces(info, pieces, key_slot, k_t, k_n, tok_b, block)
    load_pieces(info, pieces, key_slot + 1, None, v_n, tok_b, block)
    per_query = q_len // tok_b
    for n in range(n_query):
        for i in range(per_query):
            number = n * per_query + i
            span = slice(i * tok_b, (i + 1) * tok_b)
            grad = grad_ref[number]
            g_t[n, :, span] = grad
            g_n[n, span, :] = grad.T
            delta[n, :, span] = jnp.sum(
                grad.astype(jnp.float32) * full_ref[number], 0, keepdims=True
            )
    dk[...] = jnp.zeros_like(dk)
    dv[...] = jnp.zeros_like(dv)
    dq_t[...] = jnp.zeros_like(dq_t)
    edge = prefix // block

    def one_query(n, carry):
        start = first + n * q_len
        last = jnp.maximum(start // block, edge)

        def step(kb, carry, masked):
            scores = jnp.dot(k_n[kb], q_t[n], preferred_element_type=jnp.float32)
            probs = jnp.exp2(scores - lse_ref[n])
            if masked:
                keep = allowed_mask(kb * block, start, scores.shape, prefix)
                probs = jnp.where(keep, probs, 0.0)
            d_probs = jnp.dot(v_n[kb], g_t[n], preferred_element_type=jnp.float32)
            d_scores = (probs * (d_probs - delta[n])).astype(jnp.bfloat16)
            dv[kb] += jnp.dot(
                probs.astype(jnp.bfloat16), g_n[n], preferred_element_type=jnp.float32
            )
            dk[kb] += jnp.dot(d_scores, q_n[n], preferred_element_type=jnp.float32)
            dq_t[n] += jnp.dot(k_t[kb], d_scores, preferred_element_type=jnp.float32)
            return carry

        lax.fori_loop(0, last, partial(step, masked=False), 0)
        step(last, 0, True)
        return 0

    lax.fori_loop(0, n_query, one_query, 0)
    per_block = block // tok_b
    for s, out in enumerate(outs):
        source = info[0] ^ s
        for c in range(total // rows // tok_b):
            number = (info[3] ^ c) * rows + source
            where = number // per_block
            offset = pl.multiple_of((number % per_block) * tok_b, tok_b)
            span = slice(c * tok_b, (c + 1) * tok_b)
            if not own_query:
                out[0, :, span] = (
                    dq_t[where, :, pl.ds(offset, tok_b)] * HDIM ** (-0.5)
                ).astype(jnp.bfloat16)
            out[key_slot, :, span] = (
                (dk[where, pl.ds(offset, tok_b), :] * LN2).astype(jnp.bfloat16).T
            )
            out[key_slot + 1, :, span] = (
                dv[where, pl.ds(offset, tok_b), :].astype(jnp.bfloat16).T
            )
    if own_query:
        dq_ref[...] = (dq_t[0] * HDIM ** (-0.5)).astype(jnp.bfloat16)


def attend_back(info, pieces, query, full, lse, grad, tok_b, block):
    total = len(pieces) * pieces[0].shape[-1]
    own = query is not None
    n_query, _, q_len = lse.shape
    vmem = pl.BlockSpec(memory_space=pltpu.VMEM)
    n_key = total // block
    out_shape = tuple(
        jax.ShapeDtypeStruct(pieces[0].shape[:2] + (total // 4,), jnp.bfloat16) for _ in range(4)
    )
    if own:
        out_shape += (jax.ShapeDtypeStruct(query.shape, jnp.bfloat16),)
    return pl.pallas_call(
        partial(backward_kernel, len(pieces), own, tok_b, block),
        out_shape=out_shape,
        in_specs=[pl.BlockSpec(memory_space=pltpu.SMEM)] + [vmem] * (len(pieces) + own + 3),
        out_specs=(vmem,) * len(out_shape),
        scratch_shapes=[
            pltpu.VMEM((n_query, HDIM, q_len), jnp.bfloat16),
            pltpu.VMEM((n_query, q_len, HDIM), jnp.bfloat16),
            pltpu.VMEM((n_key, HDIM, block), jnp.bfloat16),
            pltpu.VMEM((n_key, block, HDIM), jnp.bfloat16),
            pltpu.VMEM((n_key, block, HDIM), jnp.bfloat16),
            pltpu.VMEM((n_query, HDIM, q_len), jnp.bfloat16),
            pltpu.VMEM((n_query, q_len, HDIM), jnp.bfloat16),
            pltpu.VMEM((n_query, 1, q_len), jnp.float32),
            pltpu.VMEM((n_query, HDIM, q_len), jnp.float32),
            pltpu.VMEM((n_key, block, HDIM), jnp.float32),
            pltpu.VMEM((n_key, block, HDIM), jnp.float32),
        ],
        compiler_params=pltpu.CompilerParams(vmem_limit_bytes=VMEM_LIMIT),
        cost_estimate=pl.CostEstimate(
            flops=n_query * q_len * total * 2200, bytes_accessed=4 << 20, transcendentals=0
        ),
    )(info, *pieces, *([query] if own else []), full, lse, grad)


def dot(left, right, left_dim, right_dim):
    return lax.dot_general(
        left,
        right,
        (((left_dim,), (right_dim,)), ((), ())),
        preferred_element_type=jnp.float32,
    )


def dp_swap(value):
    return lax.ppermute(value, "dp", [(0, 1), (1, 0)])


def col_send(value, pairs):
    return lax.ppermute(value, "col", pairs)


NEAR = [(0, 1), (1, 0), (2, 3), (3, 2)]
MIDDLE = [(1, 2), (2, 1)]


OUTWARD = [(1, 0), (2, 3)]
INWARD = [(0, 1), (3, 2)]


def pair_sum(value):
    return value.astype(jnp.float32) + dp_swap(value).astype(jnp.float32)


def add_low(left, right):
    return (left.astype(jnp.float32) + right.astype(jnp.float32)).astype(jnp.bfloat16)


def line_reduce(parts, beside=lambda stage, arrived: ()):
    ends = col_send(parts[3], INWARD)
    ends = after(ends, *parts[:3], *beside(0, None))
    outer = col_send(after(parts[2], ends), INWARD)
    inner = col_send(add_low(parts[2], ends), MIDDLE)
    inner, outer = after([inner, outer], *beside(1, ends))
    mid = col_send(add_low(parts[3], outer), MIDDLE)
    near = col_send(add_low(parts[1], inner), NEAR)
    near, mid = after([near, mid], *beside(2, inner))
    return [parts[0], near, mid]


def col_exchange(parts):
    return [parts[0]] + [
        col_send(parts[s], [(i, i ^ s) for i in range(len(parts))]) for s in range(1, len(parts))
    ]


def sum_everywhere(values):
    for axis in ("row", "col"):
        for step in (1, 2):
            values = values + lax.ppermute(values, axis, [(i, i ^ step) for i in range(4)])
    return values + dp_swap(values)


def dp_scatter(values, dp, axis):
    half = values.shape[axis] // 2
    values = values.astype(jnp.bfloat16)
    own = lax.dynamic_slice_in_dim(values, dp * half, half, axis)
    other = lax.dynamic_slice_in_dim(values, (1 - dp) * half, half, axis)
    return add_low(own, dp_swap(other))


def dp_gather(half, dp, axis):
    other = dp_swap(half)
    return jnp.concatenate(
        [jnp.where(dp == 0, half, other), jnp.where(dp == 0, other, half)], axis
    )


ANY = pl.BlockSpec(memory_space=pl.ANY)
IN_VMEM = pl.BlockSpec(memory_space=pltpu.VMEM)
IN_SMEM = pl.BlockSpec(memory_space=pltpu.SMEM)


def after(values, *earlier):
    single = not isinstance(values, (list, tuple))
    arrays = [values] if single else list(values)

    def nothing(*refs):
        pass

    got = pl.pallas_call(
        nothing,
        out_shape=[jax.ShapeDtypeStruct(a.shape, a.dtype) for a in arrays],
        in_specs=[ANY] * (len(arrays) + len(earlier)),
        out_specs=[ANY] * len(arrays),
        input_output_aliases={i: i for i in range(len(arrays))},
        cost_estimate=pl.CostEstimate(flops=0, bytes_accessed=0, transcendentals=0),
    )(*arrays, *earlier)
    return got[0] if single else list(got)


def cost(flops, *arrays):
    moved = sum(a.size * a.dtype.itemsize for a in arrays)
    return pl.CostEstimate(flops=flops, bytes_accessed=moved, transcendentals=0)


def small_kernel(body, out_shape, *operands, scalars=1, flops=0):
    return pl.pallas_call(
        body,
        out_shape=out_shape,
        in_specs=[IN_SMEM] * scalars + [IN_VMEM] * (len(operands) - scalars),
        out_specs=jax.tree.map(lambda _: IN_VMEM, out_shape),
        compiler_params=pltpu.CompilerParams(vmem_limit_bytes=VMEM_LIMIT),
        cost_estimate=cost(flops, *operands[scalars:], *jax.tree.leaves(out_shape)),
    )(*operands)


def shape_of(shape, dtype):
    return jax.ShapeDtypeStruct(shape, dtype)


def assemble(me, pieces, keep):
    def body(info, *refs):
        out = refs[-1]
        for s in range(len(pieces)):
            at = pl.multiple_of((info[0] ^ s) * keep, 16)
            out[pl.ds(at, keep), :] = refs[s][0:keep, :]

    piece = pieces[0]
    return small_kernel(
        body, shape_of((len(pieces) * keep, piece.shape[1]), piece.dtype), me, *pieces
    )


def feature_sums(values):
    return jnp.sum(values, 0, keepdims=True)


def normalised(total, squares, width):
    mean = total / width
    return mean, lax.rsqrt(squares / width - mean * mean + 1e-05)


def token_tiles(me, values, narrow, count):
    feat, tokens = values.shape
    tok = tokens // count
    extra = 0 if narrow is None else 128

    def body(info, *refs):
        outs = refs[-count:]
        if narrow is not None:
            rest = refs[1][...].T[:feat, :]
            cuts = []
            for _ in range(3):
                cuts.append(rest.astype(jnp.bfloat16))
                rest = rest - cuts[-1].astype(jnp.float32)
        for s in range(count):
            at = pl.multiple_of((info[0] ^ s) * tok, tok)
            outs[s][:, 0:tok] = refs[0][:, pl.ds(at, tok)]
            if narrow is not None:
                for n, cut in enumerate(cuts):
                    outs[s][:, tok + n * cut.shape[1] : tok + (n + 1) * cut.shape[1]] = cut
                outs[s][:, tok + 3 * cuts[0].shape[1] :] = jnp.zeros(
                    (feat, extra - 3 * cuts[0].shape[1]), jnp.bfloat16
                )

    return small_kernel(
        body,
        (shape_of((feat, tok + extra), jnp.bfloat16),) * count,
        me,
        values,
        *(() if narrow is None else (narrow,)),
    )


def first_norm(me, pieces, tok, kinds):
    count = len(pieces)
    feat = pieces[0].shape[0]

    def body(info, *refs):
        x_refs = refs[:count]
        x_out, n_out, cols_out = refs[count:]
        total = sum(feature_sums(x[:, 0:tok].astype(jnp.float32)) for x in x_refs)
        squares = sum(feature_sums(jnp.square(x[:, 0:tok].astype(jnp.float32))) for x in x_refs)
        mean, inv_std = normalised(total, squares, count * feat)
        for s in range(count):
            at = pl.multiple_of((info[0] ^ s) * feat, 16)
            extra = x_refs[s][:, tok:].astype(jnp.float32)
            cols = (
                extra[:, 0:kinds]
                + extra[:, kinds : 2 * kinds]
                + extra[:, 2 * kinds : 3 * kinds]
            )
            cols_out[pl.ds(at, feat), :] = cols
            value = x_refs[s][:, 0:tok]
            x_out[pl.ds(at, feat), :] = value
            n_out[pl.ds(at, feat), :] = (
                (value.astype(jnp.float32) - mean) * inv_std * cols[:, 0:1] + cols[:, 1:2]
            ).astype(jnp.bfloat16)

    return small_kernel(
        body,
        (
            shape_of((count * feat, tok), jnp.bfloat16),
            shape_of((count * feat, tok), jnp.bfloat16),
            shape_of((count * feat, kinds), jnp.float32),
        ),
        me,
        *pieces,
    )


def project_out(info, heads, last, out_full, x_tok, cols):
    width, tok = x_tok.shape

    def body(info, heads_ref, last_ref, out_ref, x_ref, cols_ref, att_ref, res_ref, n_ref):
        inner = heads_ref.shape[0] * heads_ref.shape[1]
        att_ref[0:inner, :] = heads_ref[...].reshape(inner, tok)
        att_ref[inner:width, :] = last_ref[0]
        blocks, feat, hd = out_ref.shape
        per_row = width // hd
        for r in range(blocks // per_row):
            span = slice(r * feat, (r + 1) * feat)
            res_ref[span, :] = (
                sum(
                    jnp.dot(
                        out_ref[r * per_row + (c ^ info[3])],
                        att_ref[c * hd : (c + 1) * hd, :],
                        preferred_element_type=jnp.float32,
                    )
                    for c in range(per_row)
                )
                + x_ref[span, :].astype(jnp.float32)
                + cols_ref[span, 2:3]
            )
        value = res_ref[...]
        mean, inv_std = normalised(feature_sums(value), feature_sums(value * value), width)
        n_ref[...] = ((value - mean) * inv_std * cols_ref[:, 3:4] + cols_ref[:, 4:5]).astype(
            jnp.bfloat16
        )

    return small_kernel(
        body,
        (
            shape_of((width, tok), jnp.bfloat16),
            shape_of((width, tok), jnp.float32),
            shape_of((width, tok), jnp.bfloat16),
        ),
        info,
        heads,
        last,
        out_full,
        x_tok,
        cols,
    )


def norm_gradient(parts, values_ref, gain):
    d_normed = sum(p[...].astype(jnp.float32) for p in parts)
    values = values_ref[...].astype(jnp.float32)
    width = values.shape[0]
    mean, inv_std = normalised(feature_sums(values), feature_sums(values * values), width)
    centred = (values - mean) * inv_std
    scaled = d_normed * gain
    d_values = inv_std * (
        scaled - feature_sums(scaled) / width - centred * (feature_sums(scaled * centred) / width)
    )
    return (
        d_values,
        jnp.sum(d_normed * centred, 1, keepdims=True),
        jnp.sum(d_normed, 1, keepdims=True),
    )


def second_norm_back(info, parts, residual, cot, cols, out_full):
    width, tok = residual.shape

    def body(info, *refs):
        parts_refs = refs[:3]
        res_ref, cot_ref, cols_ref, out_ref, d_ref, low_ref, sums_ref, att_ref = refs[3:]
        d_values, gain_sum, shift_sum = norm_gradient(parts_refs, res_ref, cols_ref[:, 3:4])
        d_res = cot_ref[...].astype(jnp.float32) + d_values
        low = d_res.astype(jnp.bfloat16)
        d_ref[...] = d_res
        low_ref[...] = low
        sums_ref[:, 0:1] = gain_sum
        sums_ref[:, 1:2] = shift_sum
        sums_ref[:, 2:3] = jnp.sum(low.astype(jnp.float32), 1, keepdims=True)
        blocks, feat, hd = out_ref.shape
        per_row = width // hd
        for c in range(per_row):
            att_ref[c * hd : (c + 1) * hd, :] = sum(
                lax.dot_general(
                    out_ref[r * per_row + (c ^ info[3])],
                    low_ref[r * feat : (r + 1) * feat, :],
                    (((0,), (0,)), ((), ())),
                    preferred_element_type=jnp.float32,
                )
                for r in range(blocks // per_row)
            ).astype(jnp.bfloat16)

    return small_kernel(
        body,
        (
            shape_of((width, tok), jnp.float32),
            shape_of((width, tok), jnp.bfloat16),
            shape_of((width, 3), jnp.float32),
            shape_of((width, tok), jnp.bfloat16),
        ),
        info,
        *parts,
        residual,
        cot,
        cols,
        out_full,
    )


def first_norm_back(me, parts, x_tok, d_residual, cols, count):
    width, tok = x_tok.shape
    feat = width // count

    def body(info, *refs):
        parts_refs = refs[:3]
        x_ref, d_ref, cols_ref = refs[3:6]
        outs = refs[6 : 6 + count]
        sums_ref, whole = refs[6 + count :]
        d_values, gain_sum, shift_sum = norm_gradient(parts_refs, x_ref, cols_ref[:, 0:1])
        whole[...] = d_ref[...] + d_values
        for s in range(count):
            at = pl.multiple_of((info[0] ^ s) * feat, 16)
            outs[s][...] = whole[pl.ds(at, feat), :].astype(jnp.bfloat16)
        sums_ref[:, 0:1] = gain_sum
        sums_ref[:, 1:2] = shift_sum

    vmem_count = 6
    return pl.pallas_call(
        body,
        out_shape=tuple(shape_of((feat, tok), jnp.bfloat16) for _ in range(count))
        + (shape_of((width, 2), jnp.float32),),
        in_specs=[IN_SMEM] + [IN_VMEM] * vmem_count,
        out_specs=(IN_VMEM,) * (count + 1),
        scratch_shapes=[pltpu.VMEM((width, tok), jnp.float32)],
        compiler_params=pltpu.CompilerParams(vmem_limit_bytes=VMEM_LIMIT),
        cost_estimate=cost(0, *parts, x_tok, d_residual, d_residual),
    )(me, *parts, x_tok, d_residual, cols)


def side_by_side(me, pieces, dtype):
    feat, tok = pieces[0].shape

    def body(info, *refs):
        for s in range(len(pieces)):
            at = pl.multiple_of((info[0] ^ s) * tok, tok)
            refs[-1][:, pl.ds(at, tok)] = refs[s][...].astype(dtype)

    return small_kernel(body, shape_of((feat, len(pieces) * tok), dtype), me, *pieces)


def normal_tail(value):
    z = value * 0.7071067811865476
    t = 1.0 / (1.0 + 0.5 * z)
    poly = jnp.full_like(t, 0.17087277)
    for factor in (
        -0.82215223,
        1.48851587,
        -1.13520398,
        0.27886807,
        -0.18628806,
        0.09678418,
        0.37409196,
        1.00002368,
        -1.26551223,
    ):
        poly = poly * t + factor
    return t * jnp.exp(poly - z * z)


def feed_forward(normed, cot, up, down, bias):
    width, tok = normed.shape
    hidden_len = up.shape[1]

    def body(n_ref, cot_ref, up_ref, down_ref, bias_ref, active_ref, d_ref, sent_ref):
        hidden = (
            jnp.dot(n_ref[...].T, up_ref[...], preferred_element_type=jnp.float32) + bias_ref[...]
        )
        d_active = jnp.dot(cot_ref[...].T, down_ref[...], preferred_element_type=jnp.float32)
        tail = 0.5 * normal_tail(jnp.abs(hidden))
        below = jnp.where(hidden < 0, tail, 1.0 - tail)
        density = 0.3989422804014327 * jnp.exp(-0.5 * hidden * hidden)
        active_ref[...] = (hidden * below).astype(jnp.bfloat16)
        d_hidden = (d_active * (below + hidden * density)).astype(jnp.bfloat16)
        d_ref[...] = d_hidden
        sent_ref[...] = lax.dot_general(
            up_ref[...],
            d_hidden,
            (((1,), (1,)), ((), ())),
            preferred_element_type=jnp.float32,
        ).astype(jnp.bfloat16)

    return small_kernel(
        body,
        (
            shape_of((tok, hidden_len), jnp.bfloat16),
            shape_of((tok, hidden_len), jnp.bfloat16),
            shape_of((width, tok), jnp.bfloat16),
        ),
        normed,
        cot,
        up,
        down,
        bias,
        scalars=0,
        flops=10 * tok * width * hidden_len,
    )


def block_products(left, right, feat, hd):
    rows, cols = left.shape[0] // feat, right.shape[0] // hd

    def body(left_ref, right_ref, out_ref):
        for r in range(rows):
            whole = lax.dot_general(
                left_ref[r * feat : (r + 1) * feat, :],
                right_ref[...],
                (((1,), (1,)), ((), ())),
                preferred_element_type=jnp.float32,
            ).astype(jnp.bfloat16)
            for c in range(cols):
                out_ref[r * cols + c] = whole[:, c * hd : (c + 1) * hd]

    return small_kernel(
        body, shape_of((rows * cols, feat, hd), jnp.bfloat16), left, right, scalars=0
    )


def row_products(me, left, right, count):
    feat = left.shape[0] // count

    def body(info, left_ref, right_ref, *outs):
        for s in range(count):
            at = pl.multiple_of((info[0] ^ s) * feat, 16)
            outs[s][...] = lax.dot_general(
                left_ref[pl.ds(at, feat), :],
                right_ref[...],
                (((1,), (1,)), ((), ())),
                preferred_element_type=jnp.float32,
            ).astype(jnp.bfloat16)

    shape = shape_of((feat, right.shape[0]), jnp.bfloat16)
    return small_kernel(body, (shape,) * count, me, left, right)


def mixed_gradient(me, heads, d_query, last_parts):
    count = len(heads)
    kinds, hdim, tokens = heads[0].shape
    rows = kinds * count * hdim + kinds * hdim

    def body(info, *refs):
        query_ref = refs[count]
        last_refs = refs[count + 1 : count + 4]
        out = refs[count + 4]
        for s in range(count):
            for k in range(kinds):
                at = pl.multiple_of((k * count + (info[0] ^ s)) * hdim, hdim)
                out[pl.ds(at, hdim), :] = refs[s][k]
        base = kinds * count * hdim
        out[base : base + hdim, :] = jnp.zeros((hdim, tokens), jnp.bfloat16)
        out[base : base + hdim, 0 : query_ref.shape[1]] = query_ref[...]
        for k in range(2):
            out[base + (k + 1) * hdim : base + (k + 2) * hdim, :] = sum(
                ref[k].astype(jnp.float32) for ref in last_refs
            ).astype(jnp.bfloat16)

    return small_kernel(
        body, shape_of((rows, tokens), jnp.bfloat16), me, *heads, d_query, *last_parts
    )


def with_bias_rows(weight, bias):
    return jnp.concatenate(
        [weight, bias[None], jnp.zeros((PAD - 1, weight.shape[1]), weight.dtype)], 0
    )


def strip_tables(cols, wide):
    native = 3 * D // cols
    slots = wide + HDIM
    from_native = np.full((cols, cols, slots), -1, np.int32)
    to_strip = np.full((cols, cols, slots), -1, np.int32)
    for c in range(cols):
        for s in range(cols):
            for block, group, table in ((c, c ^ s, 0), (c ^ s, c, 1)):
                count = 0
                for i in range(3):
                    for place in range(wide + HDIM):
                        last = place >= wide
                        column = i * D + (D - HDIM + place - wide if last else group * wide + place)
                        if column // native != block:
                            continue
                        slot = wide + place - wide if last else count
                        count += not last
                        if table == 0:
                            from_native[c, s, slot] = column - block * native
                        else:
                            to_strip[c, s, slot] = (
                                3 * wide + i * HDIM + place - wide if last else i * wide + place
                            )
    return from_native.reshape(cols, -1), to_strip.reshape(cols, -1)


def one_hot(table, col, size):
    slots = pick(jnp.asarray(table), col)
    return (lax.broadcasted_iota(jnp.int32, (size, table.shape[1]), 0) == slots[None]).astype(
        jnp.bfloat16
    )


def head_shards(
    block_input,
    cotangent,
    prefix_len,
    first_gain,
    first_shift,
    qkv_weight,
    qkv_bias,
    out_weight,
    out_bias,
    second_gain,
    second_shift,
    up_weight,
    up_bias,
    down_weight,
    down_bias,
):
    rows = lax.axis_size("row")
    cols = lax.axis_size("col")
    row = lax.axis_index("row")
    col = lax.axis_index("col")
    dp = lax.axis_index("dp")
    tok_a = block_input.shape[1]
    tok_b = tok_a // rows
    feat = block_input.shape[2]
    block = 4 * tok_b
    wide = rows * HDIM
    slots = wide + HDIM
    hidden_len = up_weight.shape[1]
    from_native, to_strip = strip_tables(cols, wide)

    me = row[None]
    narrow = jnp.concatenate(
        [
            jnp.stack(
                [first_gain, first_shift, out_bias, second_gain, second_shift, down_bias]
                + [jnp.zeros_like(first_gain)] * 2
            ),
            jnp.zeros((8, 384 - feat), jnp.float32),
        ],
        1,
    )

    x_got = row_exchange(list(token_tiles(me, block_input[0].T, narrow, rows)))
    spread = one_hot(from_native, col, qkv_weight.shape[1])
    sent = dot(with_bias_rows(qkv_weight, qkv_bias), spread, 1, 0).astype(jnp.bfloat16)
    out_rows = jnp.concatenate([out_weight.T, jnp.zeros((PAD, out_weight.shape[0]), jnp.bfloat16)])
    got = col_exchange(
        [
            jnp.concatenate([sent[:, s * slots : (s + 1) * slots], out_rows], 1)
            for s in range(cols)
        ]
    )
    x_got[1], *got[1:] = after([x_got[1], *got[1:]])
    out_got = [g[:feat, slots:] for g in got]
    got = [g[:, :slots] for g in got]
    x_tok, normed_one, cols_all = first_norm(me, x_got, tok_b, narrow.shape[0])

    near = col_send(normed_one, NEAR)
    mid = col_send(normed_one, MIDDLE)
    cot_got = row_exchange(
        list(token_tiles(me, after(cotangent[0].T, normed_one), None, rows))
    )
    near, mid, *cot_got[1:] = after([near, mid, *cot_got[1:]])
    inner = col_send(near, MIDDLE)
    outer = col_send(mid, OUTWARD)
    placed = one_hot(to_strip, col, 3 * slots)
    strip = dot(jnp.concatenate(got, 1), placed, 1, 1).astype(jnp.bfloat16)
    strip_bias = strip[feat].astype(jnp.float32)
    strip_near = swap(strip, 1)
    strip_far = swap(strip, 2)
    cot_tok = assemble(me, cot_got, feat)
    inner, outer, strip_near, strip_far = after([inner, outer, strip_near, strip_far], cot_tok)
    ends = col_send(inner, OUTWARD)
    qkv_strip = assemble(me, [strip, strip_near, strip_far, swap(strip_far, 1)], feat)

    up_slice = lax.all_gather(up_weight, "row", axis=0, tiled=True)
    down_slice = lax.all_gather(down_weight.T, "row", axis=0, tiled=True)

    out_full = lax.all_gather(jnp.stack(out_got), "row").reshape((-1,) + out_weight.shape)

    query_scale = LOG2E * HDIM ** (-0.5)
    scale = jnp.concatenate(
        [
            jnp.full((wide,), query_scale, jnp.float32),
            jnp.ones((2 * wide,), jnp.float32),
            jnp.full((HDIM,), query_scale, jnp.float32),
            jnp.ones((2 * HDIM,), jnp.float32),
        ]
    )
    def project(normed):
        mixed = (
            (dot(qkv_strip, normed, 0, 0) + strip_bias[:, None]) * scale[:, None]
        ).astype(jnp.bfloat16)
        by_head = mixed[: 3 * wide].reshape(3, rows, HDIM, -1)
        return mixed, [pick(by_head, row ^ s, 1) for s in range(rows)]

    first_set = jnp.concatenate([normed_one, near], 1)
    mixed_first, tiles_first = project(first_set)
    got_first = row_exchange(tiles_first)
    ends = after(ends, *tiles_first)
    middle = (col == 1) | (col == 2)
    second_set = jnp.concatenate(
        [jnp.where(middle, inner, outer), jnp.where(middle, mid, ends)], 1
    )
    mixed_second, tiles_second = project(second_set)
    got_second = row_exchange(tiles_second)
    pieces = [p for pair in zip(got_first, got_second) for p in pair]
    last_query = mixed_first[3 * wide : 3 * wide + HDIM, :tok_b]
    last_pieces = row_gather(
        jnp.concatenate(
            [m[3 * wide + HDIM :].reshape(2, HDIM, -1) for m in (mixed_first, mixed_second)], 2
        )
    )
    normed_set = jnp.concatenate([first_set, second_set], 1)
    cot_tok = after(cot_tok, second_set)
    cot_cols = lax.all_gather(cot_tok, "col")
    cot_parts = [cot_tok] + [pick(cot_cols, col ^ s) for s in range(1, cols)]

    zero = jnp.int32(0)
    info = jnp.stack([row, prefix_len[0], zero, col])
    last_info = jnp.stack([row, prefix_len[0], col * tok_a + row * tok_b, col])
    heads_out, heads_full, heads_lse = attend(
        info, pieces, None, tok_b, block, (up_slice, down_slice, last_pieces[1])
    )
    last_out, last_full, last_lse = attend(last_info, last_pieces, last_query, tok_b, block)
    heads_got = lax.all_to_all(heads_out, ("col", "row"), 0, 0, tiled=True)
    attended, residual, normed_two = project_out(
        info, heads_got, last_out, out_full, x_tok, cols_all
    )
    hidden_bias = up_bias.astype(jnp.float32)[None]

    def through_hidden(normed, s):
        return feed_forward(normed, cot_parts[s], up_slice, down_slice, hidden_bias)

    near = col_send(normed_two, NEAR)
    mid = col_send(normed_two, MIDDLE)
    through = [through_hidden(normed_two, 0)]
    near, mid = after([near, mid], through[0][2])
    inner = col_send(near, MIDDLE)
    outer = col_send(mid, OUTWARD)
    through.append(through_hidden(near, 1))
    inner, outer = after([inner, outer], through[1][2])
    ends = col_send(inner, OUTWARD)
    second = jnp.where(middle, inner, outer)
    through.append(through_hidden(second, 2))
    ends = after(ends, through[2][2])
    third = jnp.where(middle, mid, ends)
    through.append(through_hidden(third, 3))
    d_norm_sent = [t[2] for t in through]
    normed_two = jnp.concatenate([normed_two, near, second, third], 1)
    cot_all = jnp.concatenate(cot_parts, 1)
    work = {}

    def weight_products(stage, arrived):
        if stage == 0:
            return ()
        source, left = ((1, normed_two), (0, cot_all))[stage - 1]
        right = jnp.concatenate(after([t[source] for t in through], arrived), 0)
        work[stage] = right, dot(left, right, 1, 0).astype(jnp.bfloat16)
        return (work[stage][1],)

    d_norm_two = line_reduce(d_norm_sent, weight_products)
    (low_hidden, up_part), (low_active, down_part) = work[1], work[2]
    d_residual, branch, second_sums, d_attended = second_norm_back(
        info, d_norm_two, residual, cot_tok, cols_all, out_full
    )
    d_heads = lax.all_to_all(
        d_attended[: D - HDIM].reshape(rows * cols, HDIM, tok_b), ("col", "row"), 0, 0, tiled=True
    )
    *last_grads, d_last_query = attend_back(
        last_info,
        last_pieces,
        last_query,
        last_full,
        last_lse,
        d_attended[D - HDIM :][None],
        tok_b,
        block,
    )
    head_grads = attend_back(info, pieces, None, heads_full, heads_lse, d_heads, tok_b, block)
    d_last_parts = row_reduce_parts(last_grads)

    up_down_part = jnp.stack(
        [p.reshape(rows, feat, hidden_len) for p in (up_part, down_part)], 1
    )
    up_down_half = lax.psum_scatter(up_down_part, "row", scatter_dimension=0)
    active_parts = after(low_active, d_attended).reshape(cols, tok_b, hidden_len)
    partial_out = jnp.stack(
        [
            dot(down_slice, pick(active_parts, col ^ i), 1, 1).astype(jnp.bfloat16)
            for i in range(cols)
        ]
    )
    sent_out = lax.psum_scatter(partial_out, "col", scatter_dimension=0)
    out_half = lax.psum_scatter(
        block_products(branch, attended, feat, D).reshape(rows, feat, D),
        "row",
        scatter_dimension=0,
    )

    up_down_grad = pair_sum(up_down_half)
    head_got = row_exchange(list(head_grads))
    head_got[1] = after(head_got[1], up_down_grad)
    d_mixed = mixed_gradient(me, head_got, d_last_query, d_last_parts)
    d_normed_sent = [
        dot(qkv_strip, d_mixed[:, s * tok_b : (s + 1) * tok_b], 1, 0).astype(jnp.bfloat16)
        for s in range(cols)
    ]
    kept = {}

    def beside(stage, arrived):
        if stage == 0:
            parts = row_products(me, normed_set, after(d_mixed, *d_normed_sent), rows)
            beyond, kept["near"] = swap(parts[3], 1), swap(parts[1], 1)
            pair = add_low(parts[2], beyond)
            kept["own"], kept["far"] = parts[0], swap(pair, 2)
            return (pair,)
        kept[stage] = arrived
        return ()

    d_norm_one = line_reduce(d_normed_sent, beside)
    arrived = [kept[1], kept[2], d_norm_one[1]]
    near, far = after([kept["near"], kept["far"]], arrived[1])
    total = sum(p.astype(jnp.float32) for p in (kept["own"], near, far)).astype(jnp.bfloat16)
    both = jnp.concatenate([total, out_half], 1)
    half = feat // 2
    other = dp_swap(lax.dynamic_slice_in_dim(both, (1 - dp) * half, half, 0))
    total = add_low(lax.dynamic_slice_in_dim(both, dp * half, half, 0), other)
    sent = dot(total[:, : 3 * slots], placed, 1, 0).astype(jnp.bfloat16)
    hd = D // cols
    got = col_exchange(
        [
            jnp.concatenate(
                [
                    sent[:, s * slots : (s + 1) * slots],
                    lax.dynamic_slice_in_dim(total, 3 * slots + (col ^ s) * hd, hd, 1),
                ],
                1,
            )
            for s in range(cols)
        ]
    )
    qkv = dot(jnp.concatenate([g[:, :slots] for g in got], 1), spread, 1, 1)
    out = sum(g[:, slots:].astype(jnp.float32) for g in got)
    last_grad = dp_gather(jnp.concatenate([qkv, out], 1).astype(jnp.bfloat16), dp, 0)
    qkv_grad, out_grad = jnp.split(last_grad.astype(jnp.float32), [qkv_weight.shape[1]], 1)

    out_value = (
        after(sent_out, arrived[0]).astype(jnp.float32) + residual + cols_all[:, 5:6]
    ).astype(jnp.bfloat16)
    block_got = row_exchange(
        [lax.dynamic_slice_in_dim(out_value, (row ^ s) * feat, feat, 0) for s in range(rows)]
    )
    block_output = side_by_side(me, after(block_got, arrived[1]), jnp.bfloat16)
    *input_parts, first_sums = first_norm_back(
        me, d_norm_one, x_tok, d_residual, cols_all, rows
    )
    input_grad = side_by_side(me, row_exchange(input_parts), jnp.float32)

    at_row = (jnp.arange(rows) == row)[:, None]

    def own_row(values):
        return jnp.where(at_row, values[None], 0.0).reshape(-1)

    def own_col(values):
        return jnp.where((jnp.arange(cols) == col)[:, None], values[None], 0.0).reshape(-1)

    bias_strip = jnp.sum(d_mixed.astype(jnp.float32), 1)
    at_col = (jnp.arange(cols) == col)[None, :, None]
    bias_heads = jnp.where(at_col, bias_strip[: 3 * wide].reshape(3, 1, wide), 0.0)
    bias_all = jnp.concatenate(
        [bias_heads.reshape(3, -1), bias_strip[3 * wide :].reshape(3, HDIM)], 1
    ).reshape(-1)
    early = [
        own_row(jnp.sum(cotangent[0].astype(jnp.float32), 0)),
        second_sums[:, 2],
        second_sums[:, 0],
        second_sums[:, 1],
        own_col(jnp.sum(low_hidden.astype(jnp.float32), 0)),
        bias_all,
        first_sums[:, 0],
        first_sums[:, 1],
    ]
    total = sum_everywhere(jnp.concatenate(early).reshape(8, -1)).reshape(-1)

    def own_part(start, size, index):
        return lax.dynamic_slice_in_dim(total, start + index * size, size, 0)

    width = rows * feat
    up_at = 4 * width
    qkv_at = up_at + cols * hidden_len
    first_at = qkv_at + 3 * width
    return (
        block_output.T[None],
        input_grad.T[None],
        own_part(first_at, feat, row),
        own_part(first_at + width, feat, row),
        qkv_grad,
        own_part(qkv_at, 3 * width // cols, col),
        out_grad.T,
        own_part(width, feat, row),
        own_part(2 * width, feat, row),
        own_part(3 * width, feat, row),
        up_down_grad[0],
        own_part(up_at, hidden_len, col),
        up_down_grad[1].T,
        own_part(0, feat, row),
    )


def solution(mesh):
    in_specs = (
        P("dp", "col", "row"),
        P("dp", "col", "row"),
        P("dp"),
        P("row"),
        P("row"),
        P("row", "col"),
        P("col"),
        P("col", "row"),
        P("row"),
        P("row"),
        P("row"),
        P("row", "col"),
        P("col"),
        P("col", "row"),
        P("row"),
    )
    out_specs = (
        P("dp", "col", "row"),
        P("dp", "col", "row"),
        P("row"),
        P("row"),
        P("row", "col"),
        P("col"),
        P("col", "row"),
        P("row"),
        P("row"),
        P("row"),
        P("row", "col"),
        P("col"),
        P("col", "row"),
        P("row"),
    )
    one_head_each = mesh.shape["row"] == 4 and mesh.shape["col"] == 4 and mesh.shape["dp"] == 2
    body = head_shards if one_head_each else shards
    return jax.shard_map(body, mesh=mesh, in_specs=in_specs, out_specs=out_specs, check_vma=False)
```
